256 devices in a mesh: row: 16 (over z_hi, x), col: 8 (over y, core), rep: 2 (over z_lo).
Axes of the slice: x: 4, y: 4, z: 8 (z_hi: 4, z_lo: 2; z = z_hi * 2 + z_lo), core: 2. Of those that a mesh axis runs over, the one named last changes fastest.
Arguments:
- pair: bfloat16 [768, 384, 128], P(('rep', 'row'), 'col'), parts along dimension 0, may hold values from -6 to 6
- chain_lengths: int32 [8], P('rep'), parts along dimension 0, may hold values from 24 to 96, as said below
- cotangent: bfloat16 [768, 384, 128], P(('rep', 'row'), 'col'), parts along dimension 0, may hold values from -6 to 6
- norm_params: float32 [4, 128], replicated, may hold values from 0.1 to 1.9
- w_in: bfloat16 [128, 512], replicated, may hold values from -0.5 to 0.5
- w_gate: bfloat16 [128, 128], replicated, may hold values from -0.5 to 0.5
- w_out: bfloat16 [128, 128], replicated, may hold values from -0.5 to 0.5
Outputs:
- update: bfloat16 [768, 384, 128], P(('rep', 'row'), 'col'), parts along dimension 0
- grad_pair: bfloat16 [768, 384, 128], P(('rep', 'row'), 'col'), parts along dimension 0
The draws below stay inside these ranges and needn't reach their ends.
There are 2 independent parts, one for each index of `rep`. The reference program is written for one: setup_inputs(seed, part) draws one part's arguments, and reference() takes and returns one part's arrays. A program takes and returns all parts, laid end to end along the dimension named above; an argument that names none is the same for every part. Nothing has to cross between parts.
Inputs may be any that keep to these rules, and one draw needn't show every extreme that they name: `chain_lengths`: each chain length lies between 24 and 96, and both ends occur in every draw.
All inputs are finite; a program needn't handle non-finite values.
Results may differ from the reference program's by a relative error of at most 0.008.
Values may be sent and summed in bfloat16 or wider, within the bound.
No kernel may reach another device: no remote copies, remote signals or barrier semaphores. Data moves between devices by JAX's collectives and lax.ppermute only.
A program may use at most 128 MiB of HBM per device.

```python
import jax
import jax.numpy as jnp
from jax import lax

CHANNELS = 128
INNER = 128
CHAINS = 4
TOKENS = 384


def draw_chain_lengths(key, part):
    key = jax.random.fold_in(key, 11)
    lowest = TOKENS // 16
    highest = TOKENS // 4
    values = jax.random.randint(key, (CHAINS,), lowest, highest + 1)
    order = jax.random.permutation(jax.random.fold_in(key, 1), CHAINS)
    values = values.at[order[0]].set(highest).at[order[1]].set(lowest)
    return values.astype(jnp.int32)


def levels(key, shape, shards, low, high):
    def one(position, blocks):
        steps = jax.random.uniform(jax.random.fold_in(jax.random.fold_in(key, 6), position), (blocks,), jnp.float32, low / len(shards), high / len(shards))
        return jnp.repeat(jnp.exp(steps), shape[position] // blocks).reshape((-1,) + (1,) * (len(shape) - position - 1))

    factor_of = one(*shards[0])
    for cut in shards[1:]:
        factor_of = factor_of * one(*cut)
    return factor_of


def bell_draw(key, extent, deviation, most, shards=(), held_as=jnp.bfloat16):
    result = deviation * jax.random.normal(key, extent, jnp.float32)
    if shards:
        result = result * levels(key, extent, shards, -0.22, 0.18)
    return jnp.clip(result, -most, most).astype(held_as)


def setup_inputs(seed: int = 0, part: int = 0) -> dict:
    streams_of = jax.random.split(jax.random.key(seed), 8)
    own_keys = jax.random.split(jax.random.fold_in(streams_of[7], part), 8)
    pair = bell_draw(own_keys[0], (TOKENS, TOKENS, CHANNELS), 1.0, 6.0, ((0, 16), (1, 8)))
    chain_lengths = draw_chain_lengths(jax.random.fold_in(jax.random.fold_in(streams_of[7], part), 71), part)
    cotangent = bell_draw(own_keys[2], (TOKENS, TOKENS, CHANNELS), 1.0, 6.0, ((0, 16), (1, 8)))
    norm_params = jnp.clip(1.0 + 0.18 * jax.random.normal(streams_of[3], (4, CHANNELS), jnp.float32), 0.1, 1.9)
    w_in = bell_draw(streams_of[4], (CHANNELS, 4 * INNER), CHANNELS ** -0.5, 0.5)
    w_gate = bell_draw(streams_of[5], (CHANNELS, CHANNELS), CHANNELS ** -0.5, 0.5)
    w_out = bell_draw(streams_of[6], (INNER, CHANNELS), INNER ** -0.5, 0.5)
    return dict(pair=pair, chain_lengths=chain_lengths, cotangent=cotangent, norm_params=norm_params, w_in=w_in, w_gate=w_gate, w_out=w_out)


EPS = 1e-05

def normalize(values, gain, shift):
    mean = lax.optimization_barrier(jnp.mean(values, axis=-1, keepdims=True))
    centered = values - mean
    variance = lax.optimization_barrier(jnp.mean(centered * centered, axis=-1, keepdims=True))
    inverse = 1.0 / jnp.sqrt(variance + EPS)
    unit = centered * inverse
    return (unit * gain + shift, unit, inverse)

def norm_back(grad_out, unit, inverse, gain):
    scaled = grad_out * gain
    return inverse * (scaled - lax.optimization_barrier(jnp.mean(scaled, axis=-1, keepdims=True)) - unit * lax.optimization_barrier(jnp.mean(scaled * unit, axis=-1, keepdims=True)))

def reference(pair, chain_lengths, cotangent, norm_params, w_in, w_gate, w_out):
    f32 = jnp.float32
    limit = jnp.sum(chain_lengths).astype(jnp.int32)
    valid = (jnp.arange(TOKENS, dtype=jnp.int32) < limit).astype(f32)
    mask = (valid[:, None] * valid[None, :])[..., None]
    normed_f, unit_in, inv_in = normalize(pair.astype(f32), norm_params[0], norm_params[1])
    normed = normed_f.astype(jnp.bfloat16)
    flat = normed.reshape(TOKENS * TOKENS, CHANNELS)
    proj = jnp.dot(flat, w_in, preferred_element_type=f32).reshape(TOKENS, TOKENS, 4 * INNER)
    sig_a = jax.nn.sigmoid(proj[..., :INNER])
    val_a = proj[..., INNER:2 * INNER]
    sig_b = jax.nn.sigmoid(proj[..., 2 * INNER:3 * INNER])
    val_b = proj[..., 3 * INNER:]
    left = (mask * sig_a * val_a).astype(jnp.bfloat16)
    right = (mask * sig_b * val_b).astype(jnp.bfloat16)
    gate = jax.nn.sigmoid(jnp.dot(flat, w_gate, preferred_element_type=f32)).reshape(TOKENS, TOKENS, CHANNELS)
    left_f = left.astype(f32)
    right_f = right.astype(f32)
    tri = jnp.einsum('kic,kjc->ijc', left_f, right_f)
    tri_n, unit_out, inv_out = normalize(tri, norm_params[2], norm_params[3])
    tri_n = tri_n.astype(jnp.bfloat16)
    lin = jnp.dot(tri_n.reshape(-1, INNER), w_out, preferred_element_type=f32).reshape(TOKENS, TOKENS, CHANNELS)
    update = (gate * lin).astype(jnp.bfloat16)
    grad_up = cotangent.astype(f32)
    grad_lin = (grad_up * gate).astype(jnp.bfloat16)
    grad_gate = (grad_up * lin * gate * (1.0 - gate)).astype(jnp.bfloat16)
    grad_tn = jnp.dot(grad_lin.reshape(-1, CHANNELS), w_out.T, preferred_element_type=f32).reshape(TOKENS, TOKENS, INNER)
    grad_tri = norm_back(grad_tn, unit_out, inv_out, norm_params[2]).astype(jnp.bfloat16).astype(f32)
    grad_left = jnp.einsum('ijc,kjc->kic', grad_tri, right_f)
    grad_right = jnp.einsum('ijc,kic->kjc', grad_tri, left_f)
    grad_proj = jnp.concatenate([grad_left * mask * val_a * sig_a * (1.0 - sig_a), grad_left * mask * sig_a, grad_right * mask * val_b * sig_b * (1.0 - sig_b), grad_right * mask * sig_b], axis=-1).astype(jnp.bfloat16)
    grad_normed = jnp.dot(grad_proj.reshape(-1, 4 * INNER), w_in.T, preferred_element_type=f32)
    grad_normed = grad_normed + jnp.dot(grad_gate.reshape(-1, CHANNELS), w_gate.T, preferred_element_type=f32)
    grad_normed = grad_normed.reshape(TOKENS, TOKENS, CHANNELS)
    grad_pair = norm_back(grad_normed, unit_in, inv_in, norm_params[0]).astype(jnp.bfloat16)
    return (update, grad_pair)
```

```python
import functools

import jax
import jax.numpy as jnp
from jax import lax
from jax.experimental import pallas as pl
from jax.experimental.pallas import tpu as pltpu
from jax.sharding import PartitionSpec as P

EPS = 1e-05
F32 = jnp.float32
BF16 = jnp.bfloat16
MIB = 1 << 20
LAST = (((1,), (1,)), ((), ()))
FIRST = (((0,), (0,)), ((), ()))
SLOT = 64
GROUP = 4


def dot(a, b, dims=(((1,), (0,)), ((), ()))):
    return lax.dot_general(a, b, dims, preferred_element_type=F32)


def identity(n):
    row = lax.broadcasted_iota(jnp.int32, (n, n), 0)
    col = lax.broadcasted_iota(jnp.int32, (n, n), 1)
    return jnp.where(row == col, 1.0, 0.0).astype(BF16)


def low_lanes(shape):
    return lax.broadcasted_iota(jnp.int32, shape, len(shape) - 1) < SLOT


def half_turn(x):
    return pltpu.roll(x, SLOT, x.ndim - 1)


def unit_of(x):
    mean = jnp.mean(x, axis=-1, keepdims=True)
    centered = x - mean
    variance = jnp.mean(centered * centered, axis=-1, keepdims=True)
    inverse = lax.rsqrt(variance + EPS)
    return centered * inverse, inverse


def mask_of(ids_ref, len_ref, row, shape):
    limit = len_ref[0]
    for i in range(1, len_ref.shape[0]):
        limit = limit + len_ref[i]
    bound = jnp.where(ids_ref[0] + row < limit, limit - ids_ref[1], 0)
    return lax.broadcasted_iota(jnp.int32, shape, 0) < bound


def paired(first, second):
    gap = jnp.zeros((SLOT - first.shape[0], first.shape[1]), first.dtype)
    return jnp.concatenate([first, gap, second, gap], axis=0)


def factors_kernel(ids_ref, len_ref, pair_ref, par_ref, w_ref, msg_ref, normed_ref, scr):
    rows, cols, width = pair_ref.shape
    hidden = w_ref.shape[1] // 4
    eye = identity(hidden)
    gain, shift = par_ref[0:1, :], par_ref[1:2, :]
    w = w_ref[...]
    for start in range(0, rows, GROUP):
        x = pair_ref[start : start + GROUP].astype(F32).reshape(GROUP * cols, width)
        unit, _ = unit_of(x)
        normed = (unit * gain + shift).astype(BF16)
        normed_ref[start : start + GROUP] = normed.reshape(GROUP, cols, width)
        proj = dot(normed, w)
        left = jax.nn.sigmoid(proj[:, :hidden]) * proj[:, hidden : 2 * hidden]
        right = jax.nn.sigmoid(proj[:, 2 * hidden : 3 * hidden]) * proj[:, 3 * hidden :]
        for k in range(GROUP):
            mask = mask_of(ids_ref, len_ref, start + k, (cols, hidden))
            at = slice(k * cols, (k + 1) * cols)
            one = jnp.where(mask, left[at], 0.0).astype(BF16)
            two = jnp.where(mask, right[at], 0.0).astype(BF16)
            scr[pl.ds(start + k, hidden, stride=rows), :] = dot(eye, paired(one, two), LAST)
    msg_ref[...] = scr[...].reshape(hidden, rows, 2 * SLOT).astype(BF16)


def saved_kernel(
    ids_ref, len_ref, pair_ref, normed_ref, cot_ref, par_ref, w_in_ref, w_gate_ref, w_out_ref,
    gate_ref, scaled_ref, coef_ref, unit_ref, inv_ref,
):
    rows, cols, width = pair_ref.shape
    hidden = w_in_ref.shape[1] // 4
    w_in, w_gate, w_out = w_in_ref[...], w_gate_ref[...], w_out_ref[...]
    for start in range(0, rows, GROUP):
        size = GROUP * cols
        at = slice(start * cols, start * cols + size)
        x = pair_ref[start : start + GROUP].astype(F32).reshape(size, width)
        unit, inverse = unit_of(x)
        unit_ref[at, :] = unit
        inv_ref[at, :] = jnp.broadcast_to(inverse, (size, width))
        normed = normed_ref[start : start + GROUP].reshape(size, width)
        gate = jax.nn.sigmoid(dot(normed, w_gate))
        gate_ref[at, :] = gate
        cot = cot_ref[start : start + GROUP].astype(F32).reshape(size, width)
        grad_lin = (cot * gate).astype(BF16)
        scaled = dot(grad_lin, w_out, LAST) * par_ref[2:3, :]
        scaled_ref[at, :] = scaled - jnp.mean(scaled, axis=-1, keepdims=True)
        proj = dot(normed, w_in)
        mask = jnp.concatenate(
            [
                jnp.where(mask_of(ids_ref, len_ref, start + k, (cols, hidden)), 1.0, 0.0)
                for k in range(GROUP)
            ],
            axis=0,
        )
        for side in range(2):
            sig = jax.nn.sigmoid(proj[:, 2 * side * hidden : (2 * side + 1) * hidden])
            val = proj[:, (2 * side + 1) * hidden : (2 * side + 2) * hidden]
            kept = mask * sig
            coef_ref[2 * side, at, :] = kept * val * (1.0 - sig)
            coef_ref[2 * side + 1, at, :] = kept


def triangle_kernel(got_ref, msg_ref, left_ref, right_ref, tri_scr):
    n_row, n_col, rows, lanes = got_ref.shape
    total = n_row * rows
    low = low_lanes((total, lanes))
    for t in range(n_col // 2):
        even = got_ref[:, 2 * t].astype(F32).reshape(total, lanes)
        odd = got_ref[:, 2 * t + 1].astype(F32).reshape(total, lanes)
        at = slice(t * lanes, (t + 1) * lanes)
        left_ref[:, at] = jnp.where(low, even, half_turn(odd)).astype(BF16)
        right_ref[:, at] = jnp.where(low, half_turn(even), odd).astype(BF16)
    tri_scr[...] = dot(left_ref[...], right_ref[...], FIRST)
    low = low_lanes((n_row, 8, lanes))
    for t in range(n_col // 2):
        tile = tri_scr[:, t * lanes : (t + 1) * lanes].reshape(n_row // 2, SLOT, lanes)
        tile = tile[:, : 2 * rows].reshape(n_row, rows, lanes)
        turned = half_turn(tile)
        a, b, c = tile[:, 0:8], tile[:, 8:16], tile[:, 16:24]
        ra, rb, rc = turned[:, 0:8], turned[:, 8:16], turned[:, 16:24]
        msg_ref[:, 2 * t] = jnp.concatenate([jnp.where(low, a, rb), c], axis=1).astype(BF16)
        msg_ref[:, 2 * t + 1] = jnp.concatenate([jnp.where(low, ra, b), rc], axis=1).astype(BF16)


def norm_kernel(got_ref, scaled_ref, par_ref, msg_ref, tn_ref, scr_in, scr_out):
    hidden, fold, lanes = got_ref.shape
    rows, cols, _ = tn_ref.shape
    eye = identity(hidden)
    gain, shift = par_ref[2:3, :], par_ref[3:4, :]
    scr_in[...] = got_ref[...].astype(F32).reshape(hidden * fold, lanes)

    def one(tri, k):
        unit, inverse = unit_of(tri)
        tn_ref[k] = (unit * gain + shift).astype(BF16)
        s = scaled_ref[k * cols : (k + 1) * cols, :]
        grad = inverse * (s - unit * jnp.mean(s * unit, axis=-1, keepdims=True))
        return grad.astype(BF16)

    nothing = jnp.zeros((cols, hidden), BF16)
    for s in range(fold):
        tri = dot(eye, scr_in[pl.ds(s, hidden, stride=fold), :].astype(BF16), LAST)
        if s < 8:
            first = one(tri[:cols], s)
            second = one(tri[SLOT : SLOT + cols], s + 8)
        else:
            first = one(tri[:cols], s + 8)
            second = nothing
        scr_out[pl.ds(s, hidden, stride=fold), :] = dot(eye, paired(first, second), LAST)
    msg_ref[...] = scr_out[...].reshape(hidden, fold, lanes).astype(BF16)


def update_kernel(tn_ref, gate_ref, cot_ref, w_out_ref, w_gate_ref, update_ref, gn_ref):
    rows, cols, width = cot_ref.shape
    w_out, w_gate = w_out_ref[...], w_gate_ref[...]
    for start in range(0, rows, GROUP):
        size = GROUP * cols
        at = slice(start * cols, start * cols + size)
        lin = dot(tn_ref[start : start + GROUP].reshape(size, -1), w_out)
        gate = gate_ref[at, :]
        update_ref[start : start + GROUP] = (gate * lin).astype(BF16).reshape(GROUP, cols, width)
        cot = cot_ref[start : start + GROUP].astype(F32).reshape(size, width)
        grad_gate = (cot * lin * gate * (1.0 - gate)).astype(BF16)
        gn_ref[at, :] = dot(grad_gate, w_gate, LAST)


def factor_grads_kernel(got_ref, left_ref, right_ref, msg_ref, tri_scr, gl_scr, gr_scr):
    n_row, n_col, fold, lanes = got_ref.shape
    rows = msg_ref.shape[2]
    total = n_row * rows
    low = low_lanes((n_row, 8, lanes))
    gap = jnp.zeros((n_row // 2, SLOT - 2 * rows, lanes), F32)
    for t in range(n_col // 2):
        even = got_ref[:, 2 * t].astype(F32)
        odd = got_ref[:, 2 * t + 1].astype(F32)
        te, to = half_turn(even), half_turn(odd)
        tile = jnp.concatenate(
            [
                jnp.where(low, even[:, :8], to[:, :8]),
                jnp.where(low, te[:, :8], odd[:, :8]),
                jnp.where(low, even[:, 8:], to[:, 8:]),
            ],
            axis=1,
        ).reshape(n_row // 2, 2 * rows, lanes)
        tile = jnp.concatenate([tile, gap], axis=1).reshape(n_row // 2 * SLOT, lanes)
        tri_scr[:, t * lanes : (t + 1) * lanes] = tile.astype(BF16)
    gl_scr[...] = dot(right_ref[...], tri_scr[...], LAST)
    gr_scr[...] = dot(left_ref[...], tri_scr[...])
    low = low_lanes((total, lanes))
    for t in range(n_col // 2):
        a = gl_scr[:, t * lanes : (t + 1) * lanes]
        b = gr_scr[:, t * lanes : (t + 1) * lanes]
        even = jnp.where(low, a, half_turn(b)).reshape(n_row, rows, lanes)
        odd = jnp.where(low, half_turn(a), b).reshape(n_row, rows, lanes)
        msg_ref[:, 2 * t] = even.astype(BF16)
        msg_ref[:, 2 * t + 1] = odd.astype(BF16)


def pair_grad_kernel(got_ref, coef_ref, unit_ref, inv_ref, gn_ref, par_ref, w_in_ref, out_ref, scr):
    hidden, rows, lanes = got_ref.shape
    _, cols, width = out_ref.shape
    eye = identity(hidden)
    gain = par_ref[0:1, :]
    w_in = w_in_ref[...]
    scr[...] = got_ref[...].astype(F32).reshape(hidden * rows, lanes)
    for start in range(0, rows, GROUP):
        size = GROUP * cols
        at = slice(start * cols, start * cols + size)
        left, right = [], []
        for k in range(start, start + GROUP):
            both = dot(eye, scr[pl.ds(k, hidden, stride=rows), :].astype(BF16), LAST)
            left.append(both[:cols])
            right.append(both[SLOT : SLOT + cols])
        left, right = jnp.concatenate(left, axis=0), jnp.concatenate(right, axis=0)
        grad_proj = jnp.concatenate(
            [
                (side * coef_ref[n, at, :]).astype(BF16)
                for n, side in enumerate((left, left, right, right))
            ],
            axis=1,
        )
        s = (dot(grad_proj, w_in, LAST) + gn_ref[at, :]) * gain
        unit = unit_ref[at, :]
        grad = inv_ref[at, :] * (
            s
            - jnp.mean(s, axis=-1, keepdims=True)
            - unit * jnp.mean(s * unit, axis=-1, keepdims=True)
        )
        out_ref[start : start + GROUP] = grad.astype(BF16).reshape(GROUP, cols, width)


def call(kernel, ins, outs, scratch=(), scalars=0, limit=24, flops=0, moved=0):
    smem = pl.BlockSpec(memory_space=pltpu.SMEM)
    vmem = pl.BlockSpec(memory_space=pltpu.VMEM)
    return pl.pallas_call(
        kernel,
        out_shape=[jax.ShapeDtypeStruct(s, d) for s, d in outs],
        in_specs=[smem] * scalars + [vmem] * (len(ins) - scalars),
        out_specs=[vmem] * len(outs),
        scratch_shapes=[pltpu.VMEM(s, d) for s, d in scratch],
        compiler_params=pltpu.CompilerParams(vmem_limit_bytes=limit * MIB),
        cost_estimate=pl.CostEstimate(flops=flops, bytes_accessed=moved, transcendentals=0),
    )(*ins)


def exchange(x):
    return lax.all_to_all(x, ("row", "col"), 0, 0, tiled=True)


def local(pair, chain_lengths, cotangent, norm_params, w_in, w_gate, w_out):
    rows, cols, width = pair.shape
    hidden = w_out.shape[0]
    n_row, n_col = lax.axis_size("row"), lax.axis_size("col")
    assert hidden == n_row * n_col == 2 * SLOT and width == hidden
    assert rows == 24 and cols == 2 * rows
    size, lanes, fold = rows * cols, 2 * SLOT, 16
    total, wide = n_row * rows, n_col * SLOT
    ids = jnp.stack([lax.axis_index("row") * rows, lax.axis_index("col") * cols]).astype(jnp.int32)

    msg, normed = call(
        factors_kernel,
        (ids, chain_lengths, pair, norm_params, w_in),
        [((hidden, rows, lanes), BF16), ((rows, cols, width), BF16)],
        [((hidden * rows, lanes), F32)],
        scalars=2,
        flops=2 * size * width * 4 * hidden,
        moved=8 * MIB,
    )
    got = exchange(msg)
    flat = ((size, width), F32)
    gate, scaled, coef, unit, inverse = call(
        saved_kernel,
        (ids, chain_lengths, pair, normed, cotangent, norm_params, w_in, w_gate, w_out),
        [flat, flat, ((4, size, hidden), F32), flat, flat],
        scalars=2,
        flops=2 * size * width * 6 * hidden,
        moved=24 * MIB,
    )
    msg, left, right = call(
        triangle_kernel,
        (got.reshape(n_row, n_col, rows, lanes),),
        [((n_row, n_col, fold, lanes), BF16), ((total, wide), BF16), ((total, wide), BF16)],
        [((wide, wide), F32)],
        flops=2 * total * wide * wide,
        moved=4 * MIB,
    )
    got = exchange(msg.reshape(hidden, fold, lanes))
    msg, tri_normed = call(
        norm_kernel,
        (got, scaled, norm_params),
        [((hidden, fold, lanes), BF16), ((rows, cols, width), BF16)],
        [((hidden * fold, lanes), F32)] * 2,
        flops=2 * size * width * hidden,
        moved=4 * MIB,
    )
    got = exchange(msg)
    update, grad_normed = call(
        update_kernel,
        (tri_normed, gate, cotangent, w_out, w_gate),
        [((rows, cols, width), BF16), flat],
        flops=4 * size * width * hidden,
        moved=12 * MIB,
    )
    (msg,) = call(
        factor_grads_kernel,
        (got.reshape(n_row, n_col, fold, lanes), left, right),
        [((n_row, n_col, rows, lanes), BF16)],
        [((wide, wide), BF16), ((total, wide), F32), ((total, wide), F32)],
        flops=4 * total * wide * wide,
        moved=4 * MIB,
    )
    got = exchange(msg.reshape(hidden, rows, lanes))
    (grad_pair,) = call(
        pair_grad_kernel,
        (got, coef, unit, inverse, grad_normed, norm_params, w_in),
        [((rows, cols, width), BF16)],
        [((hidden * rows, lanes), F32)],
        flops=2 * size * width * 4 * hidden,
        moved=8 * MIB,
    )
    return (update, grad_pair)


def solution(mesh):
    block = P(("rep", "row"), "col", None)
    return jax.shard_map(
        local,
        mesh=mesh,
        in_specs=(block, P("rep"), block, P(), P(), P(), P()),
        out_specs=(block, block),
        check_vma=False,
    )
```

```python
import functools

import jax
import jax.numpy as jnp
from jax import lax
from jax.experimental import pallas as pl
from jax.experimental.pallas import tpu as pltpu
from jax.sharding import PartitionSpec as P

EPS = 1e-05
F32 = jnp.float32
BF16 = jnp.bfloat16
MIB = 1 << 20
LAST = (((1,), (1,)), ((), ()))
FIRST = (((0,), (0,)), ((), ()))
SLOT = 64
GROUP = 4


def dot(a, b, dims=(((1,), (0,)), ((), ()))):
    return lax.dot_general(a, b, dims, preferred_element_type=F32)


def identity(n):
    row = lax.broadcasted_iota(jnp.int32, (n, n), 0)
    col = lax.broadcasted_iota(jnp.int32, (n, n), 1)
    return jnp.where(row == col, 1.0, 0.0).astype(BF16)


def low_lanes(shape):
    return lax.broadcasted_iota(jnp.int32, shape, len(shape) - 1) < SLOT


def half_turn(x):
    return pltpu.roll(x, SLOT, x.ndim - 1)


def unit_of(x):
    mean = jnp.mean(x, axis=-1, keepdims=True)
    centered = x - mean
    variance = jnp.mean(centered * centered, axis=-1, keepdims=True)
    inverse = lax.rsqrt(variance + EPS)
    return centered * inverse, inverse


def mask_of(ids_ref, len_ref, row, shape):
    limit = len_ref[0]
    for i in range(1, len_ref.shape[0]):
        limit = limit + len_ref[i]
    bound = jnp.where(ids_ref[0] + row < limit, limit - ids_ref[1], 0)
    return lax.broadcasted_iota(jnp.int32, shape, 0) < bound


def start(source, target, sem):
    copy = pltpu.make_async_copy(source, target, sem)
    copy.start()
    return copy


def paired(first, second):
    gap = jnp.zeros((SLOT - first.shape[0], first.shape[1]), first.dtype)
    return jnp.concatenate([first, gap, second, gap], axis=0)


def factors_kernel(
    ids_ref, len_ref, pair_ref, par_ref, w_ref, msg_ref,
    scr, pair_buf, par_buf, w_buf, len_buf, sems,
):
    rows, cols, width = pair_ref.shape
    hidden = w_ref.shape[1] // 4
    sources = (pair_ref, w_ref, par_ref, len_ref)
    targets = (pair_buf, w_buf, par_buf, len_buf)
    copies = [start(x, y, sems.at[n]) for n, (x, y) in enumerate(zip(sources, targets))]
    eye = identity(hidden)
    for copy in copies:
        copy.wait()
    gain, shift = par_buf[0:1, :], par_buf[1:2, :]
    w = w_buf[...]
    for first in range(0, rows, GROUP):
        x = pair_buf[first : first + GROUP].astype(F32).reshape(GROUP * cols, width)
        unit, _ = unit_of(x)
        normed = (unit * gain + shift).astype(BF16)
        proj = dot(normed, w)
        left = jax.nn.sigmoid(proj[:, :hidden]) * proj[:, hidden : 2 * hidden]
        right = jax.nn.sigmoid(proj[:, 2 * hidden : 3 * hidden]) * proj[:, 3 * hidden :]
        for k in range(GROUP):
            mask = mask_of(ids_ref, len_buf, first + k, (cols, hidden))
            at = slice(k * cols, (k + 1) * cols)
            one = jnp.where(mask, left[at], 0.0).astype(BF16)
            two = jnp.where(mask, right[at], 0.0).astype(BF16)
            scr[pl.ds(first + k, hidden, stride=rows), :] = dot(eye, paired(one, two), LAST)
    msg_ref[...] = scr[...].reshape(hidden, rows, 2 * SLOT).astype(BF16)


def saved_kernel(
    ids_ref, len_ref, pair_ref, after_ref, cot_ref, par_ref, w_in_ref, w_gate_ref, w_out_ref,
    gate_ref, scaled_ref, coef_ref, unit_ref, inv_ref,
):
    rows, cols, width = pair_ref.shape
    hidden = w_in_ref.shape[1] // 4
    w_in, w_gate, w_out = w_in_ref[...], w_gate_ref[...], w_out_ref[...]
    for first in range(0, rows, GROUP):
        size = GROUP * cols
        at = slice(first * cols, first * cols + size)
        x = pair_ref[first : first + GROUP].astype(F32).reshape(size, width)
        unit, inverse = unit_of(x)
        unit_ref[at, :] = unit
        inv_ref[at, :] = jnp.broadcast_to(inverse, (size, width))
        normed = (unit * par_ref[0:1, :] + par_ref[1:2, :]).astype(BF16)
        gate = jax.nn.sigmoid(dot(normed, w_gate))
        gate_ref[at, :] = gate
        cot = cot_ref[first : first + GROUP].astype(F32).reshape(size, width)
        grad_lin = (cot * gate).astype(BF16)
        scaled = dot(grad_lin, w_out, LAST) * par_ref[2:3, :]
        scaled_ref[at, :] = scaled - jnp.mean(scaled, axis=-1, keepdims=True)
        proj = dot(normed, w_in)
        mask = jnp.concatenate(
            [
                jnp.where(mask_of(ids_ref, len_ref, first + k, (cols, hidden)), 1.0, 0.0)
                for k in range(GROUP)
            ],
            axis=0,
        )
        for side in range(2):
            sig = jax.nn.sigmoid(proj[:, 2 * side * hidden : (2 * side + 1) * hidden])
            val = proj[:, (2 * side + 1) * hidden : (2 * side + 2) * hidden]
            kept = mask * sig
            coef_ref[2 * side, at, :] = kept * val * (1.0 - sig)
            coef_ref[2 * side + 1, at, :] = kept


def triangle_kernel(got_ref, msg_ref, left_ref, right_ref, tri_scr, left_buf, right_buf, sems):
    n_row, n_col, rows, lanes = got_ref.shape
    total = n_row * rows
    low = low_lanes((total, lanes))
    for t in range(n_col // 2):
        even = got_ref[:, 2 * t].astype(F32).reshape(total, lanes)
        odd = got_ref[:, 2 * t + 1].astype(F32).reshape(total, lanes)
        at = slice(t * lanes, (t + 1) * lanes)
        left_buf[:, at] = jnp.where(low, even, half_turn(odd)).astype(BF16)
        right_buf[:, at] = jnp.where(low, half_turn(even), odd).astype(BF16)
    copies = [start(left_buf, left_ref, sems.at[0]), start(right_buf, right_ref, sems.at[1])]
    tri_scr[...] = dot(left_buf[...], right_buf[...], FIRST)
    low = low_lanes((n_row, 8, lanes))
    for t in range(n_col // 2):
        tile = tri_scr[:, t * lanes : (t + 1) * lanes].reshape(n_row // 2, SLOT, lanes)
        tile = tile[:, : 2 * rows].reshape(n_row, rows, lanes)
        turned = half_turn(tile)
        a, b, c = tile[:, 0:8], tile[:, 8:16], tile[:, 16:24]
        ra, rb, rc = turned[:, 0:8], turned[:, 8:16], turned[:, 16:24]
        msg_ref[:, 2 * t] = jnp.concatenate([jnp.where(low, a, rb), c], axis=1).astype(BF16)
        msg_ref[:, 2 * t + 1] = jnp.concatenate([jnp.where(low, ra, b), rc], axis=1).astype(BF16)
    for copy in copies:
        copy.wait()


def norm_kernel(
    got_ref, scaled_ref, par_ref, msg_ref, tn_ref,
    scr_in, scr_out, tri_buf, grad_buf, scaled_buf, par_buf, tn_buf, sems,
):
    hidden, fold, lanes = got_ref.shape
    rows, cols, _ = tn_ref.shape
    copies = [start(par_ref, par_buf, sems.at[0]), start(scaled_ref, scaled_buf, sems.at[1])]
    eye = identity(hidden)
    scr_in[...] = got_ref[...].astype(F32).reshape(hidden * fold, lanes)
    for s in range(fold):
        tri = dot(eye, scr_in[pl.ds(s, hidden, stride=fold), :].astype(BF16), LAST)
        if s < 8:
            tri_buf[s * cols : (s + 1) * cols, :] = tri[:cols]
            tri_buf[(s + 8) * cols : (s + 9) * cols, :] = tri[SLOT : SLOT + cols]
        else:
            tri_buf[(s + 8) * cols : (s + 9) * cols, :] = tri[:cols]
    for copy in copies:
        copy.wait()
    gain, shift = par_buf[2:3, :], par_buf[3:4, :]
    size = GROUP * cols
    for first in range(0, rows, GROUP):
        at = slice(first * cols, first * cols + size)
        unit, inverse = unit_of(tri_buf[at, :])
        tn = (unit * gain + shift).astype(BF16)
        tn_buf[first : first + GROUP] = tn.reshape(GROUP, cols, hidden)
        s = scaled_buf[at, :]
        grad = inverse * (s - unit * jnp.mean(s * unit, axis=-1, keepdims=True))
        grad_buf[at, :] = grad.astype(BF16)
    copy = start(tn_buf, tn_ref, sems.at[2])
    nothing = jnp.zeros((cols, hidden), BF16)
    for s in range(fold):
        if s < 8:
            first = grad_buf[s * cols : (s + 1) * cols, :]
            second = grad_buf[(s + 8) * cols : (s + 9) * cols, :]
        else:
            first = grad_buf[(s + 8) * cols : (s + 9) * cols, :]
            second = nothing
        scr_out[pl.ds(s, hidden, stride=fold), :] = dot(eye, paired(first, second), LAST)
    msg_ref[...] = scr_out[...].reshape(hidden, fold, lanes).astype(BF16)
    copy.wait()


def update_kernel(tn_ref, gate_ref, cot_ref, w_out_ref, w_gate_ref, update_ref, gn_ref):
    rows, cols, width = cot_ref.shape
    w_out, w_gate = w_out_ref[...], w_gate_ref[...]
    for first in range(0, rows, GROUP):
        size = GROUP * cols
        at = slice(first * cols, first * cols + size)
        lin = dot(tn_ref[first : first + GROUP].reshape(size, -1), w_out)
        gate = gate_ref[at, :]
        update_ref[first : first + GROUP] = (gate * lin).astype(BF16).reshape(GROUP, cols, width)
        cot = cot_ref[first : first + GROUP].astype(F32).reshape(size, width)
        grad_gate = (cot * lin * gate * (1.0 - gate)).astype(BF16)
        gn_ref[at, :] = dot(grad_gate, w_gate, LAST)


def factor_grads_kernel(
    got_ref, left_ref, right_ref, msg_ref, tri_scr, gl_scr, gr_scr, left_buf, right_buf, sems
):
    n_row, n_col, fold, lanes = got_ref.shape
    copies = [start(right_ref, right_buf, sems.at[0]), start(left_ref, left_buf, sems.at[1])]
    rows = msg_ref.shape[2]
    total = n_row * rows
    low = low_lanes((n_row, 8, lanes))
    gap = jnp.zeros((n_row // 2, SLOT - 2 * rows, lanes), F32)
    for t in range(n_col // 2):
        even = got_ref[:, 2 * t].astype(F32)
        odd = got_ref[:, 2 * t + 1].astype(F32)
        te, to = half_turn(even), half_turn(odd)
        tile = jnp.concatenate(
            [
                jnp.where(low, even[:, :8], to[:, :8]),
                jnp.where(low, te[:, :8], odd[:, :8]),
                jnp.where(low, even[:, 8:], to[:, 8:]),
            ],
            axis=1,
        ).reshape(n_row // 2, 2 * rows, lanes)
        tile = jnp.concatenate([tile, gap], axis=1).reshape(n_row // 2 * SLOT, lanes)
        tri_scr[:, t * lanes : (t + 1) * lanes] = tile.astype(BF16)
    copies[0].wait()
    gl_scr[...] = dot(right_buf[...], tri_scr[...], LAST)
    copies[1].wait()
    gr_scr[...] = dot(left_buf[...], tri_scr[...])
    low = low_lanes((total, lanes))
    for t in range(n_col // 2):
        a = gl_scr[:, t * lanes : (t + 1) * lanes]
        b = gr_scr[:, t * lanes : (t + 1) * lanes]
        even = jnp.where(low, a, half_turn(b)).reshape(n_row, rows, lanes)
        odd = jnp.where(low, half_turn(a), b).reshape(n_row, rows, lanes)
        msg_ref[:, 2 * t] = even.astype(BF16)
        msg_ref[:, 2 * t + 1] = odd.astype(BF16)


def pair_grad_kernel(
    got_ref, coef_ref, unit_ref, inv_ref, gn_ref, par_ref, w_in_ref, out_ref,
    scr, left_buf, right_buf, coef_buf, unit_buf, inv_buf, gn_buf, par_buf, w_buf, sems,
):
    hidden, rows, lanes = got_ref.shape
    _, cols, width = out_ref.shape
    sources = (coef_ref, gn_ref, unit_ref, inv_ref, w_in_ref, par_ref)
    targets = (coef_buf, gn_buf, unit_buf, inv_buf, w_buf, par_buf)
    copies = [start(x, y, sems.at[n]) for n, (x, y) in enumerate(zip(sources, targets))]
    eye = identity(hidden)
    scr[...] = got_ref[...].astype(F32).reshape(hidden * rows, lanes)
    for k in range(rows):
        both = dot(eye, scr[pl.ds(k, hidden, stride=rows), :].astype(BF16), LAST)
        left_buf[k * cols : (k + 1) * cols, :] = both[:cols]
        right_buf[k * cols : (k + 1) * cols, :] = both[SLOT : SLOT + cols]
    for copy in copies:
        copy.wait()
    gain = par_buf[0:1, :]
    w_in = w_buf[...]
    size = GROUP * cols
    for first in range(0, rows, GROUP):
        at = slice(first * cols, first * cols + size)
        left, right = left_buf[at, :], right_buf[at, :]
        grad_proj = jnp.concatenate(
            [
                (side * coef_buf[m, at, :]).astype(BF16)
                for m, side in enumerate((left, left, right, right))
            ],
            axis=1,
        )
        s = (dot(grad_proj, w_in, LAST) + gn_buf[at, :]) * gain
        unit = unit_buf[at, :]
        grad = inv_buf[at, :] * (
            s
            - jnp.mean(s, axis=-1, keepdims=True)
            - unit * jnp.mean(s * unit, axis=-1, keepdims=True)
        )
        out_ref[first : first + GROUP] = grad.astype(BF16).reshape(GROUP, cols, width)


def call(kernel, ins, outs, scratch=(), smem=(), sems=(), limit=24, flops=0, moved=0):
    spaces = {"s": pltpu.SMEM, "v": pltpu.VMEM, "b": pltpu.VMEM, "h": pltpu.HBM}
    extra = [pltpu.SMEM(s, d) for s, d in smem]
    if sems:
        extra.append(pltpu.SemaphoreType.DMA(sems))
    return pl.pallas_call(
        kernel,
        out_shape=[
            jax.ShapeDtypeStruct(s, d) if place == "v" else pltpu.HBM(s, d)
            for s, d, place in outs
        ],
        in_specs=[pl.BlockSpec(memory_space=spaces[place]) for _, place in ins],
        out_specs=[pl.BlockSpec(memory_space=spaces[place]) for _, _, place in outs],
        scratch_shapes=[pltpu.VMEM(s, d) for s, d in scratch] + extra,
        compiler_params=pltpu.CompilerParams(vmem_limit_bytes=limit * MIB),
        cost_estimate=pl.CostEstimate(flops=flops, bytes_accessed=moved, transcendentals=0),
    )(
        *(
            pltpu.with_memory_space_constraint(x, pltpu.HBM) if place == "h" else x
            for x, place in ins
        )
    )


def exchange(x):
    return lax.all_to_all(x, ("row", "col"), 0, 0, tiled=True)


def local(pair, chain_lengths, cotangent, norm_params, w_in, w_gate, w_out):
    rows, cols, width = pair.shape
    hidden = w_out.shape[0]
    n_row, n_col = lax.axis_size("row"), lax.axis_size("col")
    assert hidden == n_row * n_col == 2 * SLOT and width == hidden
    assert rows == 24 and cols == 2 * rows
    size, lanes, fold = rows * cols, 2 * SLOT, 16
    total, wide = n_row * rows, n_col * SLOT
    ids = jnp.stack([lax.axis_index("row") * rows, lax.axis_index("col") * cols]).astype(jnp.int32)

    flat = (size, width)
    block = (rows, cols, width)
    par = (norm_params.shape, F32)
    (msg,) = call(
        factors_kernel,
        [(ids, "s"), (chain_lengths, "h"), (pair, "h"), (norm_params, "h"), (w_in, "h")],
        [((hidden, rows, lanes), BF16, "v")],
        [((hidden * rows, lanes), F32), (block, BF16), par, (w_in.shape, BF16)],
        smem=[(chain_lengths.shape, jnp.int32)],
        sems=(4,),
        flops=2 * size * width * 4 * hidden,
        moved=8 * MIB,
    )
    got = exchange(msg)
    msg, left, right = call(
        triangle_kernel,
        [(got.reshape(n_row, n_col, rows, lanes), "v")],
        [((n_row, n_col, fold, lanes), BF16, "v")] + [((total, wide), BF16, "h")] * 2,
        [((wide, wide), F32)] + [((total, wide), BF16)] * 2,
        sems=(2,),
        flops=2 * total * wide * wide,
        moved=4 * MIB,
    )
    got = exchange(msg.reshape(hidden, fold, lanes))
    gate, scaled, coef, unit, inverse = call(
        saved_kernel,
        [(ids, "s"), (chain_lengths, "s"), (pair, "v"), (left, "h"), (cotangent, "v"), (norm_params, "v")]
        + [(w_in, "v"), (w_gate, "v"), (w_out, "v")],
        [(flat, F32, "b"), (flat, F32, "b"), ((4,) + flat, F32, "b")] + [(flat, F32, "b")] * 2,
        flops=2 * size * width * 6 * hidden,
        moved=24 * MIB,
    )
    msg, tri_normed = call(
        norm_kernel,
        [(got, "v"), (scaled, "h"), (norm_params, "h")],
        [((hidden, fold, lanes), BF16, "v"), (block, BF16, "h")],
        [((hidden * fold, lanes), F32)] * 2
        + [(flat, F32), (flat, BF16), (flat, F32), par, (block, BF16)],
        sems=(3,),
        flops=2 * size * width * hidden,
        moved=4 * MIB,
    )
    got = exchange(msg)
    update, grad_normed = call(
        update_kernel,
        [(tri_normed, "v"), (gate, "v"), (cotangent, "v"), (w_out, "v"), (w_gate, "v")],
        [(block, BF16, "b"), (flat, F32, "b")],
        flops=4 * size * width * hidden,
        moved=12 * MIB,
    )
    (msg,) = call(
        factor_grads_kernel,
        [(got.reshape(n_row, n_col, fold, lanes), "v"), (left, "h"), (right, "h")],
        [((n_row, n_col, rows, lanes), BF16, "v")],
        [((wide, wide), BF16)] + [((total, wide), F32)] * 2 + [((total, wide), BF16)] * 2,
        sems=(2,),
        flops=4 * total * wide * wide,
        moved=4 * MIB,
    )
    got = exchange(msg.reshape(hidden, rows, lanes))
    (grad_pair,) = call(
        pair_grad_kernel,
        [(got, "v"), (coef, "h"), (unit, "h"), (inverse, "h"), (grad_normed, "h")]
        + [(norm_params, "h"), (w_in, "h")],
        [(block, BF16, "v")],
        [((hidden * rows, lanes), F32), (flat, F32), (flat, F32), ((4,) + flat, F32)]
        + [(flat, F32)] * 3
        + [par, (w_in.shape, BF16)],
        sems=(6,),
        flops=2 * size * width * 4 * hidden,
        moved=8 * MIB,
    )
    return (update, grad_pair)


def solution(mesh):
    block = P(("rep", "row"), "col", None)
    return jax.shard_map(
        local,
        mesh=mesh,
        in_specs=(block, P("rep"), block, P(), P(), P(), P()),
        out_specs=(block, block),
        check_vma=False,
    )
```

```python
import jax
import jax.numpy as jnp
from jax import lax
from jax.experimental import pallas as pl
from jax.experimental.pallas import tpu as pltpu
from jax.sharding import Mesh
from jax.sharding import PartitionSpec as P

EPS = 1e-05
F32 = jnp.float32
BF16 = jnp.bfloat16
MIB = 1 << 20
LAST = (((1,), (1,)), ((), ()))
FIRST = (((0,), (0,)), ((), ()))
SLOT = 64
GROUP = 4


def dot(a, b, dims=(((1,), (0,)), ((), ()))):
    return lax.dot_general(a, b, dims, preferred_element_type=F32)


def identity(n):
    row = lax.broadcasted_iota(jnp.int32, (n, n), 0)
    col = lax.broadcasted_iota(jnp.int32, (n, n), 1)
    return jnp.where(row == col, 1.0, 0.0).astype(BF16)


def low_lanes(shape):
    return lax.broadcasted_iota(jnp.int32, shape, len(shape) - 1) < SLOT


def half_turn(x):
    return pltpu.roll(x, SLOT, x.ndim - 1)


def unit_of(x):
    mean = jnp.mean(x, axis=-1, keepdims=True)
    centered = x - mean
    variance = jnp.mean(centered * centered, axis=-1, keepdims=True)
    inverse = lax.rsqrt(variance + EPS)
    return centered * inverse, inverse


def mask_of(ids_ref, len_ref, row, shape):
    limit = len_ref[0]
    for i in range(1, len_ref.shape[0]):
        limit = limit + len_ref[i]
    bound = jnp.where(ids_ref[0] + row < limit, limit - ids_ref[1], 0)
    return lax.broadcasted_iota(jnp.int32, shape, 0) < bound


def start(source, target, sem):
    copy = pltpu.make_async_copy(source, target, sem)
    copy.start()
    return copy


def paired(first, second):
    gap = jnp.zeros((SLOT - first.shape[0], first.shape[1]), first.dtype)
    return jnp.concatenate([first, gap, second, gap], axis=0)


def factors_kernel(
    ids_ref, len_ref, pair_ref, par_ref, w_ref, msg_ref,
    scr, pair_buf, par_buf, w_buf, len_buf, sems,
):
    rows, cols, width = pair_ref.shape
    hidden = w_ref.shape[1] // 4
    half = hidden // 2
    sources = (pair_ref, w_ref, par_ref, len_ref)
    targets = (pair_buf, w_buf, par_buf, len_buf)
    copies = [start(x, y, sems.at[n]) for n, (x, y) in enumerate(zip(sources, targets))]
    eye = identity(hidden)
    for copy in copies:
        copy.wait()
    gain, shift = par_buf[0:1, :], par_buf[1:2, :]
    w = w_buf[...]
    for first in range(0, rows, GROUP):
        x = pair_buf[first : first + GROUP].astype(F32).reshape(GROUP * cols, width)
        unit, _ = unit_of(x)
        normed = (unit * gain + shift).astype(BF16)
        proj = dot(normed, w)
        left = jax.nn.sigmoid(proj[:, :hidden]) * proj[:, hidden : 2 * hidden]
        right = jax.nn.sigmoid(proj[:, 2 * hidden : 3 * hidden]) * proj[:, 3 * hidden :]
        for k in range(GROUP):
            mask = mask_of(ids_ref, len_buf, first + k, (cols, hidden))
            at = slice(k * cols, (k + 1) * cols)
            one = jnp.where(mask, left[at], 0.0).astype(BF16)
            two = jnp.where(mask, right[at], 0.0).astype(BF16)
            turned = dot(eye, paired(one, two), LAST)
            scr[pl.ds(first + k, half, stride=2 * rows), :] = turned[:half]
            scr[pl.ds(rows + first + k, half, stride=2 * rows), :] = turned[half:]
    msg_ref[...] = scr[...].reshape(msg_ref.shape).astype(BF16)


def saved_kernel(
    ids_ref, len_ref, pair_ref, after_ref, cot_ref, par_ref, w_in_ref, w_gate_ref, w_out_ref,
    gate_ref, scaled_ref, coef_ref, unit_ref, inv_ref, scr,
):
    rows, cols, width = pair_ref.shape
    hidden = w_in_ref.shape[1] // 4
    half = hidden // 2
    low = low_lanes((half, 2 * SLOT))
    w_in, w_gate, w_out = w_in_ref[...], w_gate_ref[...], w_out_ref[...]
    for first in range(0, rows, GROUP):
        size = GROUP * cols
        at = slice(first * cols, first * cols + size)
        x = pair_ref[first : first + GROUP].astype(F32).reshape(size, width)
        unit, inverse = unit_of(x)
        unit_ref[at, :] = unit
        inv_ref[at, :] = jnp.broadcast_to(inverse, (size, width))
        normed = (unit * par_ref[0:1, :] + par_ref[1:2, :]).astype(BF16)
        gate = jax.nn.sigmoid(dot(normed, w_gate))
        gate_ref[at, :] = gate
        cot = cot_ref[first : first + GROUP].astype(F32).reshape(size, width)
        grad_lin = (cot * gate).astype(BF16)
        scaled = dot(grad_lin, w_out, LAST) * par_ref[2:3, :]
        scaled = scaled - jnp.mean(scaled, axis=-1, keepdims=True)
        proj = dot(normed, w_in)
        masks = []
        for k in range(GROUP):
            one = scaled[k * cols : (k + 1) * cols]
            turned = jnp.transpose(paired(one, one))
            turned = jnp.where(low, turned[:half], turned[half:])
            scr[pl.ds(first + k, half, stride=rows), :] = turned
            mask = mask_of(ids_ref, len_ref, first + k, (cols, hidden))
            masks.append(jnp.where(mask, 1.0, 0.0))
        mask = jnp.concatenate(masks, axis=0)
        for side in range(2):
            sig = jax.nn.sigmoid(proj[:, 2 * side * hidden : (2 * side + 1) * hidden])
            val = proj[:, (2 * side + 1) * hidden : (2 * side + 2) * hidden]
            kept = mask * sig
            coef_ref[2 * side, at, :] = kept * val * (1.0 - sig)
            coef_ref[2 * side + 1, at, :] = kept
    scaled_ref[...] = scr[...].reshape(scaled_ref.shape)


def triangle_kernel(
    ids_ref, own_ref, other_ref, msg_ref, left_ref, right_ref, tri_scr, left_buf, right_buf, sems
):
    n_row, n_y, _, rows, lanes = own_ref.shape
    total = n_row * rows
    core = ids_ref[2]
    low = low_lanes((total, lanes))
    for side, ref in enumerate((own_ref, other_ref)):
        for c in range(2):
            for t in range(n_y // 2):
                even = ref[:, 2 * t, c].astype(F32).reshape(total, lanes)
                odd = ref[:, 2 * t + 1, c].astype(F32).reshape(total, lanes)
                at = slice(t * lanes, (t + 1) * lanes)
                left_buf[c, side, :, at] = jnp.where(low, even, half_turn(odd)).astype(BF16)
                right_buf[c, side, :, at] = jnp.where(low, half_turn(even), odd).astype(BF16)
    copies = [start(left_buf, left_ref, sems.at[0]), start(right_buf, right_ref, sems.at[1])]
    low = low_lanes((n_y, 2, rows, lanes))
    for side in range(2):
        for c in range(2):
            tri_scr[side, c] = dot(left_buf[c, side], right_buf[c, 0], FIRST)
    for side in range(2):
        place = core if side == 0 else 1 - core
        for t in range(n_y // 2):
            a, b = (
                tri_scr[side, c, :, t * lanes : (t + 1) * lanes]
                .reshape(n_y, SLOT, lanes)[:, : 2 * rows]
                .reshape(n_y, 2, rows, lanes)
                for c in range(2)
            )
            msg_ref[:, place, :, 2 * t] = jnp.where(low, a, half_turn(b)).astype(BF16)
            msg_ref[:, place, :, 2 * t + 1] = jnp.where(low, half_turn(a), b).astype(BF16)
    for copy in copies:
        copy.wait()


def norm_kernel(got_ref, scaled_ref, msg_ref, scr, scaled_buf, sems):
    half, rows, lanes = got_ref.shape
    copy = start(scaled_ref, scaled_buf, sems.at[0])
    scr[...] = got_ref[...].astype(F32)

    def mean(x):
        part = jnp.sum(x, axis=0)
        return (part + half_turn(part)) * (1.0 / (2 * half))

    copy.wait()
    for first in range(0, rows, 8):
        at = slice(first, first + 8)
        x = scr[:, at]
        x = x - mean(x)[None]
        inverse = lax.rsqrt(mean(x * x) + EPS)
        s = scaled_buf[:, at]
        along = inverse * inverse * mean(s * x)
        scr[:, at] = inverse[None] * (s - x * along[None])
    msg_ref[...] = scr[...].astype(BF16)


def update_kernel(
    got_ref, gate_ref, cot_ref, par_ref, w_out_ref, w_gate_ref, update_ref, gn_ref, scr
):
    rows, cols, width = cot_ref.shape
    half, _, lanes = got_ref.shape
    w_out, w_gate = w_out_ref[...], w_gate_ref[...]
    gain, shift = par_ref[2:3, :], par_ref[3:4, :]
    eye = identity(lanes)
    pick = jnp.concatenate([eye[:cols], eye[SLOT : SLOT + cols]], axis=1)
    nothing = jnp.zeros((half, lanes), BF16)
    scr[...] = got_ref[...].astype(F32).reshape(half * rows, lanes)
    for first in range(0, rows, GROUP):
        size = GROUP * cols
        at = slice(first * cols, first * cols + size)
        tri = []
        for k in range(first, first + GROUP):
            x = scr[pl.ds(k, half, stride=rows), :].astype(BF16)
            both = jnp.concatenate(
                [jnp.concatenate([x, nothing], axis=1), jnp.concatenate([nothing, x], axis=1)],
                axis=0,
            )
            tri.append(dot(pick, both, LAST))
        unit, _ = unit_of(jnp.concatenate(tri, axis=0))
        lin = dot((unit * gain + shift).astype(BF16), w_out)
        gate = gate_ref[at, :]
        update_ref[first : first + GROUP] = (gate * lin).astype(BF16).reshape(GROUP, cols, width)
        cot = cot_ref[first : first + GROUP].astype(F32).reshape(size, width)
        grad_gate = (cot * lin * gate * (1.0 - gate)).astype(BF16)
        gn_ref[at, :] = dot(grad_gate, w_gate, LAST)


def factor_grads_kernel(
    ids_ref, own_ref, other_ref, left_ref, right_ref, msg_ref,
    tri_scr, gl_scr, gr_scr, left_buf, right_buf, sems,
):
    n_y, _, _, _, rows, lanes = own_ref.shape
    n_row = msg_ref.shape[0]
    total = n_row * rows
    core = ids_ref[2]
    copies = [start(right_ref, right_buf, sems.at[0]), start(left_ref, left_buf, sems.at[1])]
    low = low_lanes((n_y, 2, rows, lanes))
    gap = jnp.zeros((n_y, SLOT - 2 * rows, lanes), F32)
    for n, (ref, place) in enumerate(((own_ref, core), (own_ref, 1 - core), (other_ref, core))):
        for t in range(n_y // 2):
            even = ref[:, place, :, 2 * t].astype(F32)
            odd = ref[:, place, :, 2 * t + 1].astype(F32)
            first = jnp.where(low, even, half_turn(odd))
            second = jnp.where(low, half_turn(even), odd)
            for c, tile in enumerate((first, second)):
                tile = jnp.concatenate([tile.reshape(n_y, 2 * rows, lanes), gap], axis=1)
                tile = tile.reshape(n_y * SLOT, lanes).astype(BF16)
                tri_scr[c, n, :, t * lanes : (t + 1) * lanes] = tile
    for copy in copies:
        copy.wait()
    for c in range(2):
        gl_scr[c] = dot(right_buf[c, 0], tri_scr[c, 0], LAST) + dot(
            right_buf[c, 1], tri_scr[c, 2], LAST
        )
        gr_scr[c] = dot(left_buf[c, 0], tri_scr[c, 0]) + dot(left_buf[c, 1], tri_scr[c, 1])
    low = low_lanes((total, lanes))
    for c in range(2):
        for t in range(n_y // 2):
            a = gl_scr[c, :, t * lanes : (t + 1) * lanes]
            b = gr_scr[c, :, t * lanes : (t + 1) * lanes]
            even = jnp.where(low, a, half_turn(b)).reshape(n_row, rows, lanes)
            odd = jnp.where(low, half_turn(a), b).reshape(n_row, rows, lanes)
            msg_ref[:, 2 * t, c] = even.astype(BF16)
            msg_ref[:, 2 * t + 1, c] = odd.astype(BF16)


def pair_grad_kernel(
    got_ref, coef_ref, unit_ref, inv_ref, gn_ref, par_ref, w_in_ref, out_ref,
    scr, left_buf, right_buf, coef_buf, unit_buf, inv_buf, gn_buf, par_buf, w_buf, sems,
):
    half, _, rows, lanes = got_ref.shape
    _, cols, width = out_ref.shape
    sources = (coef_ref, gn_ref, unit_ref, inv_ref, w_in_ref, par_ref)
    targets = (coef_buf, gn_buf, unit_buf, inv_buf, w_buf, par_buf)
    copies = [start(x, y, sems.at[n]) for n, (x, y) in enumerate(zip(sources, targets))]
    eye = identity(2 * half)
    scr[...] = got_ref[...].astype(F32).reshape(2 * half * rows, lanes)
    for k in range(rows):
        both = jnp.concatenate(
            [scr[pl.ds(c * rows + k, half, stride=2 * rows), :] for c in range(2)], axis=0
        )
        both = dot(eye, both.astype(BF16), LAST)
        left_buf[k * cols : (k + 1) * cols, :] = both[:cols]
        right_buf[k * cols : (k + 1) * cols, :] = both[SLOT : SLOT + cols]
    for copy in copies:
        copy.wait()
    gain = par_buf[0:1, :]
    w_in = w_buf[...]
    size = GROUP * cols
    for first in range(0, rows, GROUP):
        at = slice(first * cols, first * cols + size)
        left, right = left_buf[at, :], right_buf[at, :]
        grad_proj = jnp.concatenate(
            [
                (side * coef_buf[m, at, :]).astype(BF16)
                for m, side in enumerate((left, left, right, right))
            ],
            axis=1,
        )
        s = (dot(grad_proj, w_in, LAST) + gn_buf[at, :]) * gain
        unit = unit_buf[at, :]
        grad = inv_buf[at, :] * (
            s
            - jnp.mean(s, axis=-1, keepdims=True)
            - unit * jnp.mean(s * unit, axis=-1, keepdims=True)
        )
        out_ref[first : first + GROUP] = grad.astype(BF16).reshape(GROUP, cols, width)


def call(kernel, ins, outs, scratch=(), smem=(), sems=(), limit=24, flops=0, moved=0):
    spaces = {"s": pltpu.SMEM, "v": pltpu.VMEM, "b": pltpu.VMEM, "h": pltpu.HBM}
    extra = [pltpu.SMEM(s, d) for s, d in smem]
    if sems:
        extra.append(pltpu.SemaphoreType.DMA(sems))
    return pl.pallas_call(
        kernel,
        out_shape=[
            jax.ShapeDtypeStruct(s, d) if place == "v" else pltpu.HBM(s, d)
            for s, d, place in outs
        ],
        in_specs=[pl.BlockSpec(memory_space=spaces[place]) for _, place in ins],
        out_specs=[pl.BlockSpec(memory_space=spaces[place]) for _, _, place in outs],
        scratch_shapes=[pltpu.VMEM(s, d) for s, d in scratch] + extra,
        compiler_params=pltpu.CompilerParams(vmem_limit_bytes=limit * MIB),
        cost_estimate=pl.CostEstimate(flops=flops, bytes_accessed=moved, transcendentals=0),
    )(
        *(
            pltpu.with_memory_space_constraint(x, pltpu.HBM) if place == "h" else x
            for x, place in ins
        )
    )


def exchange(x):
    return lax.all_to_all(x, ("row", "y"), 0, 0, tiled=True)


def swap(x):
    return lax.ppermute(x, "core", [(0, 1), (1, 0)])


def local(pair, chain_lengths, cotangent, norm_params, w_in, w_gate, w_out):
    rows, cols, width = pair.shape
    hidden = w_out.shape[0]
    n_row, n_y = lax.axis_size("row"), lax.axis_size("y")
    assert hidden == 2 * n_row * n_y == 2 * SLOT and width == hidden
    assert rows == 24 and cols == 2 * rows and n_row == 4 * n_y and lax.axis_size("core") == 2
    half = hidden // 2
    size, lanes = rows * cols, 2 * SLOT
    total, wide = n_row * rows, n_y * SLOT
    row, core = lax.axis_index("row"), lax.axis_index("core")
    col = 2 * lax.axis_index("y") + core
    ids = jnp.stack([row * rows, col * cols, core]).astype(jnp.int32)

    flat = (size, width)
    block = (rows, cols, width)
    par = (norm_params.shape, F32)
    factor = (2, 2, total, wide)
    two = (half, 2, rows, lanes)
    one = (half, rows, lanes)
    by_home = (n_row, n_y, 2, rows, lanes)
    by_block = (n_y, 2, 2, n_y, rows, lanes)
    (msg,) = call(
        factors_kernel,
        [(ids, "s"), (chain_lengths, "h"), (pair, "h"), (norm_params, "h"), (w_in, "h")],
        [(two, BF16, "v")],
        [((hidden * rows, lanes), F32), (block, BF16), par, (w_in.shape, BF16)],
        smem=[(chain_lengths.shape, jnp.int32)],
        sems=(4,),
        flops=2 * size * width * 4 * hidden,
        moved=8 * MIB,
    )
    got = exchange(msg)
    msg, left, right = call(
        triangle_kernel,
        [(ids, "s"), (got.reshape(by_home), "v"), (swap(got).reshape(by_home), "v")],
        [(by_block, BF16, "v"), (factor, BF16, "h"), (factor, BF16, "h")],
        [((2, 2, wide, wide), F32), (factor, BF16), (factor, BF16)],
        sems=(2,),
        flops=8 * total * wide * wide,
        moved=4 * MIB,
    )
    got = exchange(msg.reshape(one))
    gate, scaled, coef, unit, inverse = call(
        saved_kernel,
        [(ids, "s"), (chain_lengths, "s"), (pair, "v"), (left, "h"), (cotangent, "v")]
        + [(norm_params, "v"), (w_in, "v"), (w_gate, "v"), (w_out, "v")],
        [(flat, F32, "b"), (one, F32, "b"), ((4,) + flat, F32, "b")] + [(flat, F32, "b")] * 2,
        [((half * rows, lanes), F32)],
        flops=2 * size * width * 6 * hidden,
        moved=24 * MIB,
    )
    (msg,) = call(
        norm_kernel,
        [(got, "v"), (scaled, "h")],
        [(one, BF16, "v")],
        [(one, F32), (one, F32)],
        sems=(1,),
        flops=2 * size * width * hidden,
        moved=4 * MIB,
    )
    update, grad_normed = call(
        update_kernel,
        [(got, "v"), (gate, "v"), (cotangent, "v"), (norm_params, "v"), (w_out, "v")]
        + [(w_gate, "v")],
        [(block, BF16, "b"), (flat, F32, "b")],
        [((half * rows, lanes), F32)],
        flops=4 * size * width * hidden,
        moved=12 * MIB,
    )
    got = exchange(msg)
    (msg,) = call(
        factor_grads_kernel,
        [(ids, "s"), (got.reshape(by_block), "v"), (swap(got).reshape(by_block), "v")]
        + [(left, "h"), (right, "h")],
        [(by_home, BF16, "v")],
        [((2, 3, wide, wide), BF16), ((2, total, wide), F32), ((2, total, wide), F32)]
        + [(factor, BF16), (factor, BF16)],
        sems=(2,),
        flops=16 * total * wide * wide,
        moved=4 * MIB,
    )
    got = exchange(msg.reshape(two))
    (grad_pair,) = call(
        pair_grad_kernel,
        [(got, "v"), (coef, "h"), (unit, "h"), (inverse, "h"), (grad_normed, "h")]
        + [(norm_params, "h"), (w_in, "h")],
        [(block, BF16, "v")],
        [((hidden * rows, lanes), F32), (flat, F32), (flat, F32), ((4,) + flat, F32)]
        + [(flat, F32)] * 3
        + [par, (w_in.shape, BF16)],
        sems=(6,),
        flops=2 * size * width * 4 * hidden,
        moved=8 * MIB,
    )
    return (update, grad_pair)


def solution(mesh):
    n_row, n_col, n_rep = mesh.devices.shape
    mesh = Mesh(mesh.devices.reshape(n_row, n_col // 2, 2, n_rep), ("row", "y", "core", "rep"))
    block = P(("rep", "row"), ("y", "core"), None)
    return jax.shard_map(
        local,
        mesh=mesh,
        in_specs=(block, P("rep"), block, P(), P(), P(), P()),
        out_specs=(block, block),
        check_vma=False,
    )
```

```python
import jax
import jax.numpy as jnp
from jax import lax
from jax.experimental import pallas as pl
from jax.experimental.pallas import tpu as pltpu
from jax.sharding import Mesh
from jax.sharding import PartitionSpec as P

EPS = 1e-05
F32 = jnp.float32
BF16 = jnp.bfloat16
MIB = 1 << 20
LAST = (((1,), (1,)), ((), ()))
FIRST = (((0,), (0,)), ((), ()))
SLOT = 64
PIECE = 16
MSG_ROWS = 40
GROUP = 4


def dot(a, b, dims=(((1,), (0,)), ((), ()))):
    return lax.dot_general(a, b, dims, preferred_element_type=F32)


def identity(n):
    row = lax.broadcasted_iota(jnp.int32, (n, n), 0)
    col = lax.broadcasted_iota(jnp.int32, (n, n), 1)
    return jnp.where(row == col, 1.0, 0.0).astype(BF16)


def low_lanes(shape):
    return lax.broadcasted_iota(jnp.int32, shape, len(shape) - 1) < SLOT


def half_turn(x):
    return turn(x, SLOT)


def turn(x, by):
    return pltpu.roll(x, by % x.shape[-1], x.ndim - 1)


def place_in_slot(shape):
    return lax.rem(lax.broadcasted_iota(jnp.int32, shape, len(shape) - 1), SLOT)


def straight_lanes(ids_ref, shape):
    lane = lax.broadcasted_iota(jnp.int32, shape, len(shape) - 1)
    return jnp.where(lane < SLOT, 0, 1) == ids_ref[3]


def swap_pairs(x):
    return jnp.concatenate([x[n ^ 1][None] for n in range(x.shape[0])], axis=0)


def unit_of(x):
    mean = jnp.mean(x, axis=-1, keepdims=True)
    centered = x - mean
    variance = jnp.mean(centered * centered, axis=-1, keepdims=True)
    inverse = lax.rsqrt(variance + EPS)
    return centered * inverse, inverse


def mask_of(ids_ref, len_ref, row, shape):
    limit = len_ref[0]
    for i in range(1, len_ref.shape[0]):
        limit = limit + len_ref[i]
    bound = jnp.where(ids_ref[0] + row < limit, limit - ids_ref[1], 0)
    return lax.broadcasted_iota(jnp.int32, shape, 0) < bound


def start(source, target, sem):
    copy = pltpu.make_async_copy(source, target, sem)
    copy.start()
    return copy


def paired(first, second):
    gap = jnp.zeros((SLOT - first.shape[0], first.shape[1]), first.dtype)
    return jnp.concatenate([first, gap, second, gap], axis=0)


def factors_kernel(
    ids_ref, len_ref, pair_ref, par_ref, w_ref, msg_ref,
    scr, a_buf, b_buf, pair_buf, par_buf, w_buf, len_buf, sems,
):
    rows, cols, width = pair_ref.shape
    hidden = w_ref.shape[1] // 4
    half = hidden // 2
    sources = (pair_ref, w_ref, par_ref, len_ref)
    targets = (pair_buf, w_buf, par_buf, len_buf)
    copies = [start(x, y, sems.at[n]) for n, (x, y) in enumerate(zip(sources, targets))]
    eye = identity(hidden)
    for copy in copies:
        copy.wait()
    gain, shift = par_buf[0:1, :], par_buf[1:2, :]
    w = w_buf[...]
    straight = straight_lanes(ids_ref, (cols, hidden))
    for first in range(0, rows, GROUP):
        x = pair_buf[first : first + GROUP].astype(F32).reshape(GROUP * cols, width)
        unit, _ = unit_of(x)
        normed = (unit * gain + shift).astype(BF16)
        proj = dot(normed, w)
        left = jax.nn.sigmoid(proj[:, :hidden]) * proj[:, hidden : 2 * hidden]
        right = jax.nn.sigmoid(proj[:, 2 * hidden : 3 * hidden]) * proj[:, 3 * hidden :]
        for k in range(GROUP):
            mask = mask_of(ids_ref, len_buf, first + k, (cols, hidden))
            at = slice(k * cols, (k + 1) * cols)
            one, two = jnp.where(mask, left[at], 0.0), jnp.where(mask, right[at], 0.0)
            a_buf[first + k] = jnp.where(straight, one, two).astype(BF16)
            b_buf[first + k] = jnp.where(straight, two, one).astype(BF16)
    main, tail = 16, 8
    gap = jnp.zeros((2 * PIECE, hidden), BF16)
    low = place_in_slot((half, 2 * SLOT)) < PIECE
    for first in range(0, main + tail, GROUP):
        parts = []
        for s in range(first, first + GROUP):
            if s < main:
                e, at = main + s % tail, pl.ds(s // tail * PIECE, PIECE)
                parts += [a_buf[s], a_buf[e, at], b_buf[s], b_buf[e, at]]
            else:
                at = pl.ds(2 * PIECE, PIECE)
                parts += [a_buf[s, at], a_buf[s, at], gap, b_buf[s, at], b_buf[s, at], gap]
        turned = dot(eye, jnp.concatenate(parts, axis=0), LAST)
        for n, s in enumerate(range(first, first + GROUP)):
            one = turned[:half, n * hidden : (n + 1) * hidden]
            two = turned[half:, n * hidden : (n + 1) * hidden]
            if s < main:
                scr[pl.ds(s, half, stride=MSG_ROWS), :] = one
                scr[pl.ds(main + s, half, stride=MSG_ROWS), :] = two
            else:
                scr[pl.ds(main + s, half, stride=MSG_ROWS), :] = jnp.where(low, one, two)
    msg_ref[...] = scr[...].reshape(msg_ref.shape).astype(BF16)


def saved_kernel(
    ids_ref, len_ref, pair_ref, after_ref, cot_ref, par_ref, w_in_ref, w_gate_ref, w_out_ref,
    gate_ref, scaled_ref, coef_ref, unit_ref, inv_ref, scr,
):
    rows, cols, width = pair_ref.shape
    hidden = w_in_ref.shape[1] // 4
    half = hidden // 2
    first_half = ~straight_lanes(ids_ref, (half, 2 * SLOT))
    w_in, w_gate, w_out = w_in_ref[...], w_gate_ref[...], w_out_ref[...]
    for first in range(0, rows, GROUP):
        size = GROUP * cols
        at = slice(first * cols, first * cols + size)
        x = pair_ref[first : first + GROUP].astype(F32).reshape(size, width)
        unit, inverse = unit_of(x)
        unit_ref[at, :] = unit
        inv_ref[at, :] = jnp.broadcast_to(inverse, (size, width))
        normed = (unit * par_ref[0:1, :] + par_ref[1:2, :]).astype(BF16)
        gate = jax.nn.sigmoid(dot(normed, w_gate))
        gate_ref[at, :] = gate
        cot = cot_ref[first : first + GROUP].astype(F32).reshape(size, width)
        grad_lin = (cot * gate).astype(BF16)
        scaled = dot(grad_lin, w_out, LAST) * par_ref[2:3, :]
        scaled = scaled - jnp.mean(scaled, axis=-1, keepdims=True)
        proj = dot(normed, w_in)
        masks = []
        for k in range(GROUP):
            one = scaled[k * cols : (k + 1) * cols]
            turned = jnp.transpose(paired(one, one))
            turned = jnp.where(first_half, turned[:half], turned[half:])
            scr[pl.ds(first + k, half, stride=rows), :] = turned
            mask = mask_of(ids_ref, len_ref, first + k, (cols, hidden))
            masks.append(jnp.where(mask, 1.0, 0.0))
        mask = jnp.concatenate(masks, axis=0)
        for side in range(2):
            sig = jax.nn.sigmoid(proj[:, 2 * side * hidden : (2 * side + 1) * hidden])
            val = proj[:, (2 * side + 1) * hidden : (2 * side + 2) * hidden]
            kept = mask * sig
            coef_ref[2 * side, at, :] = kept * val * (1.0 - sig)
            coef_ref[2 * side + 1, at, :] = kept
    scaled_ref[...] = scr[...].reshape(scaled_ref.shape)


def triangle_kernel(
    ids_ref, own_ref, other_ref, msg_ref, left_ref, right_ref, tri_scr, left_buf, right_buf, sems
):
    n_row, n_y, _, lanes = own_ref.shape
    n_tile = n_y // 2
    rows = msg_ref.shape[-2]
    total = n_row * rows
    core = ids_ref[2]
    low = low_lanes((total, lanes))
    at_lane = place_in_slot((n_row, 8, lanes))

    def unpacked(ref, y):
        got = ref[:, y].astype(F32)
        tail = got[:, 32:40]
        result = []
        for c in range(2):
            one, two = got[:, 16 * c : 16 * c + 8], got[:, 16 * c + 8 : 16 * c + 16]
            rest = jnp.where(at_lane < 3 * PIECE, turn(tail, (2 - c) * PIECE), 0.0)
            rest = jnp.where(at_lane < 2 * PIECE, turn(two, -2 * PIECE), rest)
            rest = jnp.where(at_lane < PIECE, turn(one, -3 * PIECE), rest)
            one = jnp.where(at_lane < 3 * PIECE, one, 0.0)
            two = jnp.where(at_lane < 3 * PIECE, two, 0.0)
            result.append(jnp.concatenate([one, two, rest], axis=1).reshape(total, lanes))
        return result

    for side, ref in enumerate((own_ref, other_ref)):
        for t in range(n_tile):
            at = slice(t * lanes, (t + 1) * lanes)
            even, odd = unpacked(ref, 2 * t), unpacked(ref, 2 * t + 1)
            left_buf[0, side, :, at] = jnp.where(low, even[0], odd[0]).astype(BF16)
            right_buf[0, side, :, at] = jnp.where(low, odd[0], even[0]).astype(BF16)
            left_buf[1, side, :, at] = jnp.where(low, odd[1], even[1]).astype(BF16)
            right_buf[1, side, :, at] = jnp.where(low, even[1], odd[1]).astype(BF16)
    copies = [start(left_buf, left_ref, sems.at[0]), start(right_buf, right_ref, sems.at[1])]
    low = low_lanes((n_y, 2, rows, lanes))
    for side in range(2):
        for c in range(2):
            tri_scr[side, c] = dot(left_buf[c, side], right_buf[c, 0], FIRST)
    for side in range(2):
        place = core if side == 0 else 1 - core
        for t in range(n_tile):
            a, b = (
                tri_scr[side, c, :, t * lanes : (t + 1) * lanes]
                .reshape(n_y, SLOT, lanes)[:, : 2 * rows]
                .reshape(n_y, 2, rows, lanes)
                for c in range(2)
            )
            b = swap_pairs(b)
            msg_ref[:, place, :, 2 * t] = jnp.where(low, b, a).astype(BF16)
            msg_ref[:, place, :, 2 * t + 1] = jnp.where(low, a, b).astype(BF16)
    for copy in copies:
        copy.wait()


def norm_kernel(got_ref, scaled_ref, msg_ref, scr, scaled_buf, sems):
    half, rows, lanes = got_ref.shape
    copy = start(scaled_ref, scaled_buf, sems.at[0])
    scr[...] = got_ref[...].astype(F32)

    def mean(x):
        part = jnp.sum(x, axis=0)
        return (part + half_turn(part)) * (1.0 / (2 * half))

    copy.wait()
    for first in range(0, rows, 8):
        at = slice(first, first + 8)
        x = scr[:, at]
        x = x - mean(x)[None]
        inverse = lax.rsqrt(mean(x * x) + EPS)
        s = scaled_buf[:, at]
        along = inverse * inverse * mean(s * x)
        scr[:, at] = inverse[None] * (s - x * along[None])
    msg_ref[...] = scr[...].astype(BF16)


def update_kernel(
    ids_ref, got_ref, gate_ref, cot_ref, par_ref, w_out_ref, w_gate_ref, update_ref, gn_ref, scr
):
    rows, cols, width = cot_ref.shape
    half, _, lanes = got_ref.shape
    w_out, w_gate = w_out_ref[...], w_gate_ref[...]
    gain, shift = par_ref[2:3, :], par_ref[3:4, :]
    row = lax.broadcasted_iota(jnp.int32, (cols, 2 * lanes), 0)
    col = lax.broadcasted_iota(jnp.int32, (cols, 2 * lanes), 1)
    odd = ids_ref[3] * SLOT
    pick = (col == row + (SLOT - odd)) | (col == row + (lanes + odd))
    pick = jnp.where(pick, 1.0, 0.0).astype(BF16)
    nothing = jnp.zeros((half, lanes), BF16)
    scr[...] = got_ref[...].astype(F32).reshape(half * rows, lanes)
    for first in range(0, rows, GROUP):
        size = GROUP * cols
        at = slice(first * cols, first * cols + size)
        tri = []
        for k in range(first, first + GROUP):
            x = scr[pl.ds(k, half, stride=rows), :].astype(BF16)
            both = jnp.concatenate(
                [jnp.concatenate([x, nothing], axis=1), jnp.concatenate([nothing, x], axis=1)],
                axis=0,
            )
            tri.append(dot(pick, both, LAST))
        unit, _ = unit_of(jnp.concatenate(tri, axis=0))
        lin = dot((unit * gain + shift).astype(BF16), w_out)
        gate = gate_ref[at, :]
        update_ref[first : first + GROUP] = (gate * lin).astype(BF16).reshape(GROUP, cols, width)
        cot = cot_ref[first : first + GROUP].astype(F32).reshape(size, width)
        grad_gate = (cot * lin * gate * (1.0 - gate)).astype(BF16)
        gn_ref[at, :] = dot(grad_gate, w_gate, LAST)


def factor_grads_kernel(
    ids_ref, own_ref, other_ref, left_ref, right_ref, msg_ref,
    tri_scr, gl_scr, gr_scr, left_buf, right_buf, sems,
):
    n_y, _, _, _, rows, lanes = own_ref.shape
    n_row = msg_ref.shape[0]
    total = n_row * rows
    core = ids_ref[2]
    copies = [start(right_ref, right_buf, sems.at[0]), start(left_ref, left_buf, sems.at[1])]
    low = low_lanes((n_y, 2, rows, lanes))
    gap = jnp.zeros((n_y, SLOT - 2 * rows, lanes), F32)
    for n, (ref, place) in enumerate(((own_ref, core), (own_ref, 1 - core), (other_ref, core))):
        for t in range(n_y // 2):
            even = ref[:, place, :, 2 * t].astype(F32)
            odd = ref[:, place, :, 2 * t + 1].astype(F32)
            first = jnp.where(low, odd, even)
            second = swap_pairs(jnp.where(low, even, odd))
            for c, tile in enumerate((first, second)):
                tile = jnp.concatenate([tile.reshape(n_y, 2 * rows, lanes), gap], axis=1)
                tile = tile.reshape(n_y * SLOT, lanes).astype(BF16)
                tri_scr[c, n, :, t * lanes : (t + 1) * lanes] = tile
    for copy in copies:
        copy.wait()
    for c in range(2):
        gl_scr[c] = dot(right_buf[c, 0], tri_scr[c, 0], LAST) + dot(
            right_buf[c, 1], tri_scr[c, 2], LAST
        )
        gr_scr[c] = dot(left_buf[c, 0], tri_scr[c, 0]) + dot(left_buf[c, 1], tri_scr[c, 1])
    low = low_lanes((total, lanes))
    at_lane = place_in_slot((n_row, 8, lanes))
    for y in range(n_y):
        tails = []
        for c in range(2):
            at = slice(y // 2 * lanes, y // 2 * lanes + lanes)
            a, b = gl_scr[c, :, at], gr_scr[c, :, at]
            if (y + c) % 2:
                a, b = b, a
            both = jnp.where(low, a, b).reshape(n_row, rows, lanes)
            one, two, rest = both[:, :8], both[:, 8:16], both[:, 16:24]
            one = jnp.where(at_lane < 3 * PIECE, one, turn(rest, 3 * PIECE))
            two = jnp.where(at_lane < 3 * PIECE, two, turn(rest, 2 * PIECE))
            msg_ref[:, y, 16 * c : 16 * c + 16] = jnp.concatenate([one, two], axis=1).astype(BF16)
            tails.append(turn(rest, (c - 2) * PIECE))
        tail = jnp.where(at_lane < PIECE, tails[0], tails[1])
        msg_ref[:, y, 32:40] = tail.astype(BF16)


def pair_grad_kernel(
    ids_ref, got_ref, coef_ref, unit_ref, inv_ref, gn_ref, par_ref, w_in_ref, out_ref,
    scr, left_buf, right_buf, coef_buf, unit_buf, inv_buf, gn_buf, par_buf, w_buf, sems,
):
    half, _, lanes = got_ref.shape
    rows, cols, width = out_ref.shape
    sources = (coef_ref, gn_ref, unit_ref, inv_ref, w_in_ref, par_ref)
    targets = (coef_buf, gn_buf, unit_buf, inv_buf, w_buf, par_buf)
    copies = [start(x, y, sems.at[n]) for n, (x, y) in enumerate(zip(sources, targets))]
    eye = identity(2 * half)
    scr[...] = got_ref[...].astype(F32).reshape(half * MSG_ROWS, lanes)
    main, tail = 16, 8
    low = low_lanes((PIECE, 2 * half))
    for first in range(0, main + tail, GROUP):
        parts = []
        for s in range(first, first + GROUP):
            if s < main:
                parts += [scr[pl.ds(c * main + s, half, stride=MSG_ROWS), :] for c in range(2)]
            else:
                parts += [scr[pl.ds(main + s, half, stride=MSG_ROWS), :]] * 2
        turned = dot(eye, jnp.concatenate(parts, axis=0).astype(BF16), LAST)
        for n, s in enumerate(range(first, first + GROUP)):
            both = turned[:, n * 2 * half : (n + 1) * 2 * half]
            for buf, x in ((left_buf, both[:SLOT]), (right_buf, both[SLOT:])):
                if s < main:
                    at = (main + s % tail) * cols + s // tail * PIECE
                    buf[s * cols : (s + 1) * cols, :] = x[:cols]
                    buf[at : at + PIECE, :] = x[cols:]
                else:
                    at = s * cols + 2 * PIECE
                    buf[at : at + PIECE, :] = jnp.where(low, x[:PIECE], x[PIECE : 2 * PIECE])
    for copy in copies:
        copy.wait()
    gain = par_buf[0:1, :]
    w_in = w_buf[...]
    size = GROUP * cols
    straight = straight_lanes(ids_ref, (size, 2 * half))
    for first in range(0, rows, GROUP):
        at = slice(first * cols, first * cols + size)
        left = jnp.where(straight, left_buf[at, :], right_buf[at, :])
        right = jnp.where(straight, right_buf[at, :], left_buf[at, :])
        grad_proj = jnp.concatenate(
            [
                (side * coef_buf[m, at, :]).astype(BF16)
                for m, side in enumerate((left, left, right, right))
            ],
            axis=1,
        )
        s = (dot(grad_proj, w_in, LAST) + gn_buf[at, :]) * gain
        unit = unit_buf[at, :]
        grad = inv_buf[at, :] * (
            s
            - jnp.mean(s, axis=-1, keepdims=True)
            - unit * jnp.mean(s * unit, axis=-1, keepdims=True)
        )
        out_ref[first : first + GROUP] = grad.astype(BF16).reshape(GROUP, cols, width)


def call(kernel, ins, outs, scratch=(), smem=(), sems=(), limit=24, flops=0, moved=0):
    spaces = {"s": pltpu.SMEM, "v": pltpu.VMEM, "b": pltpu.VMEM, "h": pltpu.HBM}
    extra = [pltpu.SMEM(s, d) for s, d in smem]
    if sems:
        extra.append(pltpu.SemaphoreType.DMA(sems))
    return pl.pallas_call(
        kernel,
        out_shape=[
            jax.ShapeDtypeStruct(s, d) if place == "v" else pltpu.HBM(s, d)
            for s, d, place in outs
        ],
        in_specs=[pl.BlockSpec(memory_space=spaces[place]) for _, place in ins],
        out_specs=[pl.BlockSpec(memory_space=spaces[place]) for _, _, place in outs],
        scratch_shapes=[pltpu.VMEM(s, d) for s, d in scratch] + extra,
        compiler_params=pltpu.CompilerParams(vmem_limit_bytes=limit * MIB),
        cost_estimate=pl.CostEstimate(flops=flops, bytes_accessed=moved, transcendentals=0),
    )(
        *(
            pltpu.with_memory_space_constraint(x, pltpu.HBM) if place == "h" else x
            for x, place in ins
        )
    )


def exchange(x):
    return lax.all_to_all(x, ("row", "y"), 0, 0, tiled=True)


def swap(x):
    return lax.ppermute(x, "core", [(0, 1), (1, 0)])


def local(pair, chain_lengths, cotangent, norm_params, w_in, w_gate, w_out):
    rows, cols, width = pair.shape
    hidden = w_out.shape[0]
    n_row, n_y = lax.axis_size("row"), lax.axis_size("y")
    assert hidden == 2 * n_row * n_y == 2 * SLOT and width == hidden
    assert rows == 24 and cols == 2 * rows and n_row == 4 * n_y and lax.axis_size("core") == 2
    half = hidden // 2
    size, lanes = rows * cols, 2 * SLOT
    total, wide = n_row * rows, n_y * SLOT
    row, core = lax.axis_index("row"), lax.axis_index("core")
    col = 2 * lax.axis_index("y") + core
    ids = jnp.stack([row * rows, col * cols, core, lax.axis_index("y") % 2]).astype(jnp.int32)

    flat = (size, width)
    block = (rows, cols, width)
    par = (norm_params.shape, F32)
    factor = (2, 2, total, wide)
    two = (half, MSG_ROWS, lanes)
    one = (half, rows, lanes)
    by_home = (n_row, n_y, MSG_ROWS, lanes)
    by_block = (n_y, 2, 2, n_y, rows, lanes)
    (msg,) = call(
        factors_kernel,
        [(ids, "s"), (chain_lengths, "h"), (pair, "h"), (norm_params, "h"), (w_in, "h")],
        [(two, BF16, "v")],
        [((half * MSG_ROWS, lanes), F32), (block, BF16), (block, BF16), (block, BF16), par]
        + [(w_in.shape, BF16)],
        smem=[(chain_lengths.shape, jnp.int32)],
        sems=(4,),
        flops=2 * size * width * 4 * hidden,
        moved=8 * MIB,
    )
    got = exchange(msg)
    msg, left, right = call(
        triangle_kernel,
        [(ids, "s"), (got.reshape(by_home), "v"), (swap(got).reshape(by_home), "v")],
        [(by_block, BF16, "v"), (factor, BF16, "h"), (factor, BF16, "h")],
        [((2, 2, wide, wide), F32), (factor, BF16), (factor, BF16)],
        sems=(2,),
        flops=8 * total * wide * wide,
        moved=4 * MIB,
    )
    got = exchange(msg.reshape(one))
    gate, scaled, coef, unit, inverse = call(
        saved_kernel,
        [(ids, "s"), (chain_lengths, "s"), (pair, "v"), (left, "h"), (cotangent, "v")]
        + [(norm_params, "v"), (w_in, "v"), (w_gate, "v"), (w_out, "v")],
        [(flat, F32, "b"), (one, F32, "b"), ((4,) + flat, F32, "b")] + [(flat, F32, "b")] * 2,
        [((half * rows, lanes), F32)],
        flops=2 * size * width * 6 * hidden,
        moved=24 * MIB,
    )
    (msg,) = call(
        norm_kernel,
        [(got, "v"), (scaled, "h")],
        [(one, BF16, "v")],
        [(one, F32), (one, F32)],
        sems=(1,),
        flops=2 * size * width * hidden,
        moved=4 * MIB,
    )
    update, grad_normed = call(
        update_kernel,
        [(ids, "s"), (got, "v"), (gate, "v"), (cotangent, "v"), (norm_params, "v"), (w_out, "v")]
        + [(w_gate, "v")],
        [(block, BF16, "b"), (flat, F32, "b")],
        [((half * rows, lanes), F32)],
        flops=4 * size * width * hidden,
        moved=12 * MIB,
    )
    got = exchange(msg)
    (msg,) = call(
        factor_grads_kernel,
        [(ids, "s"), (got.reshape(by_block), "v"), (swap(got).reshape(by_block), "v")]
        + [(left, "h"), (right, "h")],
        [(by_home, BF16, "v")],
        [((2, 3, wide, wide), BF16), ((2, total, wide), F32), ((2, total, wide), F32)]
        + [(factor, BF16), (factor, BF16)],
        sems=(2,),
        flops=16 * total * wide * wide,
        moved=4 * MIB,
    )
    got = exchange(msg.reshape(two))
    (grad_pair,) = call(
        pair_grad_kernel,
        [(ids, "s"), (got, "v"), (coef, "h"), (unit, "h"), (inverse, "h"), (grad_normed, "h")]
        + [(norm_params, "h"), (w_in, "h")],
        [(block, BF16, "v")],
        [((half * MSG_ROWS, lanes), F32), (flat, F32), (flat, F32), ((4,) + flat, F32)]
        + [(flat, F32)] * 3
        + [par, (w_in.shape, BF16)],
        sems=(6,),
        flops=2 * size * width * 4 * hidden,
        moved=8 * MIB,
    )
    return (update, grad_pair)


def solution(mesh):
    n_row, n_col, n_rep = mesh.devices.shape
    mesh = Mesh(mesh.devices.reshape(n_row, n_col // 2, 2, n_rep), ("row", "y", "core", "rep"))
    block = P(("rep", "row"), ("y", "core"), None)
    return jax.shard_map(
        local,
        mesh=mesh,
        in_specs=(block, P("rep"), block, P(), P(), P(), P()),
        out_specs=(block, block),
        check_vma=False,
    )
```

```python
import jax
import jax.numpy as jnp
from jax import lax
from jax.experimental import pallas as pl
from jax.experimental.pallas import tpu as pltpu
from jax.sharding import Mesh
from jax.sharding import PartitionSpec as P

EPS = 1e-05
F32 = jnp.float32
BF16 = jnp.bfloat16
MIB = 1 << 20
LAST = (((1,), (1,)), ((), ()))
FIRST = (((0,), (0,)), ((), ()))
SLOT = 64
PIECE = 16
MSG_ROWS = 40
GROUP = 4


def dot(a, b, dims=(((1,), (0,)), ((), ()))):
    return lax.dot_general(a, b, dims, preferred_element_type=F32)


def identity(n):
    row = lax.broadcasted_iota(jnp.int32, (n, n), 0)
    col = lax.broadcasted_iota(jnp.int32, (n, n), 1)
    return jnp.where(row == col, 1.0, 0.0).astype(BF16)


def low_lanes(shape):
    return lax.broadcasted_iota(jnp.int32, shape, len(shape) - 1) < SLOT


def half_turn(x):
    return turn(x, SLOT)


def turn(x, by):
    return pltpu.roll(x, by % x.shape[-1], x.ndim - 1)


def place_in_slot(shape):
    return lax.rem(lax.broadcasted_iota(jnp.int32, shape, len(shape) - 1), SLOT)


def straight_lanes(ids_ref, shape):
    lane = lax.broadcasted_iota(jnp.int32, shape, len(shape) - 1)
    return jnp.where(lane < SLOT, 0, 1) == ids_ref[3]


def swap_pairs(x):
    return jnp.concatenate([x[n ^ 1][None] for n in range(x.shape[0])], axis=0)


def unit_of(x):
    mean = jnp.mean(x, axis=-1, keepdims=True)
    centered = x - mean
    variance = jnp.mean(centered * centered, axis=-1, keepdims=True)
    inverse = lax.rsqrt(variance + EPS)
    return centered * inverse, inverse


def mask_of(ids_ref, len_ref, row, shape):
    limit = len_ref[0]
    for i in range(1, len_ref.shape[0]):
        limit = limit + len_ref[i]
    bound = jnp.where(ids_ref[0] + row < limit, limit - ids_ref[1], 0)
    return lax.broadcasted_iota(jnp.int32, shape, 0) < bound


def start(source, target, sem):
    copy = pltpu.make_async_copy(source, target, sem)
    copy.start()
    return copy


def paired(first, second):
    gap = jnp.zeros((SLOT - first.shape[0], first.shape[1]), first.dtype)
    return jnp.concatenate([first, gap, second, gap], axis=0)


def factors_kernel(
    ids_ref, len_ref, pair_ref, par_ref, w_ref, msg_ref,
    scr, a_buf, b_buf, pair_buf, par_buf, w_buf, len_buf, sems,
):
    rows, cols, width = pair_ref.shape
    hidden = w_ref.shape[1] // 4
    half = hidden // 2
    sources = (pair_ref, w_ref, par_ref, len_ref)
    targets = (pair_buf, w_buf, par_buf, len_buf)
    copies = [start(x, y, sems.at[n]) for n, (x, y) in enumerate(zip(sources, targets))]
    eye = identity(hidden)
    for copy in copies:
        copy.wait()
    gain, shift = par_buf[0:1, :], par_buf[1:2, :]
    w = w_buf[...]
    straight = straight_lanes(ids_ref, (cols, hidden))
    for first in range(0, rows, GROUP):
        x = pair_buf[first : first + GROUP].astype(F32).reshape(GROUP * cols, width)
        unit, _ = unit_of(x)
        normed = (unit * gain + shift).astype(BF16)
        proj = dot(normed, w)
        left = jax.nn.sigmoid(proj[:, :hidden]) * proj[:, hidden : 2 * hidden]
        right = jax.nn.sigmoid(proj[:, 2 * hidden : 3 * hidden]) * proj[:, 3 * hidden :]
        for k in range(GROUP):
            mask = mask_of(ids_ref, len_buf, first + k, (cols, hidden))
            at = slice(k * cols, (k + 1) * cols)
            one, two = jnp.where(mask, left[at], 0.0), jnp.where(mask, right[at], 0.0)
            a_buf[first + k] = jnp.where(straight, one, two).astype(BF16)
            b_buf[first + k] = jnp.where(straight, two, one).astype(BF16)
    main, tail = 16, 8
    gap = jnp.zeros((2 * PIECE, hidden), BF16)
    low = place_in_slot((half, 2 * SLOT)) < PIECE
    for first in range(0, main + tail, GROUP):
        parts = []
        for s in range(first, first + GROUP):
            if s < main:
                e, at = main + s % tail, pl.ds(s // tail * PIECE, PIECE)
                parts += [a_buf[s], a_buf[e, at], b_buf[s], b_buf[e, at]]
            else:
                at = pl.ds(2 * PIECE, PIECE)
                parts += [a_buf[s, at], a_buf[s, at], gap, b_buf[s, at], b_buf[s, at], gap]
        turned = dot(eye, jnp.concatenate(parts, axis=0), LAST)
        for n, s in enumerate(range(first, first + GROUP)):
            one = turned[:half, n * hidden : (n + 1) * hidden]
            two = turned[half:, n * hidden : (n + 1) * hidden]
            if s < main:
                scr[pl.ds(s, half, stride=MSG_ROWS), :] = one
                scr[pl.ds(main + s, half, stride=MSG_ROWS), :] = two
            else:
                scr[pl.ds(main + s, half, stride=MSG_ROWS), :] = jnp.where(low, one, two)
    msg_ref[...] = scr[...].reshape(msg_ref.shape).astype(BF16)


def saved_kernel(
    ids_ref, len_ref, pair_ref, after_ref, cot_ref, par_ref, w_in_ref, w_gate_ref, w_out_ref,
    gate_ref, scaled_ref, coef_ref, scr,
):
    rows, cols, width = pair_ref.shape
    hidden = w_in_ref.shape[1] // 4
    half = hidden // 2
    first_half = ~straight_lanes(ids_ref, (half, 2 * SLOT))
    w_in, w_gate, w_out = w_in_ref[...], w_gate_ref[...], w_out_ref[...]
    for first in range(0, rows, GROUP):
        size = GROUP * cols
        at = slice(first * cols, first * cols + size)
        x = pair_ref[first : first + GROUP].astype(F32).reshape(size, width)
        unit, _ = unit_of(x)
        normed = (unit * par_ref[0:1, :] + par_ref[1:2, :]).astype(BF16)
        gate = jax.nn.sigmoid(dot(normed, w_gate))
        gate_ref[at, :] = gate
        cot = cot_ref[first : first + GROUP].astype(F32).reshape(size, width)
        grad_lin = (cot * gate).astype(BF16)
        scaled = dot(grad_lin, w_out, LAST) * par_ref[2:3, :]
        scaled = scaled - jnp.mean(scaled, axis=-1, keepdims=True)
        proj = dot(normed, w_in)
        masks = []
        for k in range(GROUP):
            one = scaled[k * cols : (k + 1) * cols]
            turned = jnp.transpose(paired(one, one))
            turned = jnp.where(first_half, turned[:half], turned[half:])
            scr[pl.ds(first + k, half, stride=rows), :] = turned
            mask = mask_of(ids_ref, len_ref, first + k, (cols, hidden))
            masks.append(jnp.where(mask, 1.0, 0.0))
        mask = jnp.concatenate(masks, axis=0)
        for side in range(2):
            sig = jax.nn.sigmoid(proj[:, 2 * side * hidden : (2 * side + 1) * hidden])
            val = proj[:, (2 * side + 1) * hidden : (2 * side + 2) * hidden]
            kept = mask * sig
            for n, x in enumerate((kept * val * (1.0 - sig), kept)):
                place = (2 * side + n) * rows * cols + first * cols
                coef_ref[place : place + size, :] = x.astype(BF16)
    scaled_ref[...] = scr[...].reshape(scaled_ref.shape)


def unpacked(ref, y, total):
    n_row, _, _, lanes = ref.shape
    at_lane = place_in_slot((n_row, 8, lanes))
    got = ref[:, y].astype(F32)
    tail = got[:, 32:40]
    result = []
    for c in range(2):
        one, two = got[:, 16 * c : 16 * c + 8], got[:, 16 * c + 8 : 16 * c + 16]
        rest = jnp.where(at_lane < 3 * PIECE, turn(tail, (2 - c) * PIECE), 0.0)
        rest = jnp.where(at_lane < 2 * PIECE, turn(two, -2 * PIECE), rest)
        rest = jnp.where(at_lane < PIECE, turn(one, -3 * PIECE), rest)
        one = jnp.where(at_lane < 3 * PIECE, one, 0.0)
        two = jnp.where(at_lane < 3 * PIECE, two, 0.0)
        result.append(jnp.concatenate([one, two, rest], axis=1).reshape(total, lanes))
    return result


def unpack_factors(ref, left, right):
    n_y, lanes = ref.shape[1], ref.shape[-1]
    total = left.shape[-2]
    low = low_lanes((total, lanes))
    for t in range(n_y // 2):
        at = slice(t * lanes, (t + 1) * lanes)
        even, odd = unpacked(ref, 2 * t, total), unpacked(ref, 2 * t + 1, total)
        left[0, :, at] = jnp.where(low, even[0], odd[0]).astype(BF16)
        left[1, :, at] = jnp.where(low, odd[1], even[1]).astype(BF16)
        if right is not None:
            right[0, :, at] = jnp.where(low, odd[0], even[0]).astype(BF16)
            right[1, :, at] = jnp.where(low, even[1], odd[1]).astype(BF16)


def triangle_kernel(
    ids_ref, own_ref, other_ref, msg_ref, tri_scr, left_buf, right_buf, msg_buf, sems
):
    n_y, lanes = own_ref.shape[1], own_ref.shape[-1]
    rows = msg_ref.shape[-2]
    core = ids_ref[2]
    unpack_factors(own_ref, left_buf.at[0], right_buf)
    unpack_factors(other_ref, left_buf.at[1], None)
    copies = []
    low = low_lanes((n_y, 2, rows, lanes))
    for side in range(2):
        for c in range(2):
            tri_scr[side, c] = dot(left_buf[side, c], right_buf[c], FIRST)
        for t in range(n_y // 2):
            a, b = (
                tri_scr[side, c, :, t * lanes : (t + 1) * lanes]
                .reshape(n_y, SLOT, lanes)[:, : 2 * rows]
                .reshape(n_y, 2, rows, lanes)
                for c in range(2)
            )
            b = swap_pairs(b)
            msg_buf[side, :, :, 2 * t] = jnp.where(low, b, a).astype(BF16)
            msg_buf[side, :, :, 2 * t + 1] = jnp.where(low, a, b).astype(BF16)
        place = core if side == 0 else 1 - core
        copies.append(start(msg_buf.at[side], msg_ref.at[:, place], sems.at[side]))
    for copy in copies:
        copy.wait()


def keep_factors_kernel(own_ref, other_ref, after_ref, factors_ref):
    for side, ref in enumerate((own_ref, other_ref)):
        unpack_factors(ref, factors_ref.at[0, side], factors_ref.at[1, side])


def norm_kernel(got_ref, scaled_ref, msg_ref, scr):
    half, rows, lanes = got_ref.shape
    scr[...] = got_ref[...].astype(F32)

    def mean(x):
        part = jnp.sum(x, axis=0)
        return (part + half_turn(part)) * (1.0 / (2 * half))

    for first in range(0, rows, 8):
        at = slice(first, first + 8)
        x = scr[:, at]
        x = x - mean(x)[None]
        inverse = lax.rsqrt(mean(x * x) + EPS)
        s = scaled_ref[:, at]
        along = inverse * inverse * mean(s * x)
        scr[:, at] = inverse[None] * (s - x * along[None])
    msg_ref[...] = scr[...].astype(BF16)


def update_kernel(
    ids_ref, got_ref, gate_ref, cot_ref, par_ref, w_out_ref, w_gate_ref, w_in_ref, coef_ref,
    pair_ref, update_ref, kept_ref, kept_par_ref, scr, sems,
):
    n_coef, n_pair = coef_ref.shape[0], pair_ref.shape[0]
    copies = [
        start(coef_ref, kept_ref.at[pl.ds(0, n_coef)], sems.at[0]),
        start(pair_ref, kept_ref.at[pl.ds(n_coef, n_pair)], sems.at[1]),
    ]
    kept_par_ref[...] = par_ref[...]
    for n in range(4):
        place = n_coef + 3 * n_pair + n * w_in_ref.shape[0]
        part = w_in_ref[:, n * w_out_ref.shape[0] : (n + 1) * w_out_ref.shape[0]]
        kept_ref[place : place + w_in_ref.shape[0], :] = part
    rows, cols, width = cot_ref.shape
    half, _, lanes = got_ref.shape
    w_out, w_gate = w_out_ref[...], w_gate_ref[...]
    gain, shift = par_ref[2:3, :], par_ref[3:4, :]
    row = lax.broadcasted_iota(jnp.int32, (cols, 2 * lanes), 0)
    col = lax.broadcasted_iota(jnp.int32, (cols, 2 * lanes), 1)
    odd = ids_ref[3] * SLOT
    pick = (col == row + (SLOT - odd)) | (col == row + (lanes + odd))
    pick = jnp.where(pick, 1.0, 0.0).astype(BF16)
    nothing = jnp.zeros((half, lanes), BF16)
    scr[...] = got_ref[...].astype(F32).reshape(half * rows, lanes)
    for first in range(0, rows, GROUP):
        size = GROUP * cols
        at = slice(first * cols, first * cols + size)
        tri = []
        for k in range(first, first + GROUP):
            x = scr[pl.ds(k, half, stride=rows), :].astype(BF16)
            both = jnp.concatenate(
                [jnp.concatenate([x, nothing], axis=1), jnp.concatenate([nothing, x], axis=1)],
                axis=0,
            )
            tri.append(dot(pick, both, LAST))
        unit, _ = unit_of(jnp.concatenate(tri, axis=0))
        lin = dot((unit * gain + shift).astype(BF16), w_out)
        gate = gate_ref[at, :]
        update_ref[first : first + GROUP] = (gate * lin).astype(BF16).reshape(GROUP, cols, width)
        cot = cot_ref[first : first + GROUP].astype(F32).reshape(size, width)
        grad_gate = (cot * lin * gate * (1.0 - gate)).astype(BF16)
        gn = dot(grad_gate, w_gate, LAST)
        high = gn.astype(BF16)
        for n, x in enumerate((high, gn - high.astype(F32))):
            place = n_coef + (1 + n) * n_pair + first * cols
            kept_ref[place : place + size, :] = x.astype(BF16)
    for copy in copies:
        copy.wait()


def factor_grads_kernel(
    ids_ref, own_ref, other_ref, factors_ref, msg_ref,
    tri_scr, gl_scr, gr_scr, msg_buf, sems,
):
    n_y, _, _, _, rows, lanes = own_ref.shape
    n_row = msg_ref.shape[0]
    total = n_row * rows
    core = ids_ref[2]
    results = []
    low = low_lanes((n_y, 2, rows, lanes))
    gap = jnp.zeros((n_y, SLOT - 2 * rows, lanes), F32)
    for n, (ref, place) in enumerate(((own_ref, core), (own_ref, 1 - core), (other_ref, core))):
        for t in range(n_y // 2):
            even = ref[:, place, :, 2 * t].astype(F32)
            odd = ref[:, place, :, 2 * t + 1].astype(F32)
            first = jnp.where(low, odd, even)
            second = swap_pairs(jnp.where(low, even, odd))
            for c, tile in enumerate((first, second)):
                tile = jnp.concatenate([tile.reshape(n_y, 2 * rows, lanes), gap], axis=1)
                tile = tile.reshape(n_y * SLOT, lanes).astype(BF16)
                tri_scr[c, n, :, t * lanes : (t + 1) * lanes] = tile
    for c in range(2):
        (left, far_left), (right, far_right) = (
            (factors_ref[n, 0, c], factors_ref[n, 1, c]) for n in range(2)
        )
        gl_scr[c] = dot(right, tri_scr[c, 0], LAST) + dot(far_right, tri_scr[c, 2], LAST)
        gr_scr[c] = dot(left, tri_scr[c, 0]) + dot(far_left, tri_scr[c, 1])
    low = low_lanes((total, lanes))
    at_lane = place_in_slot((n_row, 8, lanes))
    for y in range(n_y):
        tails = []
        for c in range(2):
            at = slice(y // 2 * lanes, y // 2 * lanes + lanes)
            a, b = gl_scr[c, :, at], gr_scr[c, :, at]
            if (y + c) % 2:
                a, b = b, a
            both = jnp.where(low, a, b).reshape(n_row, rows, lanes)
            one, two, rest = both[:, :8], both[:, 8:16], both[:, 16:24]
            one = jnp.where(at_lane < 3 * PIECE, one, turn(rest, 3 * PIECE))
            two = jnp.where(at_lane < 3 * PIECE, two, turn(rest, 2 * PIECE))
            msg_buf[y, :, 16 * c : 16 * c + 16] = jnp.concatenate([one, two], axis=1).astype(BF16)
            tails.append(turn(rest, (c - 2) * PIECE))
        tail = jnp.where(at_lane < PIECE, tails[0], tails[1])
        msg_buf[y, :, 32:40] = tail.astype(BF16)
        results.append(start(msg_buf.at[y], msg_ref.at[:, y], sems.at[y]))
    for copy in results:
        copy.wait()


def pair_grad_kernel(
    ids_ref, got_ref, kept_ref, par_ref, out_ref,
    scr, left_buf, right_buf, out_buf, sems,
):
    half, _, lanes = got_ref.shape
    rows, cols, width = out_ref.shape
    eye = identity(2 * half)
    scr[...] = got_ref[...].astype(F32).reshape(half * MSG_ROWS, lanes)
    main, tail = 16, 8
    low = low_lanes((PIECE, 2 * half))
    for first in range(0, main + tail, GROUP):
        parts = []
        for s in range(first, first + GROUP):
            if s < main:
                parts += [scr[pl.ds(c * main + s, half, stride=MSG_ROWS), :] for c in range(2)]
            else:
                parts += [scr[pl.ds(main + s, half, stride=MSG_ROWS), :]] * 2
        turned = dot(eye, jnp.concatenate(parts, axis=0).astype(BF16), LAST)
        for n, s in enumerate(range(first, first + GROUP)):
            both = turned[:, n * 2 * half : (n + 1) * 2 * half]
            for buf, x in ((left_buf, both[:SLOT]), (right_buf, both[SLOT:])):
                if s < main:
                    at = (main + s % tail) * cols + s // tail * PIECE
                    buf[s * cols : (s + 1) * cols, :] = x[:cols]
                    buf[at : at + PIECE, :] = x[cols:]
                else:
                    at = s * cols + 2 * PIECE
                    buf[at : at + PIECE, :] = jnp.where(low, x[:PIECE], x[PIECE : 2 * PIECE])
    gain = par_ref[0:1, :]
    flat = rows * cols
    w_in = jnp.concatenate(
        [kept_ref[7 * flat + n * width : 7 * flat + (n + 1) * width, :] for n in range(4)], axis=1
    )
    size = GROUP * cols
    straight = straight_lanes(ids_ref, (size, 2 * half))
    results = []
    for first in range(0, rows, GROUP):
        at = slice(first * cols, first * cols + size)
        left = jnp.where(straight, left_buf[at, :], right_buf[at, :])
        right = jnp.where(straight, right_buf[at, :], left_buf[at, :])
        coef_a, val_a, coef_b, val_b, x, gn, gn_rest = (
            kept_ref[n * flat + first * cols : n * flat + first * cols + size, :].astype(F32)
            for n in range(7)
        )
        grad_proj = jnp.concatenate(
            [
                (side * factor).astype(BF16)
                for side, factor in ((left, coef_a), (left, val_a), (right, coef_b), (right, val_b))
            ],
            axis=1,
        )
        s = (dot(grad_proj, w_in, LAST) + (gn + gn_rest)) * gain
        unit, inverse = unit_of(x)
        grad = inverse * (
            s
            - jnp.mean(s, axis=-1, keepdims=True)
            - unit * jnp.mean(s * unit, axis=-1, keepdims=True)
        )
        out_buf[first : first + GROUP] = grad.astype(BF16).reshape(GROUP, cols, width)
        if (first + GROUP) % (rows // 2) == 0:
            part = pl.ds(first + GROUP - rows // 2, rows // 2)
            n = first // (rows // 2)
            results.append(start(out_buf.at[part], out_ref.at[part], sems.at[n]))
    for copy in results:
        copy.wait()


def call(kernel, ins, outs, scratch=(), smem=(), sems=(), limit=12, flops=0, moved=0):
    spaces = {"s": pltpu.SMEM, "v": pltpu.VMEM, "b": pltpu.VMEM, "h": pltpu.HBM}
    extra = [pltpu.SMEM(s, d) for s, d in smem]
    if sems:
        extra.append(pltpu.SemaphoreType.DMA(sems))
    return pl.pallas_call(
        kernel,
        out_shape=[
            jax.ShapeDtypeStruct(s, d) if place == "v" else pltpu.HBM(s, d)
            for s, d, place in outs
        ],
        in_specs=[pl.BlockSpec(memory_space=spaces[place]) for _, place in ins],
        out_specs=[pl.BlockSpec(memory_space=spaces[place]) for _, _, place in outs],
        scratch_shapes=[pltpu.VMEM(s, d) for s, d in scratch] + extra,
        compiler_params=pltpu.CompilerParams(vmem_limit_bytes=limit * MIB),
        cost_estimate=pl.CostEstimate(flops=flops, bytes_accessed=moved, transcendentals=0),
    )(
        *(
            pltpu.with_memory_space_constraint(x, pltpu.HBM) if place == "h" else x
            for x, place in ins
        )
    )


def exchange(x):
    return lax.all_to_all(x, ("row", "y"), 0, 0, tiled=True)


def swap(x):
    return lax.ppermute(x, "core", [(0, 1), (1, 0)])


def local(pair, chain_lengths, cotangent, norm_params, w_in, w_gate, w_out):
    rows, cols, width = pair.shape
    hidden = w_out.shape[0]
    n_row, n_y = lax.axis_size("row"), lax.axis_size("y")
    assert hidden == 2 * n_row * n_y == 2 * SLOT and width == hidden
    assert rows == 24 and cols == 2 * rows and n_row == 4 * n_y and lax.axis_size("core") == 2
    half = hidden // 2
    size, lanes = rows * cols, 2 * SLOT
    total, wide = n_row * rows, n_y * SLOT
    row, core = lax.axis_index("row"), lax.axis_index("core")
    col = 2 * lax.axis_index("y") + core
    ids = jnp.stack([row * rows, col * cols, core, lax.axis_index("y") % 2]).astype(jnp.int32)

    flat = (size, width)
    block = (rows, cols, width)
    par = (norm_params.shape, F32)
    factor = (2, 2, total, wide)
    two = (half, MSG_ROWS, lanes)
    one = (half, rows, lanes)
    by_home = (n_row, n_y, MSG_ROWS, lanes)
    by_block = (n_y, 2, 2, n_y, rows, lanes)
    (msg,) = call(
        factors_kernel,
        [(ids, "s"), (chain_lengths, "h"), (pair, "h"), (norm_params, "h"), (w_in, "h")],
        [(two, BF16, "v")],
        [((half * MSG_ROWS, lanes), F32), (block, BF16), (block, BF16), (block, BF16), par]
        + [(w_in.shape, BF16)],
        smem=[(chain_lengths.shape, jnp.int32)],
        sems=(4,),
        flops=2 * size * width * 4 * hidden,
        moved=8 * MIB,
    )
    got = exchange(msg)
    own, other = got.reshape(by_home), swap(got).reshape(by_home)
    (msg,) = call(
        triangle_kernel,
        [(ids, "s"), (own, "v"), (other, "v")],
        [(by_block, BF16, "h")],
        [((2, 2, wide, wide), F32), (factor, BF16), (factor[1:], BF16)]
        + [((2, n_y, 2, n_y, rows, lanes), BF16)],
        sems=(2,),
        flops=8 * total * wide * wide,
        moved=4 * MIB,
    )
    (factors,) = call(
        keep_factors_kernel,
        [(own, "v"), (other, "v"), (msg, "h")],
        [((2,) + factor, BF16, "b")],
        flops=8 * total * wide * wide,
        moved=4 * MIB,
    )
    got = exchange(msg.reshape(one))
    gate, scaled, coef = call(
        saved_kernel,
        [(ids, "s"), (chain_lengths, "s"), (pair, "v"), (factors, "h"), (cotangent, "v")]
        + [(norm_params, "v"), (w_in, "v"), (w_gate, "v"), (w_out, "v")],
        [(flat, F32, "b"), (one, F32, "v"), ((4 * size, width), BF16, "b")],
        [((half * rows, lanes), F32)],
        flops=2 * size * width * 6 * hidden,
        moved=24 * MIB,
    )
    (msg,) = call(
        norm_kernel,
        [(got, "v"), (scaled, "v")],
        [(one, BF16, "v")],
        [(one, F32)],
        flops=2 * size * width * hidden,
        moved=4 * MIB,
    )
    update, kept, kept_par = call(
        update_kernel,
        [(ids, "s"), (got, "v"), (gate, "v"), (cotangent, "v"), (norm_params, "v"), (w_out, "v")]
        + [(w_gate, "v"), (w_in, "v"), (coef, "h"), (pair.reshape(flat), "h")],
        [(block, BF16, "b"), ((7 * size + 4 * width, width), BF16, "v"), par + ("v",)],
        [((half * rows, lanes), F32)],
        sems=(2,),
        flops=4 * size * width * hidden,
        moved=12 * MIB,
    )
    got = exchange(msg)
    (msg,) = call(
        factor_grads_kernel,
        [(ids, "s"), (got.reshape(by_block), "v"), (swap(got).reshape(by_block), "v")]
        + [(factors, "v")],
        [(by_home, BF16, "h")],
        [((2, 3, wide, wide), BF16), ((2, total, wide), F32), ((2, total, wide), F32)]
        + [((n_y, n_row, MSG_ROWS, lanes), BF16)],
        sems=(4,),
        flops=16 * total * wide * wide,
        moved=4 * MIB,
    )
    got = exchange(msg.reshape(two))
    (grad_pair,) = call(
        pair_grad_kernel,
        [(ids, "s"), (got, "v"), (kept, "v"), (kept_par, "v")],
        [(block, BF16, "h")],
        [((half * MSG_ROWS, lanes), F32), (flat, F32), (flat, F32), (block, BF16)],
        sems=(2,),
        flops=2 * size * width * 4 * hidden,
        moved=8 * MIB,
    )
    return (update, grad_pair)


def solution(mesh):
    n_row, n_col, n_rep = mesh.devices.shape
    mesh = Mesh(mesh.devices.reshape(n_row, n_col // 2, 2, n_rep), ("row", "y", "core", "rep"))
    block = P(("rep", "row"), ("y", "core"), None)
    return jax.shard_map(
        local,
        mesh=mesh,
        in_specs=(block, P("rep"), block, P(), P(), P(), P()),
        out_specs=(block, block),
        check_vma=False,
    )
```

```python
import jax
import jax.numpy as jnp
from jax import lax
from jax.experimental import pallas as pl
from jax.experimental.pallas import tpu as pltpu
from jax.sharding import Mesh
from jax.sharding import PartitionSpec as P

EPS = 1e-05
F32 = jnp.float32
BF16 = jnp.bfloat16
MIB = 1 << 20
LAST = (((1,), (1,)), ((), ()))
FIRST = (((0,), (0,)), ((), ()))
SLOT = 64
PIECE = 16
MSG_ROWS = 40
GROUP = 4


def dot(a, b, dims=(((1,), (0,)), ((), ()))):
    return lax.dot_general(a, b, dims, preferred_element_type=F32)


def identity(n):
    row = lax.broadcasted_iota(jnp.int32, (n, n), 0)
    col = lax.broadcasted_iota(jnp.int32, (n, n), 1)
    return jnp.where(row == col, 1.0, 0.0).astype(BF16)


def low_lanes(shape):
    return lax.broadcasted_iota(jnp.int32, shape, len(shape) - 1) < SLOT


def half_turn(x):
    return turn(x, SLOT)


def turn(x, by):
    return pltpu.roll(x, by % x.shape[-1], x.ndim - 1)


def place_in_slot(shape):
    return lax.rem(lax.broadcasted_iota(jnp.int32, shape, len(shape) - 1), SLOT)


def straight_lanes(ids_ref, shape):
    lane = lax.broadcasted_iota(jnp.int32, shape, len(shape) - 1)
    return jnp.where(lane < SLOT, 0, 1) == ids_ref[3]


def swap_pairs(x):
    return jnp.concatenate([x[n ^ 1][None] for n in range(x.shape[0])], axis=0)


def unit_of(x):
    mean = jnp.mean(x, axis=-1, keepdims=True)
    centered = x - mean
    variance = jnp.mean(centered * centered, axis=-1, keepdims=True)
    inverse = lax.rsqrt(variance + EPS)
    return centered * inverse, inverse


def mask_of(ids_ref, len_ref, row, shape):
    limit = len_ref[0]
    for i in range(1, len_ref.shape[0]):
        limit = limit + len_ref[i]
    bound = jnp.where(ids_ref[0] + row < limit, limit - ids_ref[1], 0)
    return lax.broadcasted_iota(jnp.int32, shape, 0) < bound


def start(source, target, sem):
    copy = pltpu.make_async_copy(source, target, sem)
    copy.start()
    return copy


def paired(first, second):
    gap = jnp.zeros((SLOT - first.shape[0], first.shape[1]), first.dtype)
    return jnp.concatenate([first, gap, second, gap], axis=0)


def factors_kernel(
    ids_ref, len_ref, pair_ref, par_ref, w_ref, msg_ref,
    scr, a_buf, b_buf, pair_buf, par_buf, w_buf, len_buf, sems,
):
    rows, cols, width = pair_ref.shape
    hidden = w_ref.shape[1] // 4
    half = hidden // 2
    sources = (pair_ref, w_ref, par_ref, len_ref)
    targets = (pair_buf, w_buf, par_buf, len_buf)
    copies = [start(x, y, sems.at[n]) for n, (x, y) in enumerate(zip(sources, targets))]
    eye = identity(hidden)
    for copy in copies:
        copy.wait()
    gain, shift = par_buf[0:1, :], par_buf[1:2, :]
    w = w_buf[...]
    straight = straight_lanes(ids_ref, (cols, hidden))
    for first in range(0, rows, GROUP):
        x = pair_buf[first : first + GROUP].astype(F32).reshape(GROUP * cols, width)
        unit, _ = unit_of(x)
        normed = (unit * gain + shift).astype(BF16)
        proj = dot(normed, w)
        left = jax.nn.sigmoid(proj[:, :hidden]) * proj[:, hidden : 2 * hidden]
        right = jax.nn.sigmoid(proj[:, 2 * hidden : 3 * hidden]) * proj[:, 3 * hidden :]
        for k in range(GROUP):
            mask = mask_of(ids_ref, len_buf, first + k, (cols, hidden))
            at = slice(k * cols, (k + 1) * cols)
            one, two = jnp.where(mask, left[at], 0.0), jnp.where(mask, right[at], 0.0)
            a_buf[first + k] = jnp.where(straight, one, two).astype(BF16)
            b_buf[first + k] = jnp.where(straight, two, one).astype(BF16)
    main, tail = 16, 8
    gap = jnp.zeros((2 * PIECE, hidden), BF16)
    low = place_in_slot((half, 2 * SLOT)) < PIECE
    for first in range(0, main + tail, GROUP):
        parts = []
        for s in range(first, first + GROUP):
            if s < main:
                e, at = main + s % tail, pl.ds(s // tail * PIECE, PIECE)
                parts += [a_buf[s], a_buf[e, at], b_buf[s], b_buf[e, at]]
            else:
                at = pl.ds(2 * PIECE, PIECE)
                parts += [a_buf[s, at], a_buf[s, at], gap, b_buf[s, at], b_buf[s, at], gap]
        turned = dot(eye, jnp.concatenate(parts, axis=0), LAST)
        for n, s in enumerate(range(first, first + GROUP)):
            one = turned[:half, n * hidden : (n + 1) * hidden]
            two = turned[half:, n * hidden : (n + 1) * hidden]
            if s < main:
                scr[pl.ds(s, half, stride=MSG_ROWS), :] = one
                scr[pl.ds(main + s, half, stride=MSG_ROWS), :] = two
            else:
                scr[pl.ds(main + s, half, stride=MSG_ROWS), :] = jnp.where(low, one, two)
    msg_ref[...] = scr[...].reshape(msg_ref.shape).astype(BF16)


def saved_kernel(
    ids_ref, len_ref, pair_ref, after_ref, cot_ref, par_ref, w_in_ref, w_gate_ref, w_out_ref,
    gate_ref, scaled_ref, coef_ref, scr,
):
    rows, cols, width = pair_ref.shape
    hidden = w_in_ref.shape[1] // 4
    half = hidden // 2
    first_half = ~straight_lanes(ids_ref, (half, 2 * SLOT))
    w_in, w_gate, w_out = w_in_ref[...], w_gate_ref[...], w_out_ref[...]
    for first in range(0, rows, GROUP):
        size = GROUP * cols
        at = slice(first * cols, first * cols + size)
        x = pair_ref[first : first + GROUP].astype(F32).reshape(size, width)
        unit, _ = unit_of(x)
        normed = (unit * par_ref[0:1, :] + par_ref[1:2, :]).astype(BF16)
        gate = jax.nn.sigmoid(dot(normed, w_gate))
        gate_ref[at, :] = gate
        cot = cot_ref[first : first + GROUP].astype(F32).reshape(size, width)
        grad_lin = (cot * gate).astype(BF16)
        scaled = dot(grad_lin, w_out, LAST) * par_ref[2:3, :]
        scaled = scaled - jnp.mean(scaled, axis=-1, keepdims=True)
        proj = dot(normed, w_in)
        masks = []
        for k in range(GROUP):
            one = scaled[k * cols : (k + 1) * cols]
            turned = jnp.transpose(paired(one, one))
            turned = jnp.where(first_half, turned[:half], turned[half:])
            scr[pl.ds(first + k, half, stride=rows), :] = turned
            mask = mask_of(ids_ref, len_ref, first + k, (cols, hidden))
            masks.append(jnp.where(mask, 1.0, 0.0))
        mask = jnp.concatenate(masks, axis=0)
        for side in range(2):
            sig = jax.nn.sigmoid(proj[:, 2 * side * hidden : (2 * side + 1) * hidden])
            val = proj[:, (2 * side + 1) * hidden : (2 * side + 2) * hidden]
            kept = mask * sig
            for n, x in enumerate((kept * val * (1.0 - sig), kept)):
                place = (2 * side + n) * rows * cols + first * cols
                coef_ref[place : place + size, :] = x.astype(BF16)
    scaled_ref[...] = scr[...].reshape(scaled_ref.shape)


def unpacked(ref, y, total):
    n_row, _, _, lanes = ref.shape
    at_lane = place_in_slot((n_row, 8, lanes))
    got = ref[:, y].astype(F32)
    tail = got[:, 32:40]
    result = []
    for c in range(2):
        one, two = got[:, 16 * c : 16 * c + 8], got[:, 16 * c + 8 : 16 * c + 16]
        rest = jnp.where(at_lane < 3 * PIECE, turn(tail, (2 - c) * PIECE), 0.0)
        rest = jnp.where(at_lane < 2 * PIECE, turn(two, -2 * PIECE), rest)
        rest = jnp.where(at_lane < PIECE, turn(one, -3 * PIECE), rest)
        one = jnp.where(at_lane < 3 * PIECE, one, 0.0)
        two = jnp.where(at_lane < 3 * PIECE, two, 0.0)
        result.append(jnp.concatenate([one, two, rest], axis=1).reshape(total, lanes))
    return result


def unpack_factors(ref, left, right):
    n_y, lanes = ref.shape[1], ref.shape[-1]
    total = left.shape[-2]
    low = low_lanes((total, lanes))
    for t in range(n_y // 2):
        at = slice(t * lanes, (t + 1) * lanes)
        even, odd = unpacked(ref, 2 * t, total), unpacked(ref, 2 * t + 1, total)
        left[0, :, at] = jnp.where(low, even[0], odd[0]).astype(BF16)
        left[1, :, at] = jnp.where(low, odd[1], even[1]).astype(BF16)
        if right is not None:
            right[0, :, at] = jnp.where(low, odd[0], even[0]).astype(BF16)
            right[1, :, at] = jnp.where(low, even[1], odd[1]).astype(BF16)


def triangle_messages(left_buf, right, tri_scr, out, rows):
    n_y, lanes = out.shape[0], out.shape[-1]
    low = low_lanes((n_y, 2, rows, lanes))
    for c in range(2):
        tri_scr[c] = dot(left_buf[c], right[c], FIRST)
    for t in range(n_y // 2):
        a, b = (
            tri_scr[c, :, t * lanes : (t + 1) * lanes]
            .reshape(n_y, SLOT, lanes)[:, : 2 * rows]
            .reshape(n_y, 2, rows, lanes)
            for c in range(2)
        )
        b = swap_pairs(b)
        out[:, :, 2 * t] = jnp.where(low, b, a).astype(BF16)
        out[:, :, 2 * t + 1] = jnp.where(low, a, b).astype(BF16)


def own_triangle_kernel(own_ref, part_ref, right_ref, tri_scr, left_buf):
    unpack_factors(own_ref, left_buf, right_ref)
    triangle_messages(left_buf, right_ref, tri_scr, part_ref, part_ref.shape[-2])


def other_triangle_kernel(
    ids_ref, other_ref, part_ref, right_ref, msg_ref, tri_scr, left_buf, part_buf, sems
):
    core = ids_ref[2]
    first = start(part_ref, msg_ref.at[:, core], sems.at[0])
    unpack_factors(other_ref, left_buf, None)
    triangle_messages(left_buf, right_ref, tri_scr, part_buf, part_ref.shape[-2])
    second = start(part_buf, msg_ref.at[:, 1 - core], sems.at[1])
    first.wait()
    second.wait()


def keep_factors_kernel(own_ref, other_ref, after_ref, factors_ref):
    for side, ref in enumerate((own_ref, other_ref)):
        unpack_factors(ref, factors_ref.at[0, side], factors_ref.at[1, side])


def norm_kernel(got_ref, scaled_ref, msg_ref, scr):
    half, rows, lanes = got_ref.shape
    scr[...] = got_ref[...].astype(F32)

    def mean(x):
        part = jnp.sum(x, axis=0)
        return (part + half_turn(part)) * (1.0 / (2 * half))

    for first in range(0, rows, 8):
        at = slice(first, first + 8)
        x = scr[:, at]
        x = x - mean(x)[None]
        inverse = lax.rsqrt(mean(x * x) + EPS)
        s = scaled_ref[:, at]
        along = inverse * inverse * mean(s * x)
        scr[:, at] = inverse[None] * (s - x * along[None])
    msg_ref[...] = scr[...].astype(BF16)


def update_kernel(
    ids_ref, got_ref, gate_ref, cot_ref, par_ref, w_out_ref, w_gate_ref, w_in_ref, coef_ref,
    pair_ref, update_ref, gn_ref, kept_coef_ref, kept_pair_ref, kept_w_in_ref, kept_par_ref,
    scr, gate_buf, cot_buf, w_out_buf, w_gate_buf, sems,
):
    sources = (coef_ref, pair_ref, w_in_ref, par_ref, gate_ref, cot_ref, w_out_ref, w_gate_ref)
    targets = (kept_coef_ref, kept_pair_ref, kept_w_in_ref, kept_par_ref)
    targets += (gate_buf, cot_buf, w_out_buf, w_gate_buf)
    copies = [start(x, y, sems.at[n]) for n, (x, y) in enumerate(zip(sources, targets))]
    for copy in copies:
        copy.wait()
    rows, cols, width = cot_ref.shape
    half, _, lanes = got_ref.shape
    w_out, w_gate = w_out_buf[...], w_gate_buf[...]
    gain, shift = kept_par_ref[2:3, :], kept_par_ref[3:4, :]
    row = lax.broadcasted_iota(jnp.int32, (cols, 2 * lanes), 0)
    col = lax.broadcasted_iota(jnp.int32, (cols, 2 * lanes), 1)
    odd = ids_ref[3] * SLOT
    pick = (col == row + (SLOT - odd)) | (col == row + (lanes + odd))
    pick = jnp.where(pick, 1.0, 0.0).astype(BF16)
    nothing = jnp.zeros((half, lanes), BF16)
    scr[...] = got_ref[...].astype(F32).reshape(half * rows, lanes)
    for first in range(0, rows, GROUP):
        size = GROUP * cols
        at = slice(first * cols, first * cols + size)
        tri = []
        for k in range(first, first + GROUP):
            x = scr[pl.ds(k, half, stride=rows), :].astype(BF16)
            both = jnp.concatenate(
                [jnp.concatenate([x, nothing], axis=1), jnp.concatenate([nothing, x], axis=1)],
                axis=0,
            )
            tri.append(dot(pick, both, LAST))
        unit, _ = unit_of(jnp.concatenate(tri, axis=0))
        lin = dot((unit * gain + shift).astype(BF16), w_out)
        gate = gate_buf[at, :]
        update_ref[first : first + GROUP] = (gate * lin).astype(BF16).reshape(GROUP, cols, width)
        cot = cot_buf[first : first + GROUP].astype(F32).reshape(size, width)
        grad_gate = (cot * lin * gate * (1.0 - gate)).astype(BF16)
        gn_ref[at, :] = dot(grad_gate, w_gate, LAST)


def unpack_grads(ref, place, tri_scr):
    n_y, _, _, _, rows, lanes = ref.shape
    low = low_lanes((n_y, 2, rows, lanes))
    gap = jnp.zeros((n_y, SLOT - 2 * rows, lanes), F32)
    for t in range(n_y // 2):
        even = ref[:, place, :, 2 * t].astype(F32)
        odd = ref[:, place, :, 2 * t + 1].astype(F32)
        first = jnp.where(low, odd, even)
        second = swap_pairs(jnp.where(low, even, odd))
        for c, tile in enumerate((first, second)):
            tile = jnp.concatenate([tile.reshape(n_y, 2 * rows, lanes), gap], axis=1)
            tile = tile.reshape(n_y * SLOT, lanes).astype(BF16)
            tri_scr[c, :, t * lanes : (t + 1) * lanes] = tile


def own_grads_kernel(ids_ref, own_ref, factors_ref, gl_ref, gr_ref, tri_scr):
    core = ids_ref[2]
    unpack_grads(own_ref, core, tri_scr.at[0])
    unpack_grads(own_ref, 1 - core, tri_scr.at[1])
    for c in range(2):
        left, far_left, right = factors_ref[0, 0, c], factors_ref[0, 1, c], factors_ref[1, 0, c]
        gl_ref[c] = dot(right, tri_scr[0, c], LAST)
        gr_ref[c] = dot(left, tri_scr[0, c]) + dot(far_left, tri_scr[1, c])


def other_grads_kernel(
    ids_ref, other_ref, factors_ref, gl_ref, gr_ref, msg_ref, tri_scr, gl_scr, msg_buf, sems
):
    n_row, n_y, _, lanes = msg_ref.shape
    total = gl_ref.shape[1]
    rows = total // n_row
    unpack_grads(other_ref, ids_ref[2], tri_scr)
    for c in range(2):
        gl_scr[c] = gl_ref[c] + dot(factors_ref[1, 1, c], tri_scr[c], LAST)
    results = []
    low = low_lanes((total, lanes))
    at_lane = place_in_slot((n_row, 8, lanes))
    for y in range(n_y):
        tails = []
        for c in range(2):
            at = slice(y // 2 * lanes, y // 2 * lanes + lanes)
            a, b = gl_scr[c, :, at], gr_ref[c, :, at]
            if (y + c) % 2:
                a, b = b, a
            both = jnp.where(low, a, b).reshape(n_row, rows, lanes)
            one, two, rest = both[:, :8], both[:, 8:16], both[:, 16:24]
            one = jnp.where(at_lane < 3 * PIECE, one, turn(rest, 3 * PIECE))
            two = jnp.where(at_lane < 3 * PIECE, two, turn(rest, 2 * PIECE))
            msg_buf[y, :, 16 * c : 16 * c + 16] = jnp.concatenate([one, two], axis=1).astype(BF16)
            tails.append(turn(rest, (c - 2) * PIECE))
        tail = jnp.where(at_lane < PIECE, tails[0], tails[1])
        msg_buf[y, :, 32:40] = tail.astype(BF16)
        results.append(start(msg_buf.at[y], msg_ref.at[:, y], sems.at[y]))
    for copy in results:
        copy.wait()


def pair_grad_kernel(
    ids_ref, got_ref, gn_ref, coef_ref, pair_ref, w_in_ref, par_ref, out_ref,
    scr, left_buf, right_buf, out_buf, sems,
):
    half, _, lanes = got_ref.shape
    rows, cols, width = out_ref.shape
    eye = identity(2 * half)
    scr[...] = got_ref[...].astype(F32).reshape(half * MSG_ROWS, lanes)
    main, tail = 16, 8
    low = low_lanes((PIECE, 2 * half))
    for first in range(0, main + tail, GROUP):
        parts = []
        for s in range(first, first + GROUP):
            if s < main:
                parts += [scr[pl.ds(c * main + s, half, stride=MSG_ROWS), :] for c in range(2)]
            else:
                parts += [scr[pl.ds(main + s, half, stride=MSG_ROWS), :]] * 2
        turned = dot(eye, jnp.concatenate(parts, axis=0).astype(BF16), LAST)
        for n, s in enumerate(range(first, first + GROUP)):
            both = turned[:, n * 2 * half : (n + 1) * 2 * half]
            for buf, x in ((left_buf, both[:SLOT]), (right_buf, both[SLOT:])):
                if s < main:
                    at = (main + s % tail) * cols + s // tail * PIECE
                    buf[s * cols : (s + 1) * cols, :] = x[:cols]
                    buf[at : at + PIECE, :] = x[cols:]
                else:
                    at = s * cols + 2 * PIECE
                    buf[at : at + PIECE, :] = jnp.where(low, x[:PIECE], x[PIECE : 2 * PIECE])
    gain = par_ref[0:1, :]
    flat = rows * cols
    w_in = w_in_ref[...]
    size = GROUP * cols
    straight = straight_lanes(ids_ref, (size, 2 * half))
    results = []
    for first in range(0, rows, GROUP):
        at = slice(first * cols, first * cols + size)
        left = jnp.where(straight, left_buf[at, :], right_buf[at, :])
        right = jnp.where(straight, right_buf[at, :], left_buf[at, :])
        coef_a, val_a, coef_b, val_b = (
            coef_ref[n * flat + first * cols : n * flat + first * cols + size, :].astype(F32)
            for n in range(4)
        )
        grad_proj = jnp.concatenate(
            [
                (side * factor).astype(BF16)
                for side, factor in ((left, coef_a), (left, val_a), (right, coef_b), (right, val_b))
            ],
            axis=1,
        )
        s = (dot(grad_proj, w_in, LAST) + gn_ref[at, :]) * gain
        unit, inverse = unit_of(pair_ref[at, :].astype(F32))
        grad = inverse * (
            s
            - jnp.mean(s, axis=-1, keepdims=True)
            - unit * jnp.mean(s * unit, axis=-1, keepdims=True)
        )
        out_buf[first : first + GROUP] = grad.astype(BF16).reshape(GROUP, cols, width)
        if (first + GROUP) % (rows // 2) == 0:
            part = pl.ds(first + GROUP - rows // 2, rows // 2)
            n = first // (rows // 2)
            results.append(start(out_buf.at[part], out_ref.at[part], sems.at[n]))
    for copy in results:
        copy.wait()


def call(kernel, ins, outs, scratch=(), smem=(), sems=(), limit=12, flops=0, moved=0):
    spaces = {"s": pltpu.SMEM, "v": pltpu.VMEM, "b": pltpu.VMEM, "h": pltpu.HBM}
    extra = [pltpu.SMEM(s, d) for s, d in smem]
    if sems:
        extra.append(pltpu.SemaphoreType.DMA(sems))
    return pl.pallas_call(
        kernel,
        out_shape=[
            jax.ShapeDtypeStruct(s, d) if place == "v" else pltpu.HBM(s, d)
            for s, d, place in outs
        ],
        in_specs=[pl.BlockSpec(memory_space=spaces[place]) for _, place in ins],
        out_specs=[pl.BlockSpec(memory_space=spaces[place]) for _, _, place in outs],
        scratch_shapes=[pltpu.VMEM(s, d) for s, d in scratch] + extra,
        compiler_params=pltpu.CompilerParams(vmem_limit_bytes=limit * MIB),
        cost_estimate=pl.CostEstimate(flops=flops, bytes_accessed=moved, transcendentals=0),
    )(
        *(
            pltpu.with_memory_space_constraint(x, pltpu.HBM) if place == "h" else x
            for x, place in ins
        )
    )


def exchange(x):
    return lax.all_to_all(x, ("row", "y"), 0, 0, tiled=True)


def swap(x):
    return lax.ppermute(x, "core", [(0, 1), (1, 0)])


def local(pair, chain_lengths, cotangent, norm_params, w_in, w_gate, w_out):
    rows, cols, width = pair.shape
    hidden = w_out.shape[0]
    n_row, n_y = lax.axis_size("row"), lax.axis_size("y")
    assert hidden == 2 * n_row * n_y == 2 * SLOT and width == hidden
    assert rows == 24 and cols == 2 * rows and n_row == 4 * n_y and lax.axis_size("core") == 2
    half = hidden // 2
    size, lanes = rows * cols, 2 * SLOT
    total, wide = n_row * rows, n_y * SLOT
    row, core = lax.axis_index("row"), lax.axis_index("core")
    col = 2 * lax.axis_index("y") + core
    ids = jnp.stack([row * rows, col * cols, core, lax.axis_index("y") % 2]).astype(jnp.int32)

    flat = (size, width)
    block = (rows, cols, width)
    par = (norm_params.shape, F32)
    factor = (2, 2, total, wide)
    two = (half, MSG_ROWS, lanes)
    one = (half, rows, lanes)
    by_home = (n_row, n_y, MSG_ROWS, lanes)
    by_block = (n_y, 2, 2, n_y, rows, lanes)
    (msg,) = call(
        factors_kernel,
        [(ids, "s"), (chain_lengths, "h"), (pair, "h"), (norm_params, "h"), (w_in, "h")],
        [(two, BF16, "v")],
        [((half * MSG_ROWS, lanes), F32), (block, BF16), (block, BF16), (block, BF16), par]
        + [(w_in.shape, BF16)],
        smem=[(chain_lengths.shape, jnp.int32)],
        sems=(4,),
        flops=2 * size * width * 4 * hidden,
        moved=8 * MIB,
    )
    got = exchange(msg)
    own, other = got.reshape(by_home), swap(got).reshape(by_home)
    half_block = (n_y, 2, n_y, rows, lanes)
    part, right = call(
        own_triangle_kernel,
        [(own, "v")],
        [(half_block, BF16, "v"), (factor[1:], BF16, "v")],
        [((2, wide, wide), F32), (factor[1:], BF16)],
        flops=4 * total * wide * wide,
        moved=4 * MIB,
    )
    (msg,) = call(
        other_triangle_kernel,
        [(ids, "s"), (other, "v"), (part, "v"), (right, "v")],
        [(by_block, BF16, "h")],
        [((2, wide, wide), F32), (factor[1:], BF16), (half_block, BF16)],
        sems=(2,),
        flops=4 * total * wide * wide,
        moved=4 * MIB,
    )
    (factors,) = call(
        keep_factors_kernel,
        [(own, "v"), (other, "v"), (msg, "h")],
        [((2,) + factor, BF16, "b")],
        flops=8 * total * wide * wide,
        moved=4 * MIB,
    )
    got = exchange(msg.reshape(one))
    gate, scaled, coef = call(
        saved_kernel,
        [(ids, "s"), (chain_lengths, "s"), (pair, "v"), (factors, "h"), (cotangent, "v")]
        + [(norm_params, "v"), (w_in, "v"), (w_gate, "v"), (w_out, "v")],
        [(flat, F32, "b"), (one, F32, "v"), ((4 * size, width), BF16, "b")],
        [((half * rows, lanes), F32)],
        flops=2 * size * width * 6 * hidden,
        moved=24 * MIB,
    )
    (msg,) = call(
        norm_kernel,
        [(got, "v"), (scaled, "v")],
        [(one, BF16, "v")],
        [(one, F32)],
        flops=2 * size * width * hidden,
        moved=4 * MIB,
    )
    update, *kept = call(
        update_kernel,
        [(ids, "s"), (got, "v"), (gate, "h"), (cotangent, "h"), (norm_params, "h")]
        + [(w_out, "h"), (w_gate, "h"), (w_in, "h"), (coef, "h"), (pair.reshape(flat), "h")],
        [(block, BF16, "b"), (flat, F32, "v"), (coef.shape, BF16, "v"), (flat, BF16, "v")]
        + [(w_in.shape, BF16, "v"), par + ("v",)],
        [((half * rows, lanes), F32), (flat, F32), (block, BF16), (w_out.shape, BF16)]
        + [(w_gate.shape, BF16)],
        sems=(8,),
        flops=4 * size * width * hidden,
        moved=12 * MIB,
    )
    got = exchange(msg)
    other = swap(got).reshape(by_block)
    summed = ((2, total, wide), F32, "v")
    gl, gr = call(
        own_grads_kernel,
        [(ids, "s"), (got.reshape(by_block), "v"), (factors, "v")],
        [summed, summed],
        [((2, 2, wide, wide), BF16)],
        flops=12 * total * wide * wide,
        moved=4 * MIB,
    )
    (msg,) = call(
        other_grads_kernel,
        [(ids, "s"), (other, "v"), (factors, "v"), (gl, "v"), (gr, "v")],
        [(by_home, BF16, "h")],
        [((2, wide, wide), BF16), ((2, total, wide), F32)]
        + [((n_y, n_row, MSG_ROWS, lanes), BF16)],
        sems=(4,),
        flops=4 * total * wide * wide,
        moved=4 * MIB,
    )
    got = exchange(msg.reshape(two))
    (grad_pair,) = call(
        pair_grad_kernel,
        [(ids, "s"), (got, "v")] + [(x, "v") for x in kept],
        [(block, BF16, "h")],
        [((half * MSG_ROWS, lanes), F32), (flat, F32), (flat, F32), (block, BF16)],
        sems=(2,),
        flops=2 * size * width * 4 * hidden,
        moved=8 * MIB,
    )
    return (update, grad_pair)


def solution(mesh):
    n_row, n_col, n_rep = mesh.devices.shape
    mesh = Mesh(mesh.devices.reshape(n_row, n_col // 2, 2, n_rep), ("row", "y", "core", "rep"))
    block = P(("rep", "row"), ("y", "core"), None)
    return jax.shard_map(
        local,
        mesh=mesh,
        in_specs=(block, P("rep"), block, P(), P(), P(), P()),
        out_specs=(block, block),
        check_vma=False,
    )
```

```python
import jax
import jax.numpy as jnp
from jax import lax
from jax.experimental import pallas as pl
from jax.experimental.pallas import tpu as pltpu
from jax.sharding import Mesh
from jax.sharding import PartitionSpec as P

EPS = 1e-05
F32 = jnp.float32
BF16 = jnp.bfloat16
MIB = 1 << 20
LAST = (((1,), (1,)), ((), ()))
FIRST = (((0,), (0,)), ((), ()))
SLOT = 64
PIECE = 16
MSG_ROWS = 40
GROUP = 4


def dot(a, b, dims=(((1,), (0,)), ((), ()))):
    return lax.dot_general(a, b, dims, preferred_element_type=F32)


def identity(n):
    row = lax.broadcasted_iota(jnp.int32, (n, n), 0)
    col = lax.broadcasted_iota(jnp.int32, (n, n), 1)
    return jnp.where(row == col, 1.0, 0.0).astype(BF16)


def low_lanes(shape):
    return lax.broadcasted_iota(jnp.int32, shape, len(shape) - 1) < SLOT


def half_turn(x):
    return turn(x, SLOT)


def turn(x, by):
    return pltpu.roll(x, by % x.shape[-1], x.ndim - 1)


def place_in_slot(shape):
    return lax.rem(lax.broadcasted_iota(jnp.int32, shape, len(shape) - 1), SLOT)


def straight_lanes(ids_ref, shape):
    lane = lax.broadcasted_iota(jnp.int32, shape, len(shape) - 1)
    return jnp.where(lane < SLOT, 0, 1) == ids_ref[3]


def swap_pairs(x):
    return jnp.concatenate([x[n ^ 1][None] for n in range(x.shape[0])], axis=0)


def unit_of(x):
    mean = jnp.mean(x, axis=-1, keepdims=True)
    centered = x - mean
    variance = jnp.mean(centered * centered, axis=-1, keepdims=True)
    inverse = lax.rsqrt(variance + EPS)
    return centered * inverse, inverse


def mask_of(ids_ref, len_ref, row, shape):
    limit = len_ref[0]
    for i in range(1, len_ref.shape[0]):
        limit = limit + len_ref[i]
    bound = jnp.where(ids_ref[0] + row < limit, limit - ids_ref[1], 0)
    return lax.broadcasted_iota(jnp.int32, shape, 0) < bound


def start(source, target, sem):
    copy = pltpu.make_async_copy(source, target, sem)
    copy.start()
    return copy


def paired(first, second):
    gap = jnp.zeros((SLOT - first.shape[0], first.shape[1]), first.dtype)
    return jnp.concatenate([first, gap, second, gap], axis=0)


def factors_kernel(
    ids_ref, len_ref, pair_ref, par_ref, w_ref, msg_ref,
    scr, a_buf, b_buf, pair_buf, par_buf, w_buf, len_buf, sems,
):
    rows, cols, width = pair_ref.shape
    hidden = w_ref.shape[1] // 4
    half = hidden // 2
    sources = (pair_ref, w_ref, par_ref, len_ref)
    targets = (pair_buf, w_buf, par_buf, len_buf)
    copies = [start(x, y, sems.at[n]) for n, (x, y) in enumerate(zip(sources, targets))]
    eye = identity(hidden)
    for copy in copies:
        copy.wait()
    gain, shift = par_buf[0:1, :], par_buf[1:2, :]
    w = w_buf[...]
    straight = straight_lanes(ids_ref, (cols, hidden))
    for first in range(0, rows, GROUP):
        x = pair_buf[first : first + GROUP].astype(F32).reshape(GROUP * cols, width)
        unit, _ = unit_of(x)
        normed = (unit * gain + shift).astype(BF16)
        proj = dot(normed, w)
        left = jax.nn.sigmoid(proj[:, :hidden]) * proj[:, hidden : 2 * hidden]
        right = jax.nn.sigmoid(proj[:, 2 * hidden : 3 * hidden]) * proj[:, 3 * hidden :]
        for k in range(GROUP):
            mask = mask_of(ids_ref, len_buf, first + k, (cols, hidden))
            at = slice(k * cols, (k + 1) * cols)
            one, two = jnp.where(mask, left[at], 0.0), jnp.where(mask, right[at], 0.0)
            a_buf[first + k] = jnp.where(straight, one, two).astype(BF16)
            b_buf[first + k] = jnp.where(straight, two, one).astype(BF16)
    main, tail = 16, 8
    gap = jnp.zeros((2 * PIECE, hidden), BF16)
    low = place_in_slot((half, 2 * SLOT)) < PIECE
    for first in range(0, main + tail, GROUP):
        parts = []
        for s in range(first, first + GROUP):
            if s < main:
                e, at = main + s % tail, pl.ds(s // tail * PIECE, PIECE)
                parts += [a_buf[s], a_buf[e, at], b_buf[s], b_buf[e, at]]
            else:
                at = pl.ds(2 * PIECE, PIECE)
                parts += [a_buf[s, at], a_buf[s, at], gap, b_buf[s, at], b_buf[s, at], gap]
        turned = dot(eye, jnp.concatenate(parts, axis=0), LAST)
        for n, s in enumerate(range(first, first + GROUP)):
            one = turned[:half, n * hidden : (n + 1) * hidden]
            two = turned[half:, n * hidden : (n + 1) * hidden]
            if s < main:
                scr[pl.ds(s, half, stride=MSG_ROWS), :] = one
                scr[pl.ds(main + s, half, stride=MSG_ROWS), :] = two
            else:
                scr[pl.ds(main + s, half, stride=MSG_ROWS), :] = jnp.where(low, one, two)
    msg_ref[...] = scr[...].reshape(msg_ref.shape).astype(BF16)


def saved_kernel(
    ids_ref, len_ref, pair_ref, after_ref, cot_ref, par_ref, w_in_ref, w_gate_ref, w_out_ref,
    gate_ref, scaled_ref, coef_ref, scr,
):
    rows, cols, width = pair_ref.shape
    hidden = w_in_ref.shape[1] // 4
    half = hidden // 2
    first_half = ~straight_lanes(ids_ref, (half, 2 * SLOT))
    w_in, w_gate, w_out = w_in_ref[...], w_gate_ref[...], w_out_ref[...]
    for first in range(0, rows, GROUP):
        size = GROUP * cols
        at = slice(first * cols, first * cols + size)
        x = pair_ref[first : first + GROUP].astype(F32).reshape(size, width)
        unit, _ = unit_of(x)
        normed = (unit * par_ref[0:1, :] + par_ref[1:2, :]).astype(BF16)
        gate = jax.nn.sigmoid(dot(normed, w_gate))
        gate_ref[at, :] = gate
        cot = cot_ref[first : first + GROUP].astype(F32).reshape(size, width)
        grad_lin = (cot * gate).astype(BF16)
        scaled = dot(grad_lin, w_out, LAST) * par_ref[2:3, :]
        scaled = scaled - jnp.mean(scaled, axis=-1, keepdims=True)
        proj = dot(normed, w_in)
        masks = []
        for k in range(GROUP):
            one = scaled[k * cols : (k + 1) * cols]
            turned = jnp.transpose(paired(one, one))
            turned = jnp.where(first_half, turned[:half], turned[half:])
            scr[pl.ds(first + k, half, stride=rows), :] = turned
            mask = mask_of(ids_ref, len_ref, first + k, (cols, hidden))
            masks.append(jnp.where(mask, 1.0, 0.0))
        mask = jnp.concatenate(masks, axis=0)
        for side in range(2):
            sig = jax.nn.sigmoid(proj[:, 2 * side * hidden : (2 * side + 1) * hidden])
            val = proj[:, (2 * side + 1) * hidden : (2 * side + 2) * hidden]
            kept = mask * sig
            for n, x in enumerate((kept * val * (1.0 - sig), kept)):
                place = (2 * side + n) * rows * cols + first * cols
                coef_ref[place : place + size, :] = x.astype(BF16)
    scaled_ref[...] = scr[...].reshape(scaled_ref.shape)


def unpacked(ref, y, total):
    n_row, _, _, lanes = ref.shape
    at_lane = place_in_slot((n_row, 8, lanes))
    got = ref[:, y].astype(F32)
    tail = got[:, 32:40]
    result = []
    for c in range(2):
        one, two = got[:, 16 * c : 16 * c + 8], got[:, 16 * c + 8 : 16 * c + 16]
        rest = jnp.where(at_lane < 3 * PIECE, turn(tail, (2 - c) * PIECE), 0.0)
        rest = jnp.where(at_lane < 2 * PIECE, turn(two, -2 * PIECE), rest)
        rest = jnp.where(at_lane < PIECE, turn(one, -3 * PIECE), rest)
        one = jnp.where(at_lane < 3 * PIECE, one, 0.0)
        two = jnp.where(at_lane < 3 * PIECE, two, 0.0)
        result.append(jnp.concatenate([one, two, rest], axis=1).reshape(total, lanes))
    return result


def unpack_factors(ref, left, right):
    n_y, lanes = ref.shape[1], ref.shape[-1]
    total = left.shape[-2]
    low = low_lanes((total, lanes))
    for t in range(n_y // 2):
        at = slice(t * lanes, (t + 1) * lanes)
        even, odd = unpacked(ref, 2 * t, total), unpacked(ref, 2 * t + 1, total)
        left[0, :, at] = jnp.where(low, even[0], odd[0]).astype(BF16)
        left[1, :, at] = jnp.where(low, odd[1], even[1]).astype(BF16)
        if right is not None:
            right[0, :, at] = jnp.where(low, odd[0], even[0]).astype(BF16)
            right[1, :, at] = jnp.where(low, even[1], odd[1]).astype(BF16)


def triangle_messages(left_buf, right, tri_scr, out, rows, send=None):
    n_y, lanes = out.shape[0], out.shape[-1]
    low = low_lanes((n_y, 2, rows, lanes))
    for c in range(2):
        tri_scr[c] = dot(left_buf[c], right[c], FIRST)
    for t in range(n_y // 2):
        a, b = (
            tri_scr[c, :, t * lanes : (t + 1) * lanes]
            .reshape(n_y, SLOT, lanes)[:, : 2 * rows]
            .reshape(n_y, 2, rows, lanes)
            for c in range(2)
        )
        b = swap_pairs(b)
        out[:, :, 2 * t] = jnp.where(low, b, a).astype(BF16)
        out[:, :, 2 * t + 1] = jnp.where(low, a, b).astype(BF16)
        if send is not None:
            send(t)


def own_triangle_kernel(own_ref, part_ref, right_ref, tri_scr, left_buf):
    unpack_factors(own_ref, left_buf, right_ref)
    triangle_messages(left_buf, right_ref, tri_scr, part_ref, part_ref.shape[-2])


def other_triangle_kernel(
    ids_ref, other_ref, part_ref, right_ref, msg_ref, tri_scr, left_buf, part_buf, sems
):
    core = ids_ref[2]
    copies = [start(part_ref, msg_ref.at[:, core], sems.at[0])]

    def send(t):
        at = pl.ds(2 * t, 2)
        target = msg_ref.at[:, 1 - core, :, at]
        copies.append(start(part_buf.at[:, :, at], target, sems.at[1 + t]))

    unpack_factors(other_ref, left_buf, None)
    triangle_messages(left_buf, right_ref, tri_scr, part_buf, part_ref.shape[-2], send)
    for copy in copies:
        copy.wait()


def keep_factors_kernel(own_ref, other_ref, after_ref, factors_ref):
    for side, ref in enumerate((own_ref, other_ref)):
        unpack_factors(ref, factors_ref.at[0, side], factors_ref.at[1, side])


def norm_kernel(got_ref, scaled_ref, msg_ref, scr):
    half, rows, lanes = got_ref.shape
    scr[...] = got_ref[...].astype(F32)

    def mean(x):
        part = jnp.sum(x, axis=0)
        return (part + half_turn(part)) * (1.0 / (2 * half))

    for first in range(0, rows, 8):
        at = slice(first, first + 8)
        x = scr[:, at]
        x = x - mean(x)[None]
        inverse = lax.rsqrt(mean(x * x) + EPS)
        s = scaled_ref[:, at]
        along = inverse * inverse * mean(s * x)
        scr[:, at] = inverse[None] * (s - x * along[None])
    msg_ref[...] = scr[...].astype(BF16)


def update_kernel(
    ids_ref, got_ref, gate_ref, cot_ref, par_ref, w_out_ref, w_gate_ref, w_in_ref, coef_ref,
    pair_ref, update_ref, gn_ref, kept_coef_ref, kept_pair_ref, kept_w_in_ref, kept_par_ref,
    scr, gate_buf, cot_buf, w_out_buf, w_gate_buf, sems,
):
    sources = (coef_ref, pair_ref, w_in_ref, par_ref, gate_ref, cot_ref, w_out_ref, w_gate_ref)
    targets = (kept_coef_ref, kept_pair_ref, kept_w_in_ref, kept_par_ref)
    targets += (gate_buf, cot_buf, w_out_buf, w_gate_buf)
    copies = [start(x, y, sems.at[n]) for n, (x, y) in enumerate(zip(sources, targets))]
    for copy in copies:
        copy.wait()
    rows, cols, width = cot_ref.shape
    half, _, lanes = got_ref.shape
    w_out, w_gate = w_out_buf[...], w_gate_buf[...]
    gain, shift = kept_par_ref[2:3, :], kept_par_ref[3:4, :]
    row = lax.broadcasted_iota(jnp.int32, (cols, 2 * lanes), 0)
    col = lax.broadcasted_iota(jnp.int32, (cols, 2 * lanes), 1)
    odd = ids_ref[3] * SLOT
    pick = (col == row + (SLOT - odd)) | (col == row + (lanes + odd))
    pick = jnp.where(pick, 1.0, 0.0).astype(BF16)
    nothing = jnp.zeros((half, lanes), BF16)
    scr[...] = got_ref[...].astype(F32).reshape(half * rows, lanes)
    for first in range(0, rows, GROUP):
        size = GROUP * cols
        at = slice(first * cols, first * cols + size)
        tri = []
        for k in range(first, first + GROUP):
            x = scr[pl.ds(k, half, stride=rows), :].astype(BF16)
            both = jnp.concatenate(
                [jnp.concatenate([x, nothing], axis=1), jnp.concatenate([nothing, x], axis=1)],
                axis=0,
            )
            tri.append(dot(pick, both, LAST))
        unit, _ = unit_of(jnp.concatenate(tri, axis=0))
        lin = dot((unit * gain + shift).astype(BF16), w_out)
        gate = gate_buf[at, :]
        update_ref[first : first + GROUP] = (gate * lin).astype(BF16).reshape(GROUP, cols, width)
        cot = cot_buf[first : first + GROUP].astype(F32).reshape(size, width)
        grad_gate = (cot * lin * gate * (1.0 - gate)).astype(BF16)
        gn_ref[at, :] = dot(grad_gate, w_gate, LAST)


def unpack_grads(ref, place, tri_scr):
    n_y, _, _, _, rows, lanes = ref.shape
    low = low_lanes((n_y, 2, rows, lanes))
    gap = jnp.zeros((n_y, SLOT - 2 * rows, lanes), F32)
    for t in range(n_y // 2):
        even = ref[:, place, :, 2 * t].astype(F32)
        odd = ref[:, place, :, 2 * t + 1].astype(F32)
        first = jnp.where(low, odd, even)
        second = swap_pairs(jnp.where(low, even, odd))
        for c, tile in enumerate((first, second)):
            tile = jnp.concatenate([tile.reshape(n_y, 2 * rows, lanes), gap], axis=1)
            tile = tile.reshape(n_y * SLOT, lanes).astype(BF16)
            tri_scr[c, :, t * lanes : (t + 1) * lanes] = tile


def own_grads_kernel(ids_ref, own_ref, factors_ref, gl_ref, gr_ref, tri_scr):
    core = ids_ref[2]
    unpack_grads(own_ref, core, tri_scr.at[0])
    unpack_grads(own_ref, 1 - core, tri_scr.at[1])
    for c in range(2):
        left, far_left, right = factors_ref[0, 0, c], factors_ref[0, 1, c], factors_ref[1, 0, c]
        gl_ref[c] = dot(right, tri_scr[0, c], LAST)
        gr_ref[c] = dot(left, tri_scr[0, c]) + dot(far_left, tri_scr[1, c])


def other_grads_kernel(
    ids_ref, other_ref, factors_ref, gl_ref, gr_ref, msg_ref, tri_scr, gl_scr, msg_buf, sems
):
    n_row, n_y, _, lanes = msg_ref.shape
    total = gl_ref.shape[1]
    rows = total // n_row
    unpack_grads(other_ref, ids_ref[2], tri_scr)
    for c in range(2):
        gl_scr[c] = gl_ref[c] + dot(factors_ref[1, 1, c], tri_scr[c], LAST)
    results = []
    low = low_lanes((total, lanes))
    at_lane = place_in_slot((n_row, 8, lanes))
    for y in range(n_y):
        tails = []
        for c in range(2):
            at = slice(y // 2 * lanes, y // 2 * lanes + lanes)
            a, b = gl_scr[c, :, at], gr_ref[c, :, at]
            if (y + c) % 2:
                a, b = b, a
            both = jnp.where(low, a, b).reshape(n_row, rows, lanes)
            one, two, rest = both[:, :8], both[:, 8:16], both[:, 16:24]
            one = jnp.where(at_lane < 3 * PIECE, one, turn(rest, 3 * PIECE))
            two = jnp.where(at_lane < 3 * PIECE, two, turn(rest, 2 * PIECE))
            msg_buf[y, :, 16 * c : 16 * c + 16] = jnp.concatenate([one, two], axis=1).astype(BF16)
            tails.append(turn(rest, (c - 2) * PIECE))
        tail = jnp.where(at_lane < PIECE, tails[0], tails[1])
        msg_buf[y, :, 32:40] = tail.astype(BF16)
        results.append(start(msg_buf.at[y], msg_ref.at[:, y], sems.at[y]))
    for copy in results:
        copy.wait()


def pair_grad_kernel(
    ids_ref, got_ref, gn_ref, coef_ref, pair_ref, w_in_ref, par_ref, out_ref,
    scr, left_buf, right_buf, out_buf, sems,
):
    half, _, lanes = got_ref.shape
    rows, cols, width = out_ref.shape
    eye = identity(2 * half)
    scr[...] = got_ref[...].astype(F32).reshape(half * MSG_ROWS, lanes)
    main, tail = 16, 8
    low = low_lanes((PIECE, 2 * half))
    for first in range(0, main + tail, GROUP):
        parts = []
        for s in range(first, first + GROUP):
            if s < main:
                parts += [scr[pl.ds(c * main + s, half, stride=MSG_ROWS), :] for c in range(2)]
            else:
                parts += [scr[pl.ds(main + s, half, stride=MSG_ROWS), :]] * 2
        turned = dot(eye, jnp.concatenate(parts, axis=0).astype(BF16), LAST)
        for n, s in enumerate(range(first, first + GROUP)):
            both = turned[:, n * 2 * half : (n + 1) * 2 * half]
            for buf, x in ((left_buf, both[:SLOT]), (right_buf, both[SLOT:])):
                if s < main:
                    at = (main + s % tail) * cols + s // tail * PIECE
                    buf[s * cols : (s + 1) * cols, :] = x[:cols]
                    buf[at : at + PIECE, :] = x[cols:]
                else:
                    at = s * cols + 2 * PIECE
                    buf[at : at + PIECE, :] = jnp.where(low, x[:PIECE], x[PIECE : 2 * PIECE])
    gain = par_ref[0:1, :]
    flat = rows * cols
    w_in = w_in_ref[...]
    group = 2 * GROUP
    size = group * cols
    straight = straight_lanes(ids_ref, (size, 2 * half))
    results = []
    for first in range(0, rows, group):
        at = slice(first * cols, first * cols + size)
        left = jnp.where(straight, left_buf[at, :], right_buf[at, :])
        right = jnp.where(straight, right_buf[at, :], left_buf[at, :])
        coef_a, val_a, coef_b, val_b = (
            coef_ref[n * flat + first * cols : n * flat + first * cols + size, :].astype(F32)
            for n in range(4)
        )
        grad_proj = jnp.concatenate(
            [
                (side * factor).astype(BF16)
                for side, factor in ((left, coef_a), (left, val_a), (right, coef_b), (right, val_b))
            ],
            axis=1,
        )
        s = (dot(grad_proj, w_in, LAST) + gn_ref[at, :]) * gain
        unit, inverse = unit_of(pair_ref[at, :].astype(F32))
        grad = inverse * (
            s
            - jnp.mean(s, axis=-1, keepdims=True)
            - unit * jnp.mean(s * unit, axis=-1, keepdims=True)
        )
        out_buf[first : first + group] = grad.astype(BF16).reshape(group, cols, width)
        part = pl.ds(first, group)
        results.append(start(out_buf.at[part], out_ref.at[part], sems.at[first // group]))
    for copy in results:
        copy.wait()


def call(kernel, ins, outs, scratch=(), smem=(), sems=(), limit=12, flops=0, moved=0):
    spaces = {"s": pltpu.SMEM, "v": pltpu.VMEM, "b": pltpu.VMEM, "h": pltpu.HBM}
    extra = [pltpu.SMEM(s, d) for s, d in smem]
    if sems:
        extra.append(pltpu.SemaphoreType.DMA(sems))
    return pl.pallas_call(
        kernel,
        out_shape=[
            jax.ShapeDtypeStruct(s, d) if place == "v" else pltpu.HBM(s, d)
            for s, d, place in outs
        ],
        in_specs=[pl.BlockSpec(memory_space=spaces[place]) for _, place in ins],
        out_specs=[pl.BlockSpec(memory_space=spaces[place]) for _, _, place in outs],
        scratch_shapes=[pltpu.VMEM(s, d) for s, d in scratch] + extra,
        compiler_params=pltpu.CompilerParams(vmem_limit_bytes=limit * MIB),
        cost_estimate=pl.CostEstimate(flops=flops, bytes_accessed=moved, transcendentals=0),
    )(
        *(
            pltpu.with_memory_space_constraint(x, pltpu.HBM) if place == "h" else x
            for x, place in ins
        )
    )


def exchange(x):
    return lax.all_to_all(x, ("row", "y"), 0, 0, tiled=True)


def swap(x):
    return lax.ppermute(x, "core", [(0, 1), (1, 0)])


def local(pair, chain_lengths, cotangent, norm_params, w_in, w_gate, w_out):
    rows, cols, width = pair.shape
    hidden = w_out.shape[0]
    n_row, n_y = lax.axis_size("row"), lax.axis_size("y")
    assert hidden == 2 * n_row * n_y == 2 * SLOT and width == hidden
    assert rows == 24 and cols == 2 * rows and n_row == 4 * n_y and lax.axis_size("core") == 2
    half = hidden // 2
    size, lanes = rows * cols, 2 * SLOT
    total, wide = n_row * rows, n_y * SLOT
    row, core = lax.axis_index("row"), lax.axis_index("core")
    col = 2 * lax.axis_index("y") + core
    ids = jnp.stack([row * rows, col * cols, core, lax.axis_index("y") % 2]).astype(jnp.int32)

    flat = (size, width)
    block = (rows, cols, width)
    par = (norm_params.shape, F32)
    factor = (2, 2, total, wide)
    two = (half, MSG_ROWS, lanes)
    one = (half, rows, lanes)
    by_home = (n_row, n_y, MSG_ROWS, lanes)
    by_block = (n_y, 2, 2, n_y, rows, lanes)
    (msg,) = call(
        factors_kernel,
        [(ids, "s"), (chain_lengths, "h"), (pair, "h"), (norm_params, "h"), (w_in, "h")],
        [(two, BF16, "v")],
        [((half * MSG_ROWS, lanes), F32), (block, BF16), (block, BF16), (block, BF16), par]
        + [(w_in.shape, BF16)],
        smem=[(chain_lengths.shape, jnp.int32)],
        sems=(4,),
        flops=2 * size * width * 4 * hidden,
        moved=8 * MIB,
    )
    got = exchange(msg)
    own, other = got.reshape(by_home), swap(got).reshape(by_home)
    half_block = (n_y, 2, n_y, rows, lanes)
    part, right = call(
        own_triangle_kernel,
        [(own, "v")],
        [(half_block, BF16, "v"), (factor[1:], BF16, "v")],
        [((2, wide, wide), F32), (factor[1:], BF16)],
        flops=4 * total * wide * wide,
        moved=4 * MIB,
    )
    (msg,) = call(
        other_triangle_kernel,
        [(ids, "s"), (other, "v"), (part, "v"), (right, "v")],
        [(by_block, BF16, "h")],
        [((2, wide, wide), F32), (factor[1:], BF16), (half_block, BF16)],
        sems=(1 + n_y // 2,),
        flops=4 * total * wide * wide,
        moved=4 * MIB,
    )
    (factors,) = call(
        keep_factors_kernel,
        [(own, "v"), (other, "v"), (msg, "h")],
        [((2,) + factor, BF16, "b")],
        flops=8 * total * wide * wide,
        moved=4 * MIB,
    )
    got = exchange(msg.reshape(one))
    gate, scaled, coef = call(
        saved_kernel,
        [(ids, "s"), (chain_lengths, "s"), (pair, "v"), (factors, "h"), (cotangent, "v")]
        + [(norm_params, "v"), (w_in, "v"), (w_gate, "v"), (w_out, "v")],
        [(flat, F32, "b"), (one, F32, "v"), ((4 * size, width), BF16, "b")],
        [((half * rows, lanes), F32)],
        flops=2 * size * width * 6 * hidden,
        moved=24 * MIB,
    )
    (msg,) = call(
        norm_kernel,
        [(got, "v"), (scaled, "v")],
        [(one, BF16, "v")],
        [(one, F32)],
        flops=2 * size * width * hidden,
        moved=4 * MIB,
    )
    update, *kept = call(
        update_kernel,
        [(ids, "s"), (got, "v"), (gate, "h"), (cotangent, "h"), (norm_params, "h")]
        + [(w_out, "h"), (w_gate, "h"), (w_in, "h"), (coef, "h"), (pair.reshape(flat), "h")],
        [(block, BF16, "b"), (flat, F32, "v"), (coef.shape, BF16, "v"), (flat, BF16, "v")]
        + [(w_in.shape, BF16, "v"), par + ("v",)],
        [((half * rows, lanes), F32), (flat, F32), (block, BF16), (w_out.shape, BF16)]
        + [(w_gate.shape, BF16)],
        sems=(8,),
        flops=4 * size * width * hidden,
        moved=12 * MIB,
    )
    got = exchange(msg)
    other = swap(got).reshape(by_block)
    summed = ((2, total, wide), F32, "v")
    gl, gr = call(
        own_grads_kernel,
        [(ids, "s"), (got.reshape(by_block), "v"), (factors, "v")],
        [summed, summed],
        [((2, 2, wide, wide), BF16)],
        flops=12 * total * wide * wide,
        moved=4 * MIB,
    )
    (msg,) = call(
        other_grads_kernel,
        [(ids, "s"), (other, "v"), (factors, "v"), (gl, "v"), (gr, "v")],
        [(by_home, BF16, "h")],
        [((2, wide, wide), BF16), ((2, total, wide), F32)]
        + [((n_y, n_row, MSG_ROWS, lanes), BF16)],
        sems=(4,),
        flops=4 * total * wide * wide,
        moved=4 * MIB,
    )
    got = exchange(msg.reshape(two))
    (grad_pair,) = call(
        pair_grad_kernel,
        [(ids, "s"), (got, "v")] + [(x, "v") for x in kept],
        [(block, BF16, "h")],
        [((half * MSG_ROWS, lanes), F32), (flat, F32), (flat, F32), (block, BF16)],
        sems=(3,),
        flops=2 * size * width * 4 * hidden,
        moved=8 * MIB,
    )
    return (update, grad_pair)


def solution(mesh):
    n_row, n_col, n_rep = mesh.devices.shape
    mesh = Mesh(mesh.devices.reshape(n_row, n_col // 2, 2, n_rep), ("row", "y", "core", "rep"))
    block = P(("rep", "row"), ("y", "core"), None)
    return jax.shard_map(
        local,
        mesh=mesh,
        in_specs=(block, P("rep"), block, P(), P(), P(), P()),
        out_specs=(block, block),
        check_vma=False,
    )
```

```python
import jax
import jax.numpy as jnp
from jax import lax
from jax.experimental import pallas as pl
from jax.experimental.pallas import tpu as pltpu
from jax.sharding import Mesh
from jax.sharding import PartitionSpec as P

EPS = 1e-05
F32 = jnp.float32
BF16 = jnp.bfloat16
MIB = 1 << 20
LAST = (((1,), (1,)), ((), ()))
FIRST = (((0,), (0,)), ((), ()))
SLOT = 64
PIECE = 16
MSG_ROWS = 40
GROUP = 4


def dot(a, b, dims=(((1,), (0,)), ((), ()))):
    return lax.dot_general(a, b, dims, preferred_element_type=F32)


def identity(n):
    row = lax.broadcasted_iota(jnp.int32, (n, n), 0)
    col = lax.broadcasted_iota(jnp.int32, (n, n), 1)
    return jnp.where(row == col, 1.0, 0.0).astype(BF16)


def low_lanes(shape):
    return lax.broadcasted_iota(jnp.int32, shape, len(shape) - 1) < SLOT


def half_turn(x):
    return turn(x, SLOT)


def turn(x, by):
    return pltpu.roll(x, by % x.shape[-1], x.ndim - 1)


def place_in_slot(shape):
    return lax.rem(lax.broadcasted_iota(jnp.int32, shape, len(shape) - 1), SLOT)


def straight_lanes(ids_ref, shape):
    lane = lax.broadcasted_iota(jnp.int32, shape, len(shape) - 1)
    return jnp.where(lane < SLOT, 0, 1) == ids_ref[3]


def swap_pairs(x):
    return jnp.concatenate([x[n ^ 1][None] for n in range(x.shape[0])], axis=0)


def unit_of(x):
    mean = jnp.mean(x, axis=-1, keepdims=True)
    centered = x - mean
    variance = jnp.mean(centered * centered, axis=-1, keepdims=True)
    inverse = lax.rsqrt(variance + EPS)
    return centered * inverse, inverse


def mask_of(ids_ref, len_ref, row, shape):
    limit = len_ref[0]
    for i in range(1, len_ref.shape[0]):
        limit = limit + len_ref[i]
    bound = jnp.where(ids_ref[0] + row < limit, limit - ids_ref[1], 0)
    return lax.broadcasted_iota(jnp.int32, shape, 0) < bound


def start(source, target, sem):
    copy = pltpu.make_async_copy(source, target, sem)
    copy.start()
    return copy


def paired(first, second):
    gap = jnp.zeros((SLOT - first.shape[0], first.shape[1]), first.dtype)
    return jnp.concatenate([first, gap, second, gap], axis=0)


def factors_kernel(
    ids_ref, len_ref, pair_ref, par_ref, w_ref, msg_ref,
    scr, a_buf, b_buf, pair_buf, par_buf, w_buf, len_buf, sems,
):
    rows, cols, width = pair_ref.shape
    hidden = w_ref.shape[1] // 4
    half = hidden // 2
    sources = (pair_ref, w_ref, par_ref, len_ref)
    targets = (pair_buf, w_buf, par_buf, len_buf)
    copies = [start(x, y, sems.at[n]) for n, (x, y) in enumerate(zip(sources, targets))]
    eye = identity(hidden)
    for copy in copies:
        copy.wait()
    gain, shift = par_buf[0:1, :], par_buf[1:2, :]
    w = w_buf[...]
    straight = straight_lanes(ids_ref, (cols, hidden))
    for first in range(0, rows, GROUP):
        x = pair_buf[first : first + GROUP].astype(F32).reshape(GROUP * cols, width)
        unit, _ = unit_of(x)
        normed = (unit * gain + shift).astype(BF16)
        proj = dot(normed, w)
        left = jax.nn.sigmoid(proj[:, :hidden]) * proj[:, hidden : 2 * hidden]
        right = jax.nn.sigmoid(proj[:, 2 * hidden : 3 * hidden]) * proj[:, 3 * hidden :]
        for k in range(GROUP):
            mask = mask_of(ids_ref, len_buf, first + k, (cols, hidden))
            at = slice(k * cols, (k + 1) * cols)
            one, two = jnp.where(mask, left[at], 0.0), jnp.where(mask, right[at], 0.0)
            a_buf[first + k] = jnp.where(straight, one, two).astype(BF16)
            b_buf[first + k] = jnp.where(straight, two, one).astype(BF16)
    main, tail = 16, 8
    gap = jnp.zeros((2 * PIECE, hidden), BF16)
    low = place_in_slot((half, 2 * SLOT)) < PIECE
    for first in range(0, main + tail, GROUP):
        parts = []
        for s in range(first, first + GROUP):
            if s < main:
                e, at = main + s % tail, pl.ds(s // tail * PIECE, PIECE)
                parts += [a_buf[s], a_buf[e, at], b_buf[s], b_buf[e, at]]
            else:
                at = pl.ds(2 * PIECE, PIECE)
                parts += [a_buf[s, at], a_buf[s, at], gap, b_buf[s, at], b_buf[s, at], gap]
        turned = dot(eye, jnp.concatenate(parts, axis=0), LAST)
        for n, s in enumerate(range(first, first + GROUP)):
            one = turned[:half, n * hidden : (n + 1) * hidden]
            two = turned[half:, n * hidden : (n + 1) * hidden]
            if s < main:
                scr[pl.ds(s, half, stride=MSG_ROWS), :] = one
                scr[pl.ds(main + s, half, stride=MSG_ROWS), :] = two
            else:
                scr[pl.ds(main + s, half, stride=MSG_ROWS), :] = jnp.where(low, one, two)
    msg_ref[...] = scr[...].reshape(msg_ref.shape).astype(BF16)


def saved_kernel(
    ids_ref, len_ref, pair_ref, after_ref, cot_ref, par_ref, w_in_ref, w_gate_ref, w_out_ref,
    gate_ref, scaled_ref, coef_ref, scr,
):
    rows, cols, width = pair_ref.shape
    hidden = w_in_ref.shape[1] // 4
    half = hidden // 2
    first_half = ~straight_lanes(ids_ref, (half, 2 * SLOT))
    w_in, w_gate, w_out = w_in_ref[...], w_gate_ref[...], w_out_ref[...]
    for first in range(0, rows, GROUP):
        size = GROUP * cols
        at = slice(first * cols, first * cols + size)
        x = pair_ref[first : first + GROUP].astype(F32).reshape(size, width)
        unit, _ = unit_of(x)
        normed = (unit * par_ref[0:1, :] + par_ref[1:2, :]).astype(BF16)
        gate = jax.nn.sigmoid(dot(normed, w_gate))
        gate_ref[at, :] = gate
        cot = cot_ref[first : first + GROUP].astype(F32).reshape(size, width)
        grad_lin = (cot * gate).astype(BF16)
        scaled = dot(grad_lin, w_out, LAST) * par_ref[2:3, :]
        scaled = scaled - jnp.mean(scaled, axis=-1, keepdims=True)
        proj = dot(normed, w_in)
        masks = []
        for k in range(GROUP):
            one = scaled[k * cols : (k + 1) * cols]
            turned = jnp.transpose(paired(one, one))
            turned = jnp.where(first_half, turned[:half], turned[half:])
            scr[pl.ds(first + k, half, stride=rows), :] = turned
            mask = mask_of(ids_ref, len_ref, first + k, (cols, hidden))
            masks.append(jnp.where(mask, 1.0, 0.0))
        mask = jnp.concatenate(masks, axis=0)
        for side in range(2):
            sig = jax.nn.sigmoid(proj[:, 2 * side * hidden : (2 * side + 1) * hidden])
            val = proj[:, (2 * side + 1) * hidden : (2 * side + 2) * hidden]
            kept = mask * sig
            for n, x in enumerate((kept * val * (1.0 - sig), kept)):
                place = (2 * side + n) * rows * cols + first * cols
                coef_ref[place : place + size, :] = x.astype(BF16)
    scaled_ref[...] = scr[...].reshape(scaled_ref.shape)


def unpacked(ref, y, total):
    n_row, _, _, lanes = ref.shape
    at_lane = place_in_slot((n_row, 8, lanes))
    got = ref[:, y].astype(F32)
    tail = got[:, 32:40]
    result = []
    for c in range(2):
        one, two = got[:, 16 * c : 16 * c + 8], got[:, 16 * c + 8 : 16 * c + 16]
        rest = jnp.where(at_lane < 3 * PIECE, turn(tail, (2 - c) * PIECE), 0.0)
        rest = jnp.where(at_lane < 2 * PIECE, turn(two, -2 * PIECE), rest)
        rest = jnp.where(at_lane < PIECE, turn(one, -3 * PIECE), rest)
        one = jnp.where(at_lane < 3 * PIECE, one, 0.0)
        two = jnp.where(at_lane < 3 * PIECE, two, 0.0)
        result.append(jnp.concatenate([one, two, rest], axis=1).reshape(total, lanes))
    return result


def unpack_factors(ref, left, right):
    n_y, lanes = ref.shape[1], ref.shape[-1]
    total = left.shape[-2]
    low = low_lanes((total, lanes))
    for t in range(n_y // 2):
        at = slice(t * lanes, (t + 1) * lanes)
        even, odd = unpacked(ref, 2 * t, total), unpacked(ref, 2 * t + 1, total)
        left[0, :, at] = jnp.where(low, even[0], odd[0]).astype(BF16)
        left[1, :, at] = jnp.where(low, odd[1], even[1]).astype(BF16)
        if right is not None:
            right[0, :, at] = jnp.where(low, odd[0], even[0]).astype(BF16)
            right[1, :, at] = jnp.where(low, even[1], odd[1]).astype(BF16)


def triangle_messages(left_buf, right, tri_scr, out, rows, send=None):
    n_y, lanes = out.shape[0], out.shape[-1]
    low = low_lanes((n_y, 2, rows, lanes))
    for c in range(2):
        tri_scr[c] = dot(left_buf[c], right[c], FIRST)
    for t in range(n_y // 2):
        a, b = (
            tri_scr[c, :, t * lanes : (t + 1) * lanes]
            .reshape(n_y, SLOT, lanes)[:, : 2 * rows]
            .reshape(n_y, 2, rows, lanes)
            for c in range(2)
        )
        b = swap_pairs(b)
        out[:, :, 2 * t] = jnp.where(low, b, a).astype(BF16)
        out[:, :, 2 * t + 1] = jnp.where(low, a, b).astype(BF16)
        if send is not None:
            send(t)


def own_triangle_kernel(own_ref, part_ref, right_ref, tri_scr, left_buf):
    unpack_factors(own_ref, left_buf, right_ref)
    triangle_messages(left_buf, right_ref, tri_scr, part_ref, part_ref.shape[-2])


def other_triangle_kernel(
    ids_ref, other_ref, part_ref, right_ref, msg_ref, tri_scr, left_buf, part_buf, sems
):
    core = ids_ref[2]
    copies = [start(part_ref, msg_ref.at[:, core], sems.at[0])]

    def send(t):
        at = pl.ds(2 * t, 2)
        target = msg_ref.at[:, 1 - core, :, at]
        copies.append(start(part_buf.at[:, :, at], target, sems.at[1 + t]))

    unpack_factors(other_ref, left_buf, None)
    triangle_messages(left_buf, right_ref, tri_scr, part_buf, part_ref.shape[-2], send)
    for copy in copies:
        copy.wait()


def keep_factors_kernel(own_ref, other_ref, after_ref, factors_ref):
    for side, ref in enumerate((own_ref, other_ref)):
        unpack_factors(ref, factors_ref.at[0, side], factors_ref.at[1, side])


def norm_kernel(got_ref, scaled_ref, msg_ref, scr):
    half, rows, lanes = got_ref.shape
    scr[...] = got_ref[...].astype(F32)

    def mean(x):
        part = jnp.sum(x, axis=0)
        return (part + half_turn(part)) * (1.0 / (2 * half))

    for first in range(0, rows, 8):
        at = slice(first, first + 8)
        x = scr[:, at]
        x = x - mean(x)[None]
        inverse = lax.rsqrt(mean(x * x) + EPS)
        s = scaled_ref[:, at]
        along = inverse * inverse * mean(s * x)
        scr[:, at] = inverse[None] * (s - x * along[None])
    msg_ref[...] = scr[...].astype(BF16)


def update_kernel(
    ids_ref, got_ref, gate_ref, cot_ref, par_ref, w_out_ref, w_gate_ref, w_in_ref, coef_ref,
    pair_ref, update_ref, gn_ref, kept_coef_ref, kept_pair_ref, kept_w_in_ref, kept_par_ref,
    scr, gate_buf, cot_buf, w_out_buf, w_gate_buf, sems,
):
    sources = (coef_ref, pair_ref, w_in_ref, par_ref, gate_ref, cot_ref, w_out_ref, w_gate_ref)
    targets = (kept_coef_ref, kept_pair_ref, kept_w_in_ref, kept_par_ref)
    targets += (gate_buf, cot_buf, w_out_buf, w_gate_buf)
    copies = [start(x, y, sems.at[n]) for n, (x, y) in enumerate(zip(sources, targets))]
    for copy in copies:
        copy.wait()
    rows, cols, width = cot_ref.shape
    half, _, lanes = got_ref.shape
    w_out, w_gate = w_out_buf[...], w_gate_buf[...]
    gain, shift = kept_par_ref[2:3, :], kept_par_ref[3:4, :]
    row = lax.broadcasted_iota(jnp.int32, (cols, 2 * lanes), 0)
    col = lax.broadcasted_iota(jnp.int32, (cols, 2 * lanes), 1)
    odd = ids_ref[3] * SLOT
    pick = (col == row + (SLOT - odd)) | (col == row + (lanes + odd))
    pick = jnp.where(pick, 1.0, 0.0).astype(BF16)
    nothing = jnp.zeros((half, lanes), BF16)
    scr[...] = got_ref[...].astype(F32).reshape(half * rows, lanes)
    for first in range(0, rows, GROUP):
        size = GROUP * cols
        at = slice(first * cols, first * cols + size)
        tri = []
        for k in range(first, first + GROUP):
            x = scr[pl.ds(k, half, stride=rows), :].astype(BF16)
            both = jnp.concatenate(
                [jnp.concatenate([x, nothing], axis=1), jnp.concatenate([nothing, x], axis=1)],
                axis=0,
            )
            tri.append(dot(pick, both, LAST))
        unit, _ = unit_of(jnp.concatenate(tri, axis=0))
        lin = dot((unit * gain + shift).astype(BF16), w_out)
        gate = gate_buf[at, :]
        update_ref[first : first + GROUP] = (gate * lin).astype(BF16).reshape(GROUP, cols, width)
        cot = cot_buf[first : first + GROUP].astype(F32).reshape(size, width)
        grad_gate = (cot * lin * gate * (1.0 - gate)).astype(BF16)
        gn_ref[at, :] = dot(grad_gate, w_gate, LAST)


def unpack_grads(ref, place, tri_scr):
    n_y, _, _, _, rows, lanes = ref.shape
    low = low_lanes((n_y, 2, rows, lanes))
    gap = jnp.zeros((n_y, SLOT - 2 * rows, lanes), F32)
    for t in range(n_y // 2):
        even = ref[:, place, :, 2 * t].astype(F32)
        odd = ref[:, place, :, 2 * t + 1].astype(F32)
        first = jnp.where(low, odd, even)
        second = swap_pairs(jnp.where(low, even, odd))
        for c, tile in enumerate((first, second)):
            tile = jnp.concatenate([tile.reshape(n_y, 2 * rows, lanes), gap], axis=1)
            tile = tile.reshape(n_y * SLOT, lanes).astype(BF16)
            tri_scr[c, :, t * lanes : (t + 1) * lanes] = tile


def own_grads_kernel(ids_ref, own_ref, factors_ref, gl_ref, gr_ref, tri_scr):
    core = ids_ref[2]
    unpack_grads(own_ref, core, tri_scr.at[0])
    unpack_grads(own_ref, 1 - core, tri_scr.at[1])
    for c in range(2):
        left, far_left, right = factors_ref[0, 0, c], factors_ref[0, 1, c], factors_ref[1, 0, c]
        gl_ref[c] = dot(right, tri_scr[0, c], LAST)
        gr_ref[c] = dot(left, tri_scr[0, c]) + dot(far_left, tri_scr[1, c])


def other_grads_kernel(
    ids_ref, other_ref, factors_ref, gl_ref, gr_ref, msg_ref, tri_scr, gl_scr, msg_buf, sems
):
    n_row, n_y, _, lanes = msg_ref.shape
    total = gl_ref.shape[1]
    rows = total // n_row
    unpack_grads(other_ref, ids_ref[2], tri_scr)
    results = []
    low = low_lanes((total, lanes))
    at_lane = place_in_slot((n_row, 8, lanes))
    for y in range(n_y):
        tails = []
        at = slice(y // 2 * lanes, y // 2 * lanes + lanes)
        if y % 2 == 0:
            for c in range(2):
                more = dot(factors_ref[1, 1, c], tri_scr[c, at, :], LAST)
                gl_scr[c, :, at] = gl_ref[c, :, at] + more
        for c in range(2):
            a, b = gl_scr[c, :, at], gr_ref[c, :, at]
            if (y + c) % 2:
                a, b = b, a
            both = jnp.where(low, a, b).reshape(n_row, rows, lanes)
            one, two, rest = both[:, :8], both[:, 8:16], both[:, 16:24]
            one = jnp.where(at_lane < 3 * PIECE, one, turn(rest, 3 * PIECE))
            two = jnp.where(at_lane < 3 * PIECE, two, turn(rest, 2 * PIECE))
            msg_buf[y, :, 16 * c : 16 * c + 16] = jnp.concatenate([one, two], axis=1).astype(BF16)
            tails.append(turn(rest, (c - 2) * PIECE))
        tail = jnp.where(at_lane < PIECE, tails[0], tails[1])
        msg_buf[y, :, 32:40] = tail.astype(BF16)
        results.append(start(msg_buf.at[y], msg_ref.at[:, y], sems.at[y]))
    for copy in results:
        copy.wait()


def pair_grad_kernel(
    ids_ref, got_ref, gn_ref, coef_ref, pair_ref, w_in_ref, par_ref, out_ref,
    scr, left_buf, right_buf, out_buf, sems,
):
    half, _, lanes = got_ref.shape
    rows, cols, width = out_ref.shape
    eye = identity(2 * half)
    scr[...] = got_ref[...].astype(F32).reshape(half * MSG_ROWS, lanes)
    main, tail = 16, 8
    low = low_lanes((PIECE, 2 * half))
    for first in range(0, main + tail, GROUP):
        parts = []
        for s in range(first, first + GROUP):
            if s < main:
                parts += [scr[pl.ds(c * main + s, half, stride=MSG_ROWS), :] for c in range(2)]
            else:
                parts += [scr[pl.ds(main + s, half, stride=MSG_ROWS), :]] * 2
        turned = dot(eye, jnp.concatenate(parts, axis=0).astype(BF16), LAST)
        for n, s in enumerate(range(first, first + GROUP)):
            both = turned[:, n * 2 * half : (n + 1) * 2 * half]
            for buf, x in ((left_buf, both[:SLOT]), (right_buf, both[SLOT:])):
                if s < main:
                    at = (main + s % tail) * cols + s // tail * PIECE
                    buf[s * cols : (s + 1) * cols, :] = x[:cols]
                    buf[at : at + PIECE, :] = x[cols:]
                else:
                    at = s * cols + 2 * PIECE
                    buf[at : at + PIECE, :] = jnp.where(low, x[:PIECE], x[PIECE : 2 * PIECE])
    gain = par_ref[0:1, :]
    flat = rows * cols
    w_in = w_in_ref[...]
    group = 2 * GROUP
    size = group * cols
    straight = straight_lanes(ids_ref, (size, 2 * half))
    results = []
    for first in range(0, rows, group):
        at = slice(first * cols, first * cols + size)
        left = jnp.where(straight, left_buf[at, :], right_buf[at, :])
        right = jnp.where(straight, right_buf[at, :], left_buf[at, :])
        coef_a, val_a, coef_b, val_b = (
            coef_ref[n * flat + first * cols : n * flat + first * cols + size, :].astype(F32)
            for n in range(4)
        )
        grad_proj = jnp.concatenate(
            [
                (side * factor).astype(BF16)
                for side, factor in ((left, coef_a), (left, val_a), (right, coef_b), (right, val_b))
            ],
            axis=1,
        )
        s = (dot(grad_proj, w_in, LAST) + gn_ref[at, :]) * gain
        unit, inverse = unit_of(pair_ref[at, :].astype(F32))
        grad = inverse * (
            s
            - jnp.mean(s, axis=-1, keepdims=True)
            - unit * jnp.mean(s * unit, axis=-1, keepdims=True)
        )
        out_buf[first : first + group] = grad.astype(BF16).reshape(group, cols, width)
        part = pl.ds(first, group)
        results.append(start(out_buf.at[part], out_ref.at[part], sems.at[first // group]))
    for copy in results:
        copy.wait()


def call(kernel, ins, outs, scratch=(), smem=(), sems=(), limit=12, flops=0, moved=0):
    spaces = {"s": pltpu.SMEM, "v": pltpu.VMEM, "b": pltpu.VMEM, "h": pltpu.HBM}
    extra = [pltpu.SMEM(s, d) for s, d in smem]
    if sems:
        extra.append(pltpu.SemaphoreType.DMA(sems))
    return pl.pallas_call(
        kernel,
        out_shape=[
            jax.ShapeDtypeStruct(s, d) if place == "v" else pltpu.HBM(s, d)
            for s, d, place in outs
        ],
        in_specs=[pl.BlockSpec(memory_space=spaces[place]) for _, place in ins],
        out_specs=[pl.BlockSpec(memory_space=spaces[place]) for _, _, place in outs],
        scratch_shapes=[pltpu.VMEM(s, d) for s, d in scratch] + extra,
        compiler_params=pltpu.CompilerParams(vmem_limit_bytes=limit * MIB),
        cost_estimate=pl.CostEstimate(flops=flops, bytes_accessed=moved, transcendentals=0),
    )(
        *(
            pltpu.with_memory_space_constraint(x, pltpu.HBM) if place == "h" else x
            for x, place in ins
        )
    )


def exchange(x):
    return lax.all_to_all(x, ("row", "y"), 0, 0, tiled=True)


def swap(x):
    return lax.ppermute(x, "core", [(0, 1), (1, 0)])


def local(pair, chain_lengths, cotangent, norm_params, w_in, w_gate, w_out):
    rows, cols, width = pair.shape
    hidden = w_out.shape[0]
    n_row, n_y = lax.axis_size("row"), lax.axis_size("y")
    assert hidden == 2 * n_row * n_y == 2 * SLOT and width == hidden
    assert rows == 24 and cols == 2 * rows and n_row == 4 * n_y and lax.axis_size("core") == 2
    half = hidden // 2
    size, lanes = rows * cols, 2 * SLOT
    total, wide = n_row * rows, n_y * SLOT
    row, core = lax.axis_index("row"), lax.axis_index("core")
    col = 2 * lax.axis_index("y") + core
    ids = jnp.stack([row * rows, col * cols, core, lax.axis_index("y") % 2]).astype(jnp.int32)

    flat = (size, width)
    block = (rows, cols, width)
    par = (norm_params.shape, F32)
    factor = (2, 2, total, wide)
    two = (half, MSG_ROWS, lanes)
    one = (half, rows, lanes)
    by_home = (n_row, n_y, MSG_ROWS, lanes)
    by_block = (n_y, 2, 2, n_y, rows, lanes)
    (msg,) = call(
        factors_kernel,
        [(ids, "s"), (chain_lengths, "h"), (pair, "h"), (norm_params, "h"), (w_in, "h")],
        [(two, BF16, "v")],
        [((half * MSG_ROWS, lanes), F32), (block, BF16), (block, BF16), (block, BF16), par]
        + [(w_in.shape, BF16)],
        smem=[(chain_lengths.shape, jnp.int32)],
        sems=(4,),
        flops=2 * size * width * 4 * hidden,
        moved=8 * MIB,
    )
    got = exchange(msg)
    own, other = got.reshape(by_home), swap(got).reshape(by_home)
    half_block = (n_y, 2, n_y, rows, lanes)
    part, right = call(
        own_triangle_kernel,
        [(own, "v")],
        [(half_block, BF16, "v"), (factor[1:], BF16, "v")],
        [((2, wide, wide), F32), (factor[1:], BF16)],
        flops=4 * total * wide * wide,
        moved=4 * MIB,
    )
    (msg,) = call(
        other_triangle_kernel,
        [(ids, "s"), (other, "v"), (part, "v"), (right, "v")],
        [(by_block, BF16, "h")],
        [((2, wide, wide), F32), (factor[1:], BF16), (half_block, BF16)],
        sems=(1 + n_y // 2,),
        flops=4 * total * wide * wide,
        moved=4 * MIB,
    )
    (factors,) = call(
        keep_factors_kernel,
        [(own, "v"), (other, "v"), (msg, "h")],
        [((2,) + factor, BF16, "b")],
        flops=8 * total * wide * wide,
        moved=4 * MIB,
    )
    got = exchange(msg.reshape(one))
    gate, scaled, coef = call(
        saved_kernel,
        [(ids, "s"), (chain_lengths, "s"), (pair, "v"), (factors, "h"), (cotangent, "v")]
        + [(norm_params, "v"), (w_in, "v"), (w_gate, "v"), (w_out, "v")],
        [(flat, F32, "b"), (one, F32, "v"), ((4 * size, width), BF16, "b")],
        [((half * rows, lanes), F32)],
        flops=2 * size * width * 6 * hidden,
        moved=24 * MIB,
    )
    (msg,) = call(
        norm_kernel,
        [(got, "v"), (scaled, "v")],
        [(one, BF16, "v")],
        [(one, F32)],
        flops=2 * size * width * hidden,
        moved=4 * MIB,
    )
    update, *kept = call(
        update_kernel,
        [(ids, "s"), (got, "v"), (gate, "h"), (cotangent, "h"), (norm_params, "h")]
        + [(w_out, "h"), (w_gate, "h"), (w_in, "h"), (coef, "h"), (pair.reshape(flat), "h")],
        [(block, BF16, "b"), (flat, F32, "v"), (coef.shape, BF16, "v"), (flat, BF16, "v")]
        + [(w_in.shape, BF16, "v"), par + ("v",)],
        [((half * rows, lanes), F32), (flat, F32), (block, BF16), (w_out.shape, BF16)]
        + [(w_gate.shape, BF16)],
        sems=(8,),
        flops=4 * size * width * hidden,
        moved=12 * MIB,
    )
    got = exchange(msg)
    other = swap(got).reshape(by_block)
    summed = ((2, total, wide), F32, "v")
    gl, gr = call(
        own_grads_kernel,
        [(ids, "s"), (got.reshape(by_block), "v"), (factors, "v")],
        [summed, summed],
        [((2, 2, wide, wide), BF16)],
        flops=12 * total * wide * wide,
        moved=4 * MIB,
    )
    (msg,) = call(
        other_grads_kernel,
        [(ids, "s"), (other, "v"), (factors, "v"), (gl, "v"), (gr, "v")],
        [(by_home, BF16, "h")],
        [((2, wide, wide), BF16), ((2, total, wide), F32)]
        + [((n_y, n_row, MSG_ROWS, lanes), BF16)],
        sems=(4,),
        flops=4 * total * wide * wide,
        moved=4 * MIB,
    )
    got = exchange(msg.reshape(two))
    (grad_pair,) = call(
        pair_grad_kernel,
        [(ids, "s"), (got, "v")] + [(x, "v") for x in kept],
        [(block, BF16, "h")],
        [((half * MSG_ROWS, lanes), F32), (flat, F32), (flat, F32), (block, BF16)],
        sems=(3,),
        flops=2 * size * width * 4 * hidden,
        moved=8 * MIB,
    )
    return (update, grad_pair)


def solution(mesh):
    n_row, n_col, n_rep = mesh.devices.shape
    mesh = Mesh(mesh.devices.reshape(n_row, n_col // 2, 2, n_rep), ("row", "y", "core", "rep"))
    block = P(("rep", "row"), ("y", "core"), None)
    return jax.shard_map(
        local,
        mesh=mesh,
        in_specs=(block, P("rep"), block, P(), P(), P(), P()),
        out_specs=(block, block),
        check_vma=False,
    )
```

```python
import jax
import jax.numpy as jnp
from jax import lax
from jax.experimental import pallas as pl
from jax.experimental.pallas import tpu as pltpu
from jax.sharding import Mesh
from jax.sharding import PartitionSpec as P

EPS = 1e-05
F32 = jnp.float32
BF16 = jnp.bfloat16
MIB = 1 << 20
LAST = (((1,), (1,)), ((), ()))
FIRST = (((0,), (0,)), ((), ()))
SLOT = 64
PIECE = 16
MSG_ROWS = 40
GROUP = 4


def dot(a, b, dims=(((1,), (0,)), ((), ()))):
    return lax.dot_general(a, b, dims, preferred_element_type=F32)


def identity(n):
    row = lax.broadcasted_iota(jnp.int32, (n, n), 0)
    col = lax.broadcasted_iota(jnp.int32, (n, n), 1)
    return jnp.where(row == col, 1.0, 0.0).astype(BF16)


def low_lanes(shape):
    return lax.broadcasted_iota(jnp.int32, shape, len(shape) - 1) < SLOT


def half_turn(x):
    return turn(x, SLOT)


def turn(x, by):
    return pltpu.roll(x, by % x.shape[-1], x.ndim - 1)


def place_in_slot(shape):
    return lax.rem(lax.broadcasted_iota(jnp.int32, shape, len(shape) - 1), SLOT)


def straight_lanes(ids_ref, shape):
    lane = lax.broadcasted_iota(jnp.int32, shape, len(shape) - 1)
    return jnp.where(lane < SLOT, 0, 1) == ids_ref[3]


def swap_pairs(x):
    return jnp.concatenate([x[n ^ 1][None] for n in range(x.shape[0])], axis=0)


def unit_of(x):
    mean = jnp.mean(x, axis=-1, keepdims=True)
    centered = x - mean
    variance = jnp.mean(centered * centered, axis=-1, keepdims=True)
    inverse = lax.rsqrt(variance + EPS)
    return centered * inverse, inverse


def mask_of(ids_ref, len_ref, row, shape):
    limit = len_ref[0]
    for i in range(1, len_ref.shape[0]):
        limit = limit + len_ref[i]
    bound = jnp.where(ids_ref[0] + row < limit, limit - ids_ref[1], 0)
    return lax.broadcasted_iota(jnp.int32, shape, 0) < bound


def start(source, target, sem):
    copy = pltpu.make_async_copy(source, target, sem)
    copy.start()
    return copy


def paired(first, second):
    gap = jnp.zeros((SLOT - first.shape[0], first.shape[1]), first.dtype)
    return jnp.concatenate([first, gap, second, gap], axis=0)


def factors_kernel(
    ids_ref, len_ref, pair_ref, par_ref, w_ref, msg_ref,
    scr, a_buf, b_buf, pair_buf, par_buf, w_buf, len_buf, sems,
):
    rows, cols, width = pair_ref.shape
    hidden = w_ref.shape[1] // 4
    half = hidden // 2
    sources = (pair_ref, w_ref, par_ref, len_ref)
    targets = (pair_buf, w_buf, par_buf, len_buf)
    copies = [start(x, y, sems.at[n]) for n, (x, y) in enumerate(zip(sources, targets))]
    eye = identity(hidden)
    for copy in copies:
        copy.wait()
    gain, shift = par_buf[0:1, :], par_buf[1:2, :]
    w = w_buf[...]
    straight = straight_lanes(ids_ref, (cols, hidden))
    for first in range(0, rows, GROUP):
        x = pair_buf[first : first + GROUP].astype(F32).reshape(GROUP * cols, width)
        unit, _ = unit_of(x)
        normed = (unit * gain + shift).astype(BF16)
        proj = dot(normed, w)
        left = jax.nn.sigmoid(proj[:, :hidden]) * proj[:, hidden : 2 * hidden]
        right = jax.nn.sigmoid(proj[:, 2 * hidden : 3 * hidden]) * proj[:, 3 * hidden :]
        for k in range(GROUP):
            mask = mask_of(ids_ref, len_buf, first + k, (cols, hidden))
            at = slice(k * cols, (k + 1) * cols)
            one, two = jnp.where(mask, left[at], 0.0), jnp.where(mask, right[at], 0.0)
            a_buf[first + k] = jnp.where(straight, one, two).astype(BF16)
            b_buf[first + k] = jnp.where(straight, two, one).astype(BF16)
    main, tail = 16, 8
    gap = jnp.zeros((2 * PIECE, hidden), BF16)
    low = place_in_slot((half, 2 * SLOT)) < PIECE
    for first in range(0, main + tail, tail):
        parts = []
        for s in range(first, first + tail):
            if s < main:
                e, at = main + s % tail, pl.ds(s // tail * PIECE, PIECE)
                parts += [a_buf[s], a_buf[e, at], b_buf[s], b_buf[e, at]]
            else:
                at = pl.ds(2 * PIECE, PIECE)
                parts += [a_buf[s, at], a_buf[s, at], gap, b_buf[s, at], b_buf[s, at], gap]
        turned = dot(eye, jnp.concatenate(parts, axis=0), LAST)
        for n, s in enumerate(range(first, first + tail)):
            one = turned[:half, n * hidden : (n + 1) * hidden]
            two = turned[half:, n * hidden : (n + 1) * hidden]
            if s < main:
                scr[pl.ds(s, half, stride=MSG_ROWS), :] = one
                scr[pl.ds(main + s, half, stride=MSG_ROWS), :] = two
            else:
                scr[pl.ds(main + s, half, stride=MSG_ROWS), :] = jnp.where(low, one, two)
    msg_ref[...] = scr[...].reshape(msg_ref.shape).astype(BF16)


def saved_kernel(
    ids_ref, len_ref, pair_ref, after_ref, cot_ref, par_ref, w_in_ref, w_gate_ref, w_out_ref,
    gate_ref, scaled_ref, coef_ref, scr,
):
    rows, cols, width = pair_ref.shape
    hidden = w_in_ref.shape[1] // 4
    half = hidden // 2
    first_half = ~straight_lanes(ids_ref, (half, 2 * SLOT))
    w_in, w_gate, w_out = w_in_ref[...], w_gate_ref[...], w_out_ref[...]
    for first in range(0, rows, GROUP):
        size = GROUP * cols
        at = slice(first * cols, first * cols + size)
        x = pair_ref[first : first + GROUP].astype(F32).reshape(size, width)
        unit, _ = unit_of(x)
        normed = (unit * par_ref[0:1, :] + par_ref[1:2, :]).astype(BF16)
        gate = jax.nn.sigmoid(dot(normed, w_gate))
        gate_ref[at, :] = gate
        cot = cot_ref[first : first + GROUP].astype(F32).reshape(size, width)
        grad_lin = (cot * gate).astype(BF16)
        scaled = dot(grad_lin, w_out, LAST) * par_ref[2:3, :]
        scaled = scaled - jnp.mean(scaled, axis=-1, keepdims=True)
        proj = dot(normed, w_in)
        masks = []
        for k in range(GROUP):
            one = scaled[k * cols : (k + 1) * cols]
            turned = jnp.transpose(paired(one, one))
            turned = jnp.where(first_half, turned[:half], turned[half:])
            scr[pl.ds(first + k, half, stride=rows), :] = turned
            mask = mask_of(ids_ref, len_ref, first + k, (cols, hidden))
            masks.append(jnp.where(mask, 1.0, 0.0))
        mask = jnp.concatenate(masks, axis=0)
        for side in range(2):
            sig = jax.nn.sigmoid(proj[:, 2 * side * hidden : (2 * side + 1) * hidden])
            val = proj[:, (2 * side + 1) * hidden : (2 * side + 2) * hidden]
            kept = mask * sig
            for n, x in enumerate((kept * val * (1.0 - sig), kept)):
                place = (2 * side + n) * rows * cols + first * cols
                coef_ref[place : place + size, :] = x.astype(BF16)
    scaled_ref[...] = scr[...].reshape(scaled_ref.shape)


def unpacked(ref, y, total):
    n_row, _, _, lanes = ref.shape
    at_lane = place_in_slot((n_row, 8, lanes))
    got = ref[:, y].astype(F32)
    tail = got[:, 32:40]
    result = []
    for c in range(2):
        one, two = got[:, 16 * c : 16 * c + 8], got[:, 16 * c + 8 : 16 * c + 16]
        rest = jnp.where(at_lane < 3 * PIECE, turn(tail, (2 - c) * PIECE), 0.0)
        rest = jnp.where(at_lane < 2 * PIECE, turn(two, -2 * PIECE), rest)
        rest = jnp.where(at_lane < PIECE, turn(one, -3 * PIECE), rest)
        one = jnp.where(at_lane < 3 * PIECE, one, 0.0)
        two = jnp.where(at_lane < 3 * PIECE, two, 0.0)
        result.append(jnp.concatenate([one, two, rest], axis=1).reshape(total, lanes))
    return result


def unpack_factors(ref, left, right):
    n_y, lanes = ref.shape[1], ref.shape[-1]
    total = left.shape[-2]
    low = low_lanes((total, lanes))
    for t in range(n_y // 2):
        at = slice(t * lanes, (t + 1) * lanes)
        even, odd = unpacked(ref, 2 * t, total), unpacked(ref, 2 * t + 1, total)
        left[0, :, at] = jnp.where(low, even[0], odd[0]).astype(BF16)
        left[1, :, at] = jnp.where(low, odd[1], even[1]).astype(BF16)
        if right is not None:
            right[0, :, at] = jnp.where(low, odd[0], even[0]).astype(BF16)
            right[1, :, at] = jnp.where(low, even[1], odd[1]).astype(BF16)


def triangle_messages(left_buf, right, tri_scr, out, rows, send=None):
    n_y, lanes = out.shape[0], out.shape[-1]
    low = low_lanes((n_y, 2, rows, lanes))
    for c in range(2):
        tri_scr[c] = dot(left_buf[c], right[c], FIRST)
    for t in range(n_y // 2):
        a, b = (
            tri_scr[c, :, t * lanes : (t + 1) * lanes]
            .reshape(n_y, SLOT, lanes)[:, : 2 * rows]
            .reshape(n_y, 2, rows, lanes)
            for c in range(2)
        )
        b = swap_pairs(b)
        out[:, :, 2 * t] = jnp.where(low, b, a).astype(BF16)
        out[:, :, 2 * t + 1] = jnp.where(low, a, b).astype(BF16)
        if send is not None:
            send(t)


def own_triangle_kernel(own_ref, part_ref, right_ref, tri_scr, left_buf):
    unpack_factors(own_ref, left_buf, right_ref)
    triangle_messages(left_buf, right_ref, tri_scr, part_ref, part_ref.shape[-2])


def other_triangle_kernel(
    ids_ref, other_ref, part_ref, right_ref, msg_ref, tri_scr, left_buf, part_buf, sems
):
    core = ids_ref[2]
    copies = [start(part_ref, msg_ref.at[:, core], sems.at[0])]

    def send(t):
        at = pl.ds(2 * t, 2)
        target = msg_ref.at[:, 1 - core, :, at]
        copies.append(start(part_buf.at[:, :, at], target, sems.at[1 + t]))

    unpack_factors(other_ref, left_buf, None)
    triangle_messages(left_buf, right_ref, tri_scr, part_buf, part_ref.shape[-2], send)
    for copy in copies:
        copy.wait()


def keep_factors_kernel(own_ref, other_ref, after_ref, factors_ref):
    for side, ref in enumerate((own_ref, other_ref)):
        unpack_factors(ref, factors_ref.at[0, side], factors_ref.at[1, side])


def norm_kernel(got_ref, scaled_ref, msg_ref, scr):
    half, rows, lanes = got_ref.shape
    scr[...] = got_ref[...].astype(F32)

    def mean(x):
        part = jnp.sum(x, axis=0)
        return (part + half_turn(part)) * (1.0 / (2 * half))

    for first in range(0, rows, 8):
        at = slice(first, first + 8)
        x = scr[:, at]
        x = x - mean(x)[None]
        inverse = lax.rsqrt(mean(x * x) + EPS)
        s = scaled_ref[:, at]
        along = inverse * inverse * mean(s * x)
        scr[:, at] = inverse[None] * (s - x * along[None])
    msg_ref[...] = scr[...].astype(BF16)


def update_kernel(
    ids_ref, got_ref, gate_ref, cot_ref, par_ref, w_out_ref, w_gate_ref, w_in_ref, coef_ref,
    pair_ref, update_ref, gn_ref, kept_coef_ref, kept_pair_ref, kept_w_in_ref, kept_par_ref,
    scr, gate_buf, cot_buf, w_out_buf, w_gate_buf, sems,
):
    sources = (coef_ref, pair_ref, w_in_ref, par_ref, gate_ref, cot_ref, w_out_ref, w_gate_ref)
    targets = (kept_coef_ref, kept_pair_ref, kept_w_in_ref, kept_par_ref)
    targets += (gate_buf, cot_buf, w_out_buf, w_gate_buf)
    copies = [start(x, y, sems.at[n]) for n, (x, y) in enumerate(zip(sources, targets))]
    for copy in copies:
        copy.wait()
    rows, cols, width = cot_ref.shape
    half, _, lanes = got_ref.shape
    w_out, w_gate = w_out_buf[...], w_gate_buf[...]
    gain, shift = kept_par_ref[2:3, :], kept_par_ref[3:4, :]
    row = lax.broadcasted_iota(jnp.int32, (cols, 2 * lanes), 0)
    col = lax.broadcasted_iota(jnp.int32, (cols, 2 * lanes), 1)
    odd = ids_ref[3] * SLOT
    pick = (col == row + (SLOT - odd)) | (col == row + (lanes + odd))
    pick = jnp.where(pick, 1.0, 0.0).astype(BF16)
    nothing = jnp.zeros((half, lanes), BF16)
    scr[...] = got_ref[...].astype(F32).reshape(half * rows, lanes)
    for first in range(0, rows, GROUP):
        size = GROUP * cols
        at = slice(first * cols, first * cols + size)
        tri = []
        for k in range(first, first + GROUP):
            x = scr[pl.ds(k, half, stride=rows), :].astype(BF16)
            both = jnp.concatenate(
                [jnp.concatenate([x, nothing], axis=1), jnp.concatenate([nothing, x], axis=1)],
                axis=0,
            )
            tri.append(dot(pick, both, LAST))
        unit, _ = unit_of(jnp.concatenate(tri, axis=0))
        lin = dot((unit * gain + shift).astype(BF16), w_out)
        gate = gate_buf[at, :]
        update_ref[first : first + GROUP] = (gate * lin).astype(BF16).reshape(GROUP, cols, width)
        cot = cot_buf[first : first + GROUP].astype(F32).reshape(size, width)
        grad_gate = (cot * lin * gate * (1.0 - gate)).astype(BF16)
        gn_ref[at, :] = dot(grad_gate, w_gate, LAST)


def unpack_grads(ref, place, tri_scr):
    n_y, _, _, _, rows, lanes = ref.shape
    low = low_lanes((n_y, 2, rows, lanes))
    gap = jnp.zeros((n_y, SLOT - 2 * rows, lanes), F32)
    for t in range(n_y // 2):
        even = ref[:, place, :, 2 * t].astype(F32)
        odd = ref[:, place, :, 2 * t + 1].astype(F32)
        first = jnp.where(low, odd, even)
        second = swap_pairs(jnp.where(low, even, odd))
        for c, tile in enumerate((first, second)):
            tile = jnp.concatenate([tile.reshape(n_y, 2 * rows, lanes), gap], axis=1)
            tile = tile.reshape(n_y * SLOT, lanes).astype(BF16)
            tri_scr[c, :, t * lanes : (t + 1) * lanes] = tile


def own_grads_kernel(ids_ref, own_ref, factors_ref, gl_ref, gr_ref, tri_scr):
    core = ids_ref[2]
    unpack_grads(own_ref, core, tri_scr.at[0])
    unpack_grads(own_ref, 1 - core, tri_scr.at[1])
    for c in range(2):
        left, far_left, right = factors_ref[0, 0, c], factors_ref[0, 1, c], factors_ref[1, 0, c]
        gl_ref[c] = dot(right, tri_scr[0, c], LAST)
        gr_ref[c] = dot(left, tri_scr[0, c]) + dot(far_left, tri_scr[1, c])


def other_grads_kernel(
    ids_ref, other_ref, factors_ref, gl_ref, gr_ref, msg_ref, tri_scr, gl_scr, msg_buf, sems
):
    n_row, n_y, _, lanes = msg_ref.shape
    total = gl_ref.shape[1]
    rows = total // n_row
    unpack_grads(other_ref, ids_ref[2], tri_scr)
    results = []
    low = low_lanes((total, lanes))
    at_lane = place_in_slot((n_row, 8, lanes))
    for y in range(n_y):
        tails = []
        at = slice(y // 2 * lanes, y // 2 * lanes + lanes)
        if y % 2 == 0:
            for c in range(2):
                more = dot(factors_ref[1, 1, c], tri_scr[c, at, :], LAST)
                gl_scr[c, :, at] = gl_ref[c, :, at] + more
        for c in range(2):
            a, b = gl_scr[c, :, at], gr_ref[c, :, at]
            if (y + c) % 2:
                a, b = b, a
            both = jnp.where(low, a, b).reshape(n_row, rows, lanes)
            one, two, rest = both[:, :8], both[:, 8:16], both[:, 16:24]
            one = jnp.where(at_lane < 3 * PIECE, one, turn(rest, 3 * PIECE))
            two = jnp.where(at_lane < 3 * PIECE, two, turn(rest, 2 * PIECE))
            msg_buf[y, :, 16 * c : 16 * c + 16] = jnp.concatenate([one, two], axis=1).astype(BF16)
            tails.append(turn(rest, (c - 2) * PIECE))
        tail = jnp.where(at_lane < PIECE, tails[0], tails[1])
        msg_buf[y, :, 32:40] = tail.astype(BF16)
        results.append(start(msg_buf.at[y], msg_ref.at[:, y], sems.at[y]))
    for copy in results:
        copy.wait()


def pair_grad_kernel(
    ids_ref, got_ref, gn_ref, coef_ref, pair_ref, w_in_ref, par_ref, out_ref,
    scr, left_buf, right_buf, out_buf, sems,
):
    half, _, lanes = got_ref.shape
    rows, cols, width = out_ref.shape
    eye = identity(2 * half)
    scr[...] = got_ref[...].astype(F32).reshape(half * MSG_ROWS, lanes)
    main, tail = 16, 8
    low = low_lanes((PIECE, 2 * half))
    for first in range(0, main + tail, tail):
        parts = []
        for s in range(first, first + tail):
            if s < main:
                parts += [scr[pl.ds(c * main + s, half, stride=MSG_ROWS), :] for c in range(2)]
            else:
                parts += [scr[pl.ds(main + s, half, stride=MSG_ROWS), :]] * 2
        turned = dot(eye, jnp.concatenate(parts, axis=0).astype(BF16), LAST)
        for n, s in enumerate(range(first, first + tail)):
            both = turned[:, n * 2 * half : (n + 1) * 2 * half]
            for buf, x in ((left_buf, both[:SLOT]), (right_buf, both[SLOT:])):
                if s < main:
                    at = (main + s % tail) * cols + s // tail * PIECE
                    buf[s * cols : (s + 1) * cols, :] = x[:cols]
                    buf[at : at + PIECE, :] = x[cols:]
                else:
                    at = s * cols + 2 * PIECE
                    buf[at : at + PIECE, :] = jnp.where(low, x[:PIECE], x[PIECE : 2 * PIECE])
    gain = par_ref[0:1, :]
    flat = rows * cols
    w_in = w_in_ref[...]
    group = 2 * GROUP
    size = group * cols
    straight = straight_lanes(ids_ref, (size, 2 * half))
    results = []
    for first in range(0, rows, group):
        at = slice(first * cols, first * cols + size)
        left = jnp.where(straight, left_buf[at, :], right_buf[at, :])
        right = jnp.where(straight, right_buf[at, :], left_buf[at, :])
        coef_a, val_a, coef_b, val_b = (
            coef_ref[n * flat + first * cols : n * flat + first * cols + size, :].astype(F32)
            for n in range(4)
        )
        grad_proj = jnp.concatenate(
            [
                (side * factor).astype(BF16)
                for side, factor in ((left, coef_a), (left, val_a), (right, coef_b), (right, val_b))
            ],
            axis=1,
        )
        s = (dot(grad_proj, w_in, LAST) + gn_ref[at, :]) * gain
        unit, inverse = unit_of(pair_ref[at, :].astype(F32))
        grad = inverse * (
            s
            - jnp.mean(s, axis=-1, keepdims=True)
            - unit * jnp.mean(s * unit, axis=-1, keepdims=True)
        )
        out_buf[first : first + group] = grad.astype(BF16).reshape(group, cols, width)
        part = pl.ds(first, group)
        results.append(start(out_buf.at[part], out_ref.at[part], sems.at[first // group]))
    for copy in results:
        copy.wait()


def call(kernel, ins, outs, scratch=(), smem=(), sems=(), limit=12, flops=0, moved=0):
    spaces = {"s": pltpu.SMEM, "v": pltpu.VMEM, "b": pltpu.VMEM, "h": pltpu.HBM}
    extra = [pltpu.SMEM(s, d) for s, d in smem]
    if sems:
        extra.append(pltpu.SemaphoreType.DMA(sems))
    return pl.pallas_call(
        kernel,
        out_shape=[
            jax.ShapeDtypeStruct(s, d) if place == "v" else pltpu.HBM(s, d)
            for s, d, place in outs
        ],
        in_specs=[pl.BlockSpec(memory_space=spaces[place]) for _, place in ins],
        out_specs=[pl.BlockSpec(memory_space=spaces[place]) for _, _, place in outs],
        scratch_shapes=[pltpu.VMEM(s, d) for s, d in scratch] + extra,
        compiler_params=pltpu.CompilerParams(vmem_limit_bytes=limit * MIB),
        cost_estimate=pl.CostEstimate(flops=flops, bytes_accessed=moved, transcendentals=0),
    )(
        *(
            pltpu.with_memory_space_constraint(x, pltpu.HBM) if place == "h" else x
            for x, place in ins
        )
    )


def exchange(x):
    return lax.all_to_all(x, ("row", "y"), 0, 0, tiled=True)


def swap(x):
    return lax.ppermute(x, "core", [(0, 1), (1, 0)])


def local(pair, chain_lengths, cotangent, norm_params, w_in, w_gate, w_out):
    rows, cols, width = pair.shape
    hidden = w_out.shape[0]
    n_row, n_y = lax.axis_size("row"), lax.axis_size("y")
    assert hidden == 2 * n_row * n_y == 2 * SLOT and width == hidden
    assert rows == 24 and cols == 2 * rows and n_row == 4 * n_y and lax.axis_size("core") == 2
    half = hidden // 2
    size, lanes = rows * cols, 2 * SLOT
    total, wide = n_row * rows, n_y * SLOT
    row, core = lax.axis_index("row"), lax.axis_index("core")
    col = 2 * lax.axis_index("y") + core
    ids = jnp.stack([row * rows, col * cols, core, lax.axis_index("y") % 2]).astype(jnp.int32)

    flat = (size, width)
    block = (rows, cols, width)
    par = (norm_params.shape, F32)
    factor = (2, 2, total, wide)
    two = (half, MSG_ROWS, lanes)
    one = (half, rows, lanes)
    by_home = (n_row, n_y, MSG_ROWS, lanes)
    by_block = (n_y, 2, 2, n_y, rows, lanes)
    (msg,) = call(
        factors_kernel,
        [(ids, "s"), (chain_lengths, "h"), (pair, "h"), (norm_params, "h"), (w_in, "h")],
        [(two, BF16, "v")],
        [((half * MSG_ROWS, lanes), F32), (block, BF16), (block, BF16), (block, BF16), par]
        + [(w_in.shape, BF16)],
        smem=[(chain_lengths.shape, jnp.int32)],
        sems=(4,),
        flops=2 * size * width * 4 * hidden,
        moved=8 * MIB,
    )
    got = exchange(msg)
    own, other = got.reshape(by_home), swap(got).reshape(by_home)
    half_block = (n_y, 2, n_y, rows, lanes)
    part, right = call(
        own_triangle_kernel,
        [(own, "v")],
        [(half_block, BF16, "v"), (factor[1:], BF16, "v")],
        [((2, wide, wide), F32), (factor[1:], BF16)],
        flops=4 * total * wide * wide,
        moved=4 * MIB,
    )
    (msg,) = call(
        other_triangle_kernel,
        [(ids, "s"), (other, "v"), (part, "v"), (right, "v")],
        [(by_block, BF16, "h")],
        [((2, wide, wide), F32), (factor[1:], BF16), (half_block, BF16)],
        sems=(1 + n_y // 2,),
        flops=4 * total * wide * wide,
        moved=4 * MIB,
    )
    (factors,) = call(
        keep_factors_kernel,
        [(own, "v"), (other, "v"), (msg, "h")],
        [((2,) + factor, BF16, "b")],
        flops=8 * total * wide * wide,
        moved=4 * MIB,
    )
    got = exchange(msg.reshape(one))
    gate, scaled, coef = call(
        saved_kernel,
        [(ids, "s"), (chain_lengths, "s"), (pair, "v"), (factors, "h"), (cotangent, "v")]
        + [(norm_params, "v"), (w_in, "v"), (w_gate, "v"), (w_out, "v")],
        [(flat, F32, "b"), (one, F32, "v"), ((4 * size, width), BF16, "b")],
        [((half * rows, lanes), F32)],
        flops=2 * size * width * 6 * hidden,
        moved=24 * MIB,
    )
    (msg,) = call(
        norm_kernel,
        [(got, "v"), (scaled, "v")],
        [(one, BF16, "v")],
        [(one, F32)],
        flops=2 * size * width * hidden,
        moved=4 * MIB,
    )
    update, *kept = call(
        update_kernel,
        [(ids, "s"), (got, "v"), (gate, "h"), (cotangent, "h"), (norm_params, "h")]
        + [(w_out, "h"), (w_gate, "h"), (w_in, "h"), (coef, "h"), (pair.reshape(flat), "h")],
        [(block, BF16, "b"), (flat, F32, "v"), (coef.shape, BF16, "v"), (flat, BF16, "v")]
        + [(w_in.shape, BF16, "v"), par + ("v",)],
        [((half * rows, lanes), F32), (flat, F32), (block, BF16), (w_out.shape, BF16)]
        + [(w_gate.shape, BF16)],
        sems=(8,),
        flops=4 * size * width * hidden,
        moved=12 * MIB,
    )
    got = exchange(msg)
    other = swap(got).reshape(by_block)
    summed = ((2, total, wide), F32, "v")
    gl, gr = call(
        own_grads_kernel,
        [(ids, "s"), (got.reshape(by_block), "v"), (factors, "v")],
        [summed, summed],
        [((2, 2, wide, wide), BF16)],
        flops=12 * total * wide * wide,
        moved=4 * MIB,
    )
    (msg,) = call(
        other_grads_kernel,
        [(ids, "s"), (other, "v"), (factors, "v"), (gl, "v"), (gr, "v")],
        [(by_home, BF16, "h")],
        [((2, wide, wide), BF16), ((2, total, wide), F32)]
        + [((n_y, n_row, MSG_ROWS, lanes), BF16)],
        sems=(4,),
        flops=4 * total * wide * wide,
        moved=4 * MIB,
    )
    got = exchange(msg.reshape(two))
    (grad_pair,) = call(
        pair_grad_kernel,
        [(ids, "s"), (got, "v")] + [(x, "v") for x in kept],
        [(block, BF16, "h")],
        [((half * MSG_ROWS, lanes), F32), (flat, F32), (flat, F32), (block, BF16)],
        sems=(3,),
        flops=2 * size * width * 4 * hidden,
        moved=8 * MIB,
    )
    return (update, grad_pair)


def solution(mesh):
    n_row, n_col, n_rep = mesh.devices.shape
    mesh = Mesh(mesh.devices.reshape(n_row, n_col // 2, 2, n_rep), ("row", "y", "core", "rep"))
    block = P(("rep", "row"), ("y", "core"), None)
    return jax.shard_map(
        local,
        mesh=mesh,
        in_specs=(block, P("rep"), block, P(), P(), P(), P()),
        out_specs=(block, block),
        check_vma=False,
    )
```
